32 devices in a mesh: blk: 8 (over z, x), feat: 4 (over y, core).
Axes of the slice: x: 2, y: 2, z: 4, core: 2. Of those that a mesh axis runs over, the one named last changes fastest.
Arguments:
- conv_maps: bfloat16 [1024, 169, 512], P('blk', None, 'feat'), may hold values from -18 to 18
- crop_counts: int32 [256], P('blk'), may hold values from 1 to 4, as said below
- fc_weight: bfloat16 [2, 4096, 9216], P(None, 'blk', 'feat'), may hold values from -0.0625 to 0.0625
- fc_bias: float32 [2, 4096], replicated, may hold values from -3 to 3
- stitch_in: float32 [2, 2, 256], P(None, None, 'feat'), may hold values from 0.3 to 1.2
- stitch_out: float32 [2, 2, 4096], P(None, None, 'feat'), may hold values from 0.3 to 1.2
- cotangent: bfloat16 [1024, 2, 4096], P('blk', None, 'feat'), may hold values from -6 to 6
Outputs:
- activations: bfloat16 [1024, 2, 4096], P('blk', None, 'feat')
- conv_grad: bfloat16 [1024, 169, 512], P('blk', None, 'feat')
- weight_grad: float32 [2, 4096, 9216], P(None, 'blk', 'feat')
- bias_grad: float32 [2, 4096], P(None, 'blk')
- stitch_in_grad: float32 [2, 2, 256], P(None, None, 'feat')
- stitch_out_grad: float32 [2, 2, 4096], P(None, None, 'feat')
The draws below stay inside these ranges and needn't reach their ends.
Inputs may be any that keep to these rules, and one draw needn't show every extreme that they name: `crop_counts`: each image has 1 to 4 crops; a blk index's slots hold its images' crops first, the rest of its 128 slots are padding; in every draw some blk index has all its images at 4 crops.
All inputs are finite; a program needn't handle non-finite values.
Results may differ from the reference program's by a relative error of at most 0.0054.
Values may be sent and summed in bfloat16 or wider, within the bound.
A program may use at most 256 MiB of HBM per device.

```python
import jax
import jax.numpy as jnp
from jax import lax

CH = 256
FF = 4096
MAP = 13
GRID = 6
TOWERS = 2
MOST = 4
IMG_DEV = 32
ROW_DEV = 128
FIN = 9216
ROWS = 1024
IMAGES = 256


def draw_crop_counts(key, part):
    key = jax.random.fold_in(key, 11)
    key_caps, key_raw, key_full = jax.random.split(key, 3)
    nblocks = IMAGES // IMG_DEV
    caps = jax.random.randint(key_caps, (nblocks, 1), 2, MOST + 1)
    raw = jax.random.randint(key_raw, (nblocks, IMG_DEV), 0, 1 << 20)
    counts = 1 + raw % caps
    full_index = jax.random.randint(key_full, (), 0, nblocks)
    block_ids = jnp.arange(nblocks)[:, None]
    counts = jnp.where(block_ids == full_index, MOST, counts)
    other = (full_index + 1) % nblocks
    image_ids = jnp.arange(IMG_DEV)[None, :]
    counts = jnp.where((block_ids == other) & (image_ids == 0), 1, counts)
    return counts.reshape(IMAGES).astype(jnp.int32)


def shard_levels(own_key, extent, pieces, smallest, high):
    def one(axis_at, blocks):
        draws = jax.random.uniform(jax.random.fold_in(jax.random.fold_in(own_key, 6), axis_at), (blocks,), jnp.float32, smallest / len(pieces), high / len(pieces))
        return jnp.repeat(jnp.exp(draws), extent[axis_at] // blocks).reshape((-1,) + (1,) * (len(extent) - axis_at - 1))

    gain = one(*pieces[0])
    for cut in pieces[1:]:
        gain = gain * one(*cut)
    return gain


def normal_values(key, extent, deviation, bound, cuts=(), dtype=jnp.bfloat16):
    entries = deviation * jax.random.normal(key, extent, jnp.float32)
    if cuts:
        entries = entries * shard_levels(key, extent, cuts, -0.22, 0.18)
    return jnp.clip(entries, -bound, bound).astype(dtype)


def setup_inputs(seed: int = 0) -> dict:
    arg_keys = jax.random.split(jax.random.key(seed), 8)
    return {
        "conv_maps": normal_values(arg_keys[0], (ROWS, MAP * MAP, CH * TOWERS), 3.0, 18.0, ((0, 8), (2, 4))),
        "crop_counts": draw_crop_counts(jax.random.fold_in(arg_keys[7], 71), 0),
        "fc_weight": normal_values(arg_keys[2], (TOWERS, FF, FIN), FIN ** -0.5, 0.0625, ((1, 8), (2, 4))),
        "fc_bias": normal_values(arg_keys[3], (TOWERS, FF), 0.5, 3.0, (), jnp.float32),
        "stitch_in": jnp.clip(0.3 + 0.90000004 * jax.random.uniform(arg_keys[4], (TOWERS, TOWERS, CH), jnp.float32) ** shard_levels(arg_keys[4], (TOWERS, TOWERS, CH), ((2, 4),), -0.2, 0.2), 0.3, 1.2),
        "stitch_out": jnp.clip(0.3 + 0.90000004 * jax.random.uniform(arg_keys[5], (TOWERS, TOWERS, FF), jnp.float32) ** shard_levels(arg_keys[5], (TOWERS, TOWERS, FF), ((2, 4),), -0.2, 0.2), 0.3, 1.2),
        "cotangent": normal_values(arg_keys[6], (ROWS, TOWERS, FF), 1.0, 6.0, ((0, 8), (2, 4))),
    }


@jax.custom_vjp
def low(v):
    return lax.optimization_barrier(v.astype(jnp.bfloat16)).astype(jnp.float32)

@jax.custom_vjp
def low_back(v):
    return v

def low_keep(v):
    return (low(v), None)

def low_pass(kept, grad):
    return (grad,)

def back_keep(v):
    return (v, None)

def back_low(kept, grad):
    return (low(grad),)
low.defvjp(low_keep, low_pass)
low_back.defvjp(back_keep, back_low)

def pool_table():
    position = jnp.arange(MAP * MAP)
    row_pos = position // MAP
    col_pos = position % MAP
    cell = jnp.arange(GRID * GRID)
    row_cell = cell // GRID
    col_cell = cell % GRID
    down = row_pos[:, None] - 2 * row_cell[None, :]
    across = col_pos[:, None] - 2 * col_cell[None, :]
    inside = (down >= 0) & (down < 3) & (across >= 0) & (across < 3)
    return inside.astype(jnp.float32)

def tower_block(conv, weight, bias, stitch_in, stitch_out, live):
    highest = lax.Precision.HIGHEST
    rows_here = conv.shape[0]
    conv_split = conv.reshape(rows_here, MAP * MAP, CH, TOWERS)
    pooled = jnp.einsum('rpct,pq->rtcq', conv_split, pool_table(), precision=highest) / 9.0
    mixed = jnp.einsum('tuc,rucq->rtcq', stitch_in, pooled, precision=highest)
    feats = low(mixed).reshape(rows_here, TOWERS, FIN)
    pre = jnp.einsum('rtf,tkf->rtk', feats, weight, precision=highest) + bias[None]
    pre = low_back(pre)
    act = jax.nn.gelu(pre)
    out = jnp.einsum('tuk,ruk->rtk', stitch_out, act, precision=highest)
    return out * live[:, None, None]

def reference(conv_maps, crop_counts, fc_weight, fc_bias, stitch_in, stitch_out, cotangent):
    weight32 = fc_weight.astype(jnp.float32)
    bias32 = fc_bias.astype(jnp.float32)
    s_in = stitch_in.astype(jnp.float32)
    s_out = stitch_out.astype(jnp.float32)
    nblocks = IMAGES // IMG_DEV
    conv_blocks = conv_maps.reshape(nblocks, ROW_DEV, MAP * MAP, CH * TOWERS)
    count_blocks = crop_counts.reshape(nblocks, IMG_DEV)
    cot_blocks = cotangent.reshape(nblocks, ROW_DEV, TOWERS, FF)

    def step(carry, block):
        conv_here, counts_here, cot_here = block
        live = (jnp.arange(ROW_DEV) < jnp.sum(counts_here)).astype(jnp.float32)

        def forward(conv, weight, bias, first, second):
            return tower_block(conv, weight, bias, first, second, live)
        out, pull = jax.vjp(forward, conv_here.astype(jnp.float32), weight32, bias32, s_in, s_out)
        grad_conv, grad_weight, grad_bias, grad_in, grad_out = pull(cot_here.astype(jnp.float32))
        total_w, total_b, total_in, total_out = carry
        carry = (total_w + grad_weight, total_b + grad_bias, total_in + grad_in, total_out + grad_out)
        return (carry, (out.astype(jnp.bfloat16), grad_conv.astype(jnp.bfloat16)))
    init = (jnp.zeros((TOWERS, FF, FIN), jnp.float32), jnp.zeros((TOWERS, FF), jnp.float32), jnp.zeros((TOWERS, TOWERS, CH), jnp.float32), jnp.zeros((TOWERS, TOWERS, FF), jnp.float32))
    sums, stacked = lax.scan(step, init, (conv_blocks, count_blocks, cot_blocks))
    weight_grad, bias_grad, stitch_in_grad, stitch_out_grad = sums
    activations = stacked[0].reshape(ROWS, TOWERS, FF)
    conv_grad = stacked[1].reshape(ROWS, MAP * MAP, CH * TOWERS)
    return (activations, conv_grad, weight_grad, bias_grad, stitch_in_grad, stitch_out_grad)
```

```python
import functools

import jax
import jax.numpy as jnp
from jax import lax
from jax.experimental import pallas as pl
from jax.experimental.pallas import tpu as pltpu
from jax.sharding import PartitionSpec as P

MAP = 13
GRID = 6
TOWERS = 2
CHUNK = 16
SPAN = 4
PLACES = 8
FEATS = 4
RING_BLK = (0, 2, 4, 6, 7, 5, 3, 1)
MESH = pl.DeviceIdType.MESH
f32 = jnp.float32
bf16 = jnp.bfloat16
i32 = jnp.int32


def pool_table(dtype):
    position = jnp.arange(MAP * MAP)
    row_pos = position // MAP
    col_pos = position % MAP
    cell = jnp.arange(GRID * GRID)
    row_cell = cell // GRID
    col_cell = cell % GRID
    down = row_pos[:, None] - 2 * row_cell[None, :]
    across = col_pos[:, None] - 2 * col_cell[None, :]
    inside = (down >= 0) & (down < 3) & (across >= 0) & (across < 3)
    return inside.astype(dtype)


def stitch_first(pooled, stitch_in):
    return jnp.einsum("tuc,rucq->rtcq", stitch_in, pooled, precision=lax.Precision.HIGHEST)


def stitch_head(pre, stitch_out):
    act = jax.nn.gelu(pre)
    return jnp.einsum("tuk,ruk->rtk", stitch_out, act, precision=lax.Precision.HIGHEST)


def body_plain(conv_maps, crop_counts, fc_weight, fc_bias, stitch_in, stitch_out, cotangent):
    num_rows = conv_maps.shape[0]
    merged = conv_maps.shape[2]
    chans = merged // TOWERS
    cols = fc_weight.shape[1]
    feat_idx = lax.axis_index("feat")
    blk_idx = lax.axis_index("blk")
    sums = jnp.einsum("rpm,pq->rqm", conv_maps, pool_table(bf16), preferred_element_type=f32)
    pooled = jnp.transpose(sums.reshape(num_rows, GRID * GRID, chans, TOWERS), (0, 3, 2, 1)) * (
        1.0 / 9.0
    )
    mixed, pull_first = jax.vjp(stitch_first, pooled, stitch_in)
    feats = mixed.astype(bf16).reshape(num_rows, TOWERS, -1)
    own_cols = jnp.einsum(
        "rtf,tnf->rtn",
        lax.all_gather(feats, "blk", axis=0, tiled=True),
        fc_weight,
        preferred_element_type=f32,
    )
    partial_value = lax.all_to_all(own_cols, "blk", split_axis=0, concat_axis=2, tiled=True)
    pre = lax.psum_scatter(partial_value, "feat", scatter_dimension=2, tiled=True)
    quarter = pre.shape[2]
    bias_part = lax.dynamic_slice_in_dim(fc_bias, feat_idx * quarter, quarter, 1)
    pre = pre + bias_part[None]
    live = (jnp.arange(num_rows) < jnp.sum(crop_counts)).astype(f32)
    stitched, pull_head = jax.vjp(stitch_head, pre, stitch_out)
    activations = (live[:, None, None] * stitched).astype(bf16)
    grad_out = live[:, None, None] * cotangent.astype(f32)
    grad_pre, grad_so = pull_head(grad_out)
    grad_low = grad_pre.astype(bf16)
    grad_all = lax.all_gather(grad_low, "feat", axis=2, tiled=True)
    bias_terms = jnp.sum(grad_all, axis=0, dtype=f32)
    grad_cols = lax.all_to_all(grad_all, "blk", split_axis=2, concat_axis=0, tiled=True)
    weight_grad = jnp.einsum(
        "rtf,rtn->tnf",
        lax.all_gather(feats, "blk", axis=0, tiled=True),
        grad_cols,
        preferred_element_type=f32,
    )
    grad_feats = jnp.einsum(
        "rtn,tnf->rtf",
        grad_all,
        lax.all_gather(fc_weight, "blk", axis=1, tiled=True),
        preferred_element_type=f32,
    )
    grad_mixed = grad_feats.reshape(num_rows, TOWERS, chans, -1)
    grad_pooled, grad_si = pull_first(grad_mixed)
    spread = jnp.einsum(
        "rtcq,pq->rpct", grad_pooled * (1.0 / 9.0), pool_table(f32), precision=lax.Precision.HIGHEST
    )
    conv_grad = spread.reshape(num_rows, MAP * MAP, merged).astype(bf16)
    stitch_in_grad, stitch_out_grad, bias_total = lax.psum((grad_si, grad_so, bias_terms), "blk")
    bias_grad = lax.dynamic_slice_in_dim(bias_total, blk_idx * cols, cols, 1)
    return (activations, conv_grad, weight_grad, bias_grad, stitch_in_grad, stitch_out_grad)


def ring_place(blk):
    z, x = lax.div(blk, 2), lax.rem(blk, 2)
    return z + x * (7 - 2 * z)


def ring_blk(place):
    x = lax.div(place, 4)
    return 2 * (place + x * (7 - 2 * place)) + x


def fc_kernel(
    steps,
    n_ref, so_ref, bias_ref, x_ref, cot_ref, w_hbm,
    act_out, gf_out, wg_hbm, bg_out, sog_out,
    w, x, land, ring_tx, ex_tx, ex_rx, gp, part, sum_rx, held, sums,
    cot_rx, acts, act_tx, act_rx, sog_acc, sog_tx, sog_rx, wg_tx,
    kd, nn, start, tot, slot_rc, slot_live,
    w_sem, ag_ss, ag_rs, rs_ss, rs_rs, ex_ss, ex_rs, gp_ss, gp_rs,
    cot_ss, cot_rs, act_ss, act_rs, sog_ss, sog_rs, wg_sem,
):
    blk, feat = lax.axis_index("blk"), lax.axis_index("feat")
    place = ring_place(blk)
    ring_to = (ring_blk(lax.rem(place + 1, 8)), ring_blk(lax.rem(place + 7, 8)))
    ring_from = (lax.rem(place + 7, 8), lax.rem(place + 1, 8))
    groups = x.shape[0] - 1
    slots = groups * SPAN
    sent = 2 * (steps - 1)
    feats_dim = x.shape[-1]
    units = w.shape[1]
    quarter = units // FEATS
    row_feat = lax.div(blk, 2)
    half_at = lax.rem(blk, 2) * FEATS + feat
    mine = row_feat == feat

    w_copy = pltpu.make_async_copy(w_hbm, w, w_sem)
    w_copy.start()

    bar = pltpu.get_barrier_semaphore()

    def hello(dev):
        pl.semaphore_signal(bar, inc=1, device_id=dev, device_id_type=MESH)

    for d in (0, 1):
        hello((ring_to[d], feat))
    for o in range(1, FEATS):
        hello((blk, lax.rem(feat + o, FEATS)))

    def hello_far(s, carry):
        to = (2 * feat + lax.div(s, FEATS), lax.rem(s, FEATS))

        @pl.when(jnp.logical_or(to[0] != blk, to[1] != feat))
        def _():
            hello(to)

        @pl.when(jnp.logical_or(s != blk, row_feat != feat))
        def _():
            hello((s, row_feat))

        return carry

    lax.fori_loop(0, 8, hello_far, 0)
    pl.semaphore_wait(bar, jnp.where(mine, 2 + 3 + 14, 2 + 3 + 16))

    def cot_copy(s):
        return pltpu.make_async_remote_copy(
            src_ref=cot_ref.at[s], dst_ref=cot_rx.at[blk], send_sem=cot_ss.at[s],
            recv_sem=cot_rs.at[blk],
            device_id=(2 * feat + lax.div(s, FEATS), lax.rem(s, FEATS)), device_id_type=MESH)

    def cot_wait(r):
        return pltpu.make_async_remote_copy(
            src_ref=cot_ref.at[0], dst_ref=cot_rx.at[r], send_sem=cot_ss.at[0],
            recv_sem=cot_rs.at[r], device_id=(r, row_feat), device_id_type=MESH)

    def far_not_me(s):
        return jnp.logical_or(2 * feat + lax.div(s, FEATS) != blk, lax.rem(s, FEATS) != feat)

    def near_not_me(r):
        return jnp.logical_or(r != blk, row_feat != feat)

    for c in range(8):
        for t in range(TOWERS):
            x[groups, t, c // SPAN, c % SPAN] = x_ref[c, t]

    run = jnp.int32(0)
    for q in range(PLACES):
        n = n_ref[RING_BLK[q]]
        k = jnp.clip(lax.div(n + (CHUNK - 1), CHUNK), 2, 8)
        first = lax.div(run + k + 1, 2) - lax.div(run + 1, 2)
        kd[q] = first
        kd[PLACES + q] = k - first
        nn[q] = n
        run = run + k

    def ring_unit_copy(d, m):
        return pltpu.make_async_remote_copy(
            src_ref=ring_tx.at[d, lax.rem(m, 4)], dst_ref=land.at[d, m],
            send_sem=ag_ss.at[d, lax.rem(m, 4)], recv_sem=ag_rs.at[d, m],
            device_id=(ring_to[d], feat), device_id_type=MESH)

    own_k = (kd[place], kd[PLACES + place])
    prev_k = tuple(kd[d * PLACES + ring_from[d]] for d in (0, 1))
    own_base = (0, own_k[0])
    for m in (0, 1):
        for d in (0, 1):
            c = own_base[d]
            ring_tx[d, m] = x[groups, m, lax.div(c, SPAN), lax.rem(c, SPAN)] if d else x[groups, m, 0, 0]
            ring_unit_copy(d, jnp.int32(m)).start()

    def cot_send(s, carry):
        @pl.when(far_not_me(s))
        def _():
            cot_copy(s).start()

        @pl.when(jnp.logical_not(far_not_me(s)))
        def _():
            cot_rx[blk] = cot_ref[s]

        return carry

    lax.fori_loop(0, 8, cot_send, 0)

    for d in (0, 1):
        run = jnp.int32(0)
        for h in range(1, PLACES + 1):
            at = lax.rem(place + (PLACES - h if d == 0 else h), PLACES)
            start[d * PLACES + at] = run
            run = run + kd[d * PLACES + at]
        tot[d] = run

        def fill(i, carry, d=d):
            h, c = carry
            hc = jnp.minimum(h, PLACES)
            at = lax.rem(place + (2 * PLACES - hc if d == 0 else hc), PLACES)
            chunk = jnp.minimum(c + (0 if d == 0 else kd[at]), 7)
            live = jnp.clip(nn[at] - CHUNK * chunk, 0, CHUNK)
            slot_rc[d * slots + i] = ring_blk(at) * 8 + chunk
            slot_live[d * slots + i] = jnp.where(h <= PLACES, live, 0)
            over = c + 1 >= kd[d * PLACES + at]
            return jnp.where(over, h + 1, h), jnp.where(over, 0, c + 1)

        lax.fori_loop(0, slots, fill, (jnp.int32(1), jnp.int32(0)))

    own_at = (tot[0] - own_k[0], tot[1] - own_k[1])
    held[...] = jnp.zeros_like(held)
    sog_acc[...] = jnp.zeros_like(sog_acc)
    w_copy.wait()

    def ex_copy(slot, g, o):
        to = lax.rem(feat + o, FEATS)
        return pltpu.make_async_remote_copy(
            src_ref=ex_tx.at[slot, to], dst_ref=ex_rx.at[g, feat], send_sem=ex_ss.at[slot, o - 1],
            recv_sem=ex_rs.at[g, feat], device_id=(blk, to), device_id_type=MESH)

    def ex_wait(g, o):
        src = lax.rem(feat + o, FEATS)
        return pltpu.make_async_remote_copy(
            src_ref=ex_tx.at[0, src], dst_ref=ex_rx.at[g, src], send_sem=ex_ss.at[0, o - 1],
            recv_sem=ex_rs.at[g, src], device_id=(blk, src), device_id_type=MESH)

    def gp_copy(g, o):
        to = lax.rem(feat + o, FEATS)
        return pltpu.make_async_remote_copy(
            src_ref=gp.at[g, feat], dst_ref=gp.at[g, feat], send_sem=gp_ss.at[g, o - 1],
            recv_sem=gp_rs.at[g, feat], device_id=(blk, to), device_id_type=MESH)

    def gp_wait(g, o):
        src = lax.rem(feat + o, FEATS)
        return pltpu.make_async_remote_copy(
            src_ref=gp.at[g, src], dst_ref=gp.at[g, src], send_sem=gp_ss.at[g, o - 1],
            recv_sem=gp_rs.at[g, src], device_id=(blk, src), device_id_type=MESH)

    def forward(g):
        slot = lax.rem(g, 2)

        @pl.when(g >= 2)
        def _():
            for o in range(1, FEATS):
                ex_copy(slot, g, o).wait_send()

        for t in range(TOWERS):
            rows = x[g, t].reshape(2 * SPAN * CHUNK, feats_dim)
            for h in range(2):
                out = lax.dot_general(
                    rows, w[t, 2 * h * quarter:2 * (h + 1) * quarter],
                    (((1,), (1,)), ((), ())), preferred_element_type=f32)
                for e in range(2):
                    ex_tx[slot, 2 * h + e, t] = out[:, e * quarter:(e + 1) * quarter].reshape(
                        2 * SPAN, CHUNK, quarter)
        for o in range(1, FEATS):
            ex_copy(slot, g, o).start()
        ex_rx[g, feat] = ex_tx[slot, feat]

    bias_here = bias_ref[:, pl.ds(pl.multiple_of(blk * units + feat * quarter, quarter), quarter)]

    def head(g):
        for o in range(1, FEATS):
            ex_wait(g, o).wait_recv()

        def one(s, carry):
            d, ci = lax.div(s, SPAN), lax.rem(s, SPAN)
            i = g * SPAN + ci
            rc = slot_rc[d * slots + i]
            live = slot_live[d * slots + i]
            mask = jnp.where(
                lax.broadcasted_iota(i32, (CHUNK, quarter), 0) < live, f32(1), f32(0))
            act, slope, cot = [], [], []
            for t in range(TOWERS):
                pre = ex_rx[g, 0, t, s]
                for q in range(1, FEATS):
                    pre = pre + ex_rx[g, q, t, s]
                pre = pre + bias_here[t:t + 1]
                square = pre * pre
                th = jnp.tanh(f32(0.7978845608028654) * (pre + f32(0.044715) * (square * pre)))
                cdf = f32(0.5) * (f32(1) + th)
                act.append(pre * cdf)
                slope.append(cdf + f32(0.5) * pre * (f32(1) - th * th) * (
                    f32(0.7978845608028654) * (f32(1) + f32(3 * 0.044715) * square)))
                cot.append(cot_rx[lax.div(rc, 8), lax.rem(rc, 8), t].astype(f32) * mask)
            for t in range(TOWERS):
                out = so_ref[2 * t:2 * t + 1] * act[0] + so_ref[2 * t + 1:2 * t + 2] * act[1]
                acts[i, d, t] = (out * mask).astype(bf16)
                for u in range(TOWERS):
                    sog_acc[2 * t + u] = sog_acc[2 * t + u] + cot[t] * act[u]
            for u in range(TOWERS):
                back = so_ref[u:u + 1] * cot[0] + so_ref[2 + u:3 + u] * cot[1]
                gp[g, feat, u, s] = (slope[u] * back).astype(bf16)
            return carry

        lax.fori_loop(0, 2 * SPAN, one, 0)
        for o in range(1, FEATS):
            gp_copy(g, o).start()

    tile = feats_dim // 3

    def backward(g):
        for o in range(1, FEATS):
            gp_wait(g, o).wait_recv()
        for t in range(TOWERS):
            rows = jnp.concatenate(
                [gp[g, q, t].reshape(2 * SPAN * CHUNK, quarter) for q in range(FEATS)], axis=1)
            for n in range(3):
                part[t, :, :, n * tile:(n + 1) * tile] = jnp.dot(
                    rows, w[t, :, n * tile:(n + 1) * tile],
                    preferred_element_type=f32).reshape(2 * SPAN, CHUNK, tile)

    wide = feats_dim // 6

    def wg_copy(q):
        return pltpu.make_async_copy(
            wg_tx.at[lax.rem(q, 2)],
            wg_hbm.at[lax.div(q, 6), :, pl.ds(pl.multiple_of(lax.rem(q, 6) * wide, 128), wide)],
            wg_sem.at[lax.rem(q, 2)])

    def weight_tile(q):
        t = lax.div(q, 6)
        cols = pl.ds(pl.multiple_of(lax.rem(q, 6) * wide, 128), wide)

        @pl.when(q >= 2)
        def _():
            wg_copy(q).wait()

        rows = x[0:groups, t, :, :, :, cols].reshape(groups * 2 * SPAN * CHUNK, wide)
        for e in range(FEATS):
            grads = gp[0:groups, e, t].reshape(groups * 2 * SPAN * CHUNK, quarter)
            wg_tx[lax.rem(q, 2), e * quarter:(e + 1) * quarter] = lax.dot_general(
                grads, rows, (((0,), (0,)), ((), ())), preferred_element_type=f32)
        wg_copy(q).start()

    def gather_unit(g, q):
        u = 2 * SPAN * g + q
        ci, t = lax.div(q, 2), lax.rem(q, 2)
        i = SPAN * g + ci
        for d in (0, 1):
            c = jnp.clip(i - own_at[d], 0, own_k[d] - 1) + own_base[d]
            own = x[groups, t, lax.div(c, SPAN), lax.rem(c, SPAN)]

            @pl.when(u < sent)
            def _(d=d, own=own):
                ring_unit_copy(d, u).wait_recv()
                x[g, t, d, ci] = jnp.where(i >= own_at[d], own, land[d, u])

            @pl.when(u >= sent)
            def _(d=d, own=own):
                x[g, t, d, ci] = own

        m = u + 2
        for d in (0, 1):
            @pl.when(m < sent)
            def _(d=d):
                @pl.when(m >= 4)
                def _():
                    ring_unit_copy(d, m).wait_send()

                im = i + 1
                here = im < own_k[d]
                cm = jnp.minimum(im, own_k[d] - 1) + own_base[d]
                src = jnp.maximum(im - own_k[d], 0)
                ring_tx[d, lax.rem(m, 4)] = x[
                    jnp.where(here, groups, lax.div(src, SPAN)), t,
                    jnp.where(here, lax.div(cm, SPAN), d),
                    jnp.where(here, lax.rem(cm, SPAN), lax.rem(src, SPAN))]
                ring_unit_copy(d, m).start()

    def sum_copy(d, v):
        return pltpu.make_async_remote_copy(
            src_ref=sums.at[d, v], dst_ref=sum_rx.at[d, v], send_sem=rs_ss.at[d, v],
            recv_sem=rs_rs.at[d, v], device_id=(ring_to[d], feat), device_id_type=MESH)

    def sum_unit(g, q):
        v = 2 * SPAN * g + q
        ci, t = lax.div(q, 2), lax.rem(q, 2)
        for d in (0, 1):
            @pl.when(jnp.logical_and(v >= 2, v - 2 < sent))
            def _(d=d):
                sum_copy(d, v - 2).wait_recv()
                held[d, lax.rem(v - 2, 8)] = sum_rx[d, v - 2]

            came = held[d, lax.rem(v - 2 * prev_k[d] + 8, 8)].astype(f32)
            value = part[t, d * SPAN + ci] + came * jnp.where(v >= 2 * prev_k[d], f32(1), f32(0))
            sums[d, v] = value.astype(bf16)

            @pl.when(v < sent)
            def _(d=d):
                sum_copy(d, v).start()

    def act_copy(r):
        return pltpu.make_async_remote_copy(
            src_ref=act_tx.at[r], dst_ref=act_rx.at[half_at], send_sem=act_ss.at[r],
            recv_sem=act_rs.at[half_at], device_id=(r, row_feat), device_id_type=MESH)

    def act_wait(s):
        return pltpu.make_async_remote_copy(
            src_ref=act_tx.at[0], dst_ref=act_rx.at[s], send_sem=act_ss.at[0],
            recv_sem=act_rs.at[s], device_id=(blk, feat), device_id_type=MESH)

    def sog_copy(r):
        return pltpu.make_async_remote_copy(
            src_ref=sog_tx, dst_ref=sog_rx.at[half_at], send_sem=sog_ss.at[r],
            recv_sem=sog_rs.at[half_at], device_id=(r, row_feat), device_id_type=MESH)

    def sog_wait(s):
        return pltpu.make_async_remote_copy(
            src_ref=sog_tx, dst_ref=sog_rx.at[s], send_sem=sog_ss.at[0],
            recv_sem=sog_rs.at[s], device_id=(blk, feat), device_id_type=MESH)

    def send_acts():
        sog_tx[...] = jnp.concatenate(
            [jnp.sum(sog_acc[e], axis=0, keepdims=True) for e in range(4)] * 2, axis=0)

        def pick(rc, carry):
            r, c = lax.div(rc, 8), lax.rem(rc, 8)
            at = ring_place(r)
            first, second = kd[at], kd[PLACES + at]
            d = jnp.where(c >= first, 1, 0)
            i = jnp.minimum(start[d * PLACES + at] + c - d * first, slots - 1)
            keep = jnp.where(c < first + second, f32(1), f32(0))
            for t in range(TOWERS):
                act_tx[r, c, t] = (acts[i, d, t].astype(f32) * keep).astype(bf16)
            return carry

        lax.fori_loop(0, PLACES * 8, pick, 0)

        def send(r, carry):
            @pl.when(near_not_me(r))
            def _():
                act_copy(r).start()
                sog_copy(r).start()

            @pl.when(jnp.logical_not(near_not_me(r)))
            def _():
                act_rx[half_at] = act_tx[r]
                sog_rx[half_at] = sog_tx[...]

            return carry

        lax.fori_loop(0, PLACES, send, 0)

    def iteration(it, carry):
        @pl.when(it >= 3)
        def _():
            backward(it - 3)

        @pl.when(it == 2)
        def _():
            def arrived(r, carry):
                @pl.when(near_not_me(r))
                def _():
                    cot_wait(r).wait_recv()

                return carry

            lax.fori_loop(0, PLACES, arrived, 0)

        @pl.when(jnp.logical_and(it >= 2, it < groups + 2))
        def _():
            head(it - 2)

        @pl.when(jnp.logical_and(it >= 1, it < groups + 1))
        def _():
            forward(it - 1)

        @pl.when(it == groups + 1)
        def _():
            send_acts()

        def unit(q, carry):
            @pl.when(it < groups)
            def _():
                gather_unit(it, q)

            @pl.when(it >= 3)
            def _():
                sum_unit(it - 3, q)

            @pl.when(jnp.logical_and(it == groups + 2, q < 6))
            def _():
                weight_tile(2 * q)
                weight_tile(2 * q + 1)

            return carry

        lax.fori_loop(0, 2 * SPAN, unit, 0)
        return carry

    lax.fori_loop(0, groups + 3, iteration, 0)

    for c in range(8):
        d = jnp.where(c >= own_k[0], 1, 0)
        i = jnp.where(c >= own_k[0], own_at[1] + c - own_k[0], own_at[0] + c)
        i = jnp.clip(i, 0, slots - 1)
        keep = jnp.where(c < own_k[0] + own_k[1], f32(1), f32(0))
        for t in range(TOWERS):
            gf_out[c, t] = (sums[d, 2 * i + t].astype(f32) * keep).astype(bf16)

    for e in range(FEATS):
        for t in range(TOWERS):
            def add(g, total, e=e, t=t):
                return total + jnp.sum(gp[g, e, t].astype(f32), axis=0)

            total = lax.fori_loop(0, groups, add, jnp.zeros((CHUNK, quarter), f32))
            bg_out[t:t + 1, e * quarter:(e + 1) * quarter] = jnp.sum(total, axis=0, keepdims=True)

    def finish(s, carry):
        @pl.when(far_not_me(s))
        def _():
            act_wait(s).wait_recv()
            sog_wait(s).wait_recv()
            cot_copy(s).wait_send()

        @pl.when(near_not_me(s))
        def _():
            act_copy(s).wait_send()
            sog_copy(s).wait_send()

        return carry

    lax.fori_loop(0, 8, finish, 0)
    act_out[...] = act_rx[...]
    sog_out[...] = sog_rx[...]

    def finish_sums(v, carry):
        for d in (0, 1):
            sum_copy(d, v).wait_send()
        return carry

    lax.fori_loop(0, sent, finish_sums, 0)
    for m in range(sent - 4, sent):
        for d in (0, 1):
            ring_unit_copy(d, jnp.int32(m)).wait_send()
    for o in range(1, FEATS):
        for g in (groups - 2, groups - 1):
            ex_copy(g % 2, g, o).wait_send()

        def finish_gp(g, carry, o=o):
            gp_copy(g, o).wait_send()
            return carry

        lax.fori_loop(0, groups, finish_gp, 0)
    for q in (10, 11):
        wg_copy(jnp.int32(q)).wait()


def fc_layer(steps, number, n, so, bias, x, cot, weight):
    units, feats_dim = weight.shape[1:]
    quarter = units // FEATS
    groups = -(-steps // SPAN)
    slots = groups * SPAN
    vm = pltpu.VMEM
    dma = pltpu.SemaphoreType.DMA
    sm = pltpu.SMEM
    unit = (CHUNK, feats_dim)
    vmem_spec = pl.BlockSpec(memory_space=pltpu.VMEM)
    any_spec = pl.BlockSpec(memory_space=pl.ANY)
    rows = 2 * slots * CHUNK
    return pl.pallas_call(
        functools.partial(fc_kernel, steps),
        out_shape=(
            jax.ShapeDtypeStruct((8, 8, TOWERS, CHUNK, quarter), bf16),
            jax.ShapeDtypeStruct((8, TOWERS) + unit, bf16),
            jax.ShapeDtypeStruct(weight.shape, f32),
            jax.ShapeDtypeStruct((TOWERS, units), f32),
            jax.ShapeDtypeStruct((8, 8, quarter), f32),
        ),
        in_specs=[pl.BlockSpec(memory_space=pltpu.SMEM)] + [vmem_spec] * 4 + [any_spec],
        out_specs=(vmem_spec, vmem_spec, any_spec, vmem_spec, vmem_spec),
        scratch_shapes=[
            vm(weight.shape, bf16),
            vm((groups + 1, TOWERS, 2, SPAN) + unit, bf16),
            vm((2, 2 * steps - 2) + unit, bf16),
            vm((2, 4) + unit, bf16),
            vm((2, FEATS, TOWERS, 2 * SPAN, CHUNK, quarter), f32),
            vm((groups, FEATS, TOWERS, 2 * SPAN, CHUNK, quarter), f32),
            vm((groups, FEATS, TOWERS, 2 * SPAN, CHUNK, quarter), bf16),
            vm((TOWERS, 2 * SPAN) + unit, f32),
            vm((2, 2 * steps - 2) + unit, bf16),
            vm((2, 8) + unit, bf16),
            vm((2, 2 * slots) + unit, bf16),
            vm((8, 8, TOWERS, CHUNK, quarter), bf16),
            vm((slots, 2, TOWERS, CHUNK, quarter), bf16),
            vm((8, 8, TOWERS, CHUNK, quarter), bf16),
            vm((8, 8, TOWERS, CHUNK, quarter), bf16),
            vm((4, CHUNK, quarter), f32),
            vm((8, quarter), f32),
            vm((8, 8, quarter), f32),
            vm((2, units, feats_dim // 6), f32),
            sm((2 * PLACES,), i32),
            sm((PLACES,), i32),
            sm((2 * PLACES,), i32),
            sm((2,), i32),
            sm((2 * slots,), i32),
            sm((2 * slots,), i32),
            dma,
            dma((2, 4)),
            dma((2, 2 * steps - 2)),
            dma((2, 2 * steps - 2)),
            dma((2, 2 * steps - 2)),
            dma((2, 3)),
            dma((groups, FEATS)),
            dma((groups, 3)),
            dma((groups, FEATS)),
            dma((8,)),
            dma((8,)),
            dma((8,)),
            dma((8,)),
            dma((8,)),
            dma((8,)),
            dma((2,)),
        ],
        cost_estimate=pl.CostEstimate(
            flops=6 * rows * TOWERS * units * feats_dim, bytes_accessed=30 << 20,
            transcendentals=rows * TOWERS * quarter),
        compiler_params=pltpu.CompilerParams(
            collective_id=number, has_side_effects=True, vmem_limit_bytes=60 << 20),
    )(n, so, bias, x, cot, weight)


CLASSES = (20, 24)


def body_ring(conv_maps, crop_counts, fc_weight, fc_bias, stitch_in, stitch_out, cotangent):
    num_rows = conv_maps.shape[0]
    merged = conv_maps.shape[2]
    chans = merged // TOWERS
    units = fc_weight.shape[1]
    quarter = units // FEATS
    chunks = num_rows // CHUNK
    feat_idx = lax.axis_index("feat")
    blk_idx = lax.axis_index("blk")
    n = lax.all_gather(jnp.sum(crop_counts), "blk")
    so = lax.all_gather(stitch_out, "feat", axis=2, tiled=True)
    so = lax.dynamic_slice_in_dim(so, blk_idx * units + feat_idx * quarter, quarter, 2).reshape(
        4, quarter)
    cot = cotangent.reshape(chunks, CHUNK, TOWERS, 8, quarter).transpose(3, 0, 2, 1, 4)
    sums = jnp.einsum("rpm,pq->rqm", conv_maps, pool_table(bf16), preferred_element_type=f32)
    pooled = jnp.transpose(sums.reshape(num_rows, GRID * GRID, chans, TOWERS), (0, 3, 2, 1)) * (
        1.0 / 9.0
    )
    mixed, pull_first = jax.vjp(stitch_first, pooled, stitch_in)
    feats = mixed.astype(bf16).reshape(chunks, CHUNK, TOWERS, -1).transpose(0, 2, 1, 3)
    need = lax.div(jnp.sum(lax.div(n + (CHUNK - 1), CHUNK)) + 1, 2)
    full = PLACES * chunks // 2
    kinds = CLASSES + (full,)
    pick = sum(((need > c).astype(i32) for c in CLASSES), jnp.int32(0))
    act, gf, weight_grad, bias_grad, sog = lax.switch(
        pick,
        [functools.partial(fc_layer, steps, at) for at, steps in enumerate(kinds)],
        n, so, fc_bias, feats, cot, fc_weight)
    activations = act.transpose(1, 3, 2, 0, 4).reshape(num_rows, TOWERS, -1)
    stitch_out_grad = sog[:, :4].transpose(1, 0, 2).reshape(TOWERS, TOWERS, -1)
    grad_mixed = gf.transpose(0, 2, 1, 3).astype(f32).reshape(num_rows, TOWERS, chans, -1)
    grad_pooled, grad_si = pull_first(grad_mixed)
    spread = jnp.einsum(
        "rtcq,pq->rpct", grad_pooled * (1.0 / 9.0), pool_table(f32), precision=lax.Precision.HIGHEST
    )
    conv_grad = spread.reshape(num_rows, MAP * MAP, merged).astype(bf16)
    stitch_in_grad = lax.psum(grad_si, "blk")
    return (activations, conv_grad, weight_grad, bias_grad, stitch_in_grad, stitch_out_grad)


def solution(mesh):
    ring = mesh.shape["blk"] == PLACES and mesh.shape["feat"] == FEATS
    return jax.shard_map(
        body_ring if ring else body_plain,
        mesh=mesh,
        in_specs=(
            P("blk", None, "feat"),
            P("blk"),
            P(None, "blk", "feat"),
            P(),
            P(None, None, "feat"),
            P(None, None, "feat"),
            P("blk", None, "feat"),
        ),
        out_specs=(
            P("blk", None, "feat"),
            P("blk", None, "feat"),
            P(None, "blk", "feat"),
            P(None, "blk"),
            P(None, None, "feat"),
            P(None, None, "feat"),
        ),
        check_vma=False,
    )
```

```python
import functools

import jax
import jax.numpy as jnp
import numpy as np
from jax import lax
from jax.experimental import pallas as pl
from jax.experimental.pallas import tpu as pltpu
from jax.sharding import PartitionSpec as P

MAP = 13
GRID = 6
TOWERS = 2
CHUNK = 16
SPAN = 4
PLACES = 8
FEATS = 4
RING_BLK = (0, 2, 4, 6, 7, 5, 3, 1)
MESH = pl.DeviceIdType.MESH
f32 = jnp.float32
bf16 = jnp.bfloat16
i32 = jnp.int32


def pool_table(dtype):
    position = jnp.arange(MAP * MAP)
    row_pos = position // MAP
    col_pos = position % MAP
    cell = jnp.arange(GRID * GRID)
    row_cell = cell // GRID
    col_cell = cell % GRID
    down = row_pos[:, None] - 2 * row_cell[None, :]
    across = col_pos[:, None] - 2 * col_cell[None, :]
    inside = (down >= 0) & (down < 3) & (across >= 0) & (across < 3)
    return inside.astype(dtype)


def stitch_first(pooled, stitch_in):
    return jnp.einsum("tuc,rucq->rtcq", stitch_in, pooled, precision=lax.Precision.HIGHEST)


def stitch_head(pre, stitch_out):
    act = jax.nn.gelu(pre)
    return jnp.einsum("tuk,ruk->rtk", stitch_out, act, precision=lax.Precision.HIGHEST)


def body_plain(conv_maps, crop_counts, fc_weight, fc_bias, stitch_in, stitch_out, cotangent):
    num_rows = conv_maps.shape[0]
    merged = conv_maps.shape[2]
    chans = merged // TOWERS
    cols = fc_weight.shape[1]
    feat_idx = lax.axis_index("feat")
    blk_idx = lax.axis_index("blk")
    sums = jnp.einsum("rpm,pq->rqm", conv_maps, pool_table(bf16), preferred_element_type=f32)
    pooled = jnp.transpose(sums.reshape(num_rows, GRID * GRID, chans, TOWERS), (0, 3, 2, 1)) * (
        1.0 / 9.0
    )
    mixed, pull_first = jax.vjp(stitch_first, pooled, stitch_in)
    feats = mixed.astype(bf16).reshape(num_rows, TOWERS, -1)
    own_cols = jnp.einsum(
        "rtf,tnf->rtn",
        lax.all_gather(feats, "blk", axis=0, tiled=True),
        fc_weight,
        preferred_element_type=f32,
    )
    partial_value = lax.all_to_all(own_cols, "blk", split_axis=0, concat_axis=2, tiled=True)
    pre = lax.psum_scatter(partial_value, "feat", scatter_dimension=2, tiled=True)
    quarter = pre.shape[2]
    bias_part = lax.dynamic_slice_in_dim(fc_bias, feat_idx * quarter, quarter, 1)
    pre = pre + bias_part[None]
    live = (jnp.arange(num_rows) < jnp.sum(crop_counts)).astype(f32)
    stitched, pull_head = jax.vjp(stitch_head, pre, stitch_out)
    activations = (live[:, None, None] * stitched).astype(bf16)
    grad_out = live[:, None, None] * cotangent.astype(f32)
    grad_pre, grad_so = pull_head(grad_out)
    grad_low = grad_pre.astype(bf16)
    grad_all = lax.all_gather(grad_low, "feat", axis=2, tiled=True)
    bias_terms = jnp.sum(grad_all, axis=0, dtype=f32)
    grad_cols = lax.all_to_all(grad_all, "blk", split_axis=2, concat_axis=0, tiled=True)
    weight_grad = jnp.einsum(
        "rtf,rtn->tnf",
        lax.all_gather(feats, "blk", axis=0, tiled=True),
        grad_cols,
        preferred_element_type=f32,
    )
    grad_feats = jnp.einsum(
        "rtn,tnf->rtf",
        grad_all,
        lax.all_gather(fc_weight, "blk", axis=1, tiled=True),
        preferred_element_type=f32,
    )
    grad_mixed = grad_feats.reshape(num_rows, TOWERS, chans, -1)
    grad_pooled, grad_si = pull_first(grad_mixed)
    spread = jnp.einsum(
        "rtcq,pq->rpct", grad_pooled * (1.0 / 9.0), pool_table(f32), precision=lax.Precision.HIGHEST
    )
    conv_grad = spread.reshape(num_rows, MAP * MAP, merged).astype(bf16)
    stitch_in_grad, stitch_out_grad, bias_total = lax.psum((grad_si, grad_so, bias_terms), "blk")
    bias_grad = lax.dynamic_slice_in_dim(bias_total, blk_idx * cols, cols, 1)
    return (activations, conv_grad, weight_grad, bias_grad, stitch_in_grad, stitch_out_grad)


def ring_place(blk):
    z, x = lax.div(blk, 2), lax.rem(blk, 2)
    return z + x * (7 - 2 * z)


def ring_blk(place):
    x = lax.div(place, 4)
    return 2 * (place + x * (7 - 2 * place)) + x


def fc_kernel(
    steps,
    n_ref, so_ref, bias_ref, x_ref, cot_ref, w_hbm,
    act_out, gf_out, wg_hbm, bg_out, sog_out,
    w, x, land, ring_tx, ex_tx, ex_rx, gp, part, sum_rx, held, sums,
    cot_rx, acts, act_tx, act_rx, sog_acc, sog_tx, sog_rx, wg_tx,
    kd, nn, start, tot, slot_rc, slot_live,
    w_sem, ag_ss, ag_rs, rs_ss, rs_rs, ex_ss, ex_rs, gp_ss, gp_rs,
    cot_ss, cot_rs, act_ss, act_rs, sog_ss, sog_rs, wg_sem,
):
    blk, feat = lax.axis_index("blk"), lax.axis_index("feat")
    place = ring_place(blk)
    ring_to = (ring_blk(lax.rem(place + 1, 8)), ring_blk(lax.rem(place + 7, 8)))
    ring_from = (lax.rem(place + 7, 8), lax.rem(place + 1, 8))
    groups = x.shape[0] - 1
    slots = groups * SPAN
    sent = 2 * (steps - 1)
    feats_dim = x.shape[-1]
    units = w.shape[1]
    quarter = units // FEATS
    row_feat = lax.div(blk, 2)
    half_at = lax.rem(blk, 2) * FEATS + feat
    mine = row_feat == feat

    w_copy = pltpu.make_async_copy(w_hbm, w, w_sem)
    w_copy.start()

    bar = pltpu.get_barrier_semaphore()

    def hello(dev):
        pl.semaphore_signal(bar, inc=1, device_id=dev, device_id_type=MESH)

    for d in (0, 1):
        hello((ring_to[d], feat))
    for o in range(1, FEATS):
        hello((blk, lax.rem(feat + o, FEATS)))

    def hello_far(s, carry):
        to = (2 * feat + lax.div(s, FEATS), lax.rem(s, FEATS))

        @pl.when(jnp.logical_or(to[0] != blk, to[1] != feat))
        def _():
            hello(to)

        @pl.when(jnp.logical_or(s != blk, row_feat != feat))
        def _():
            hello((s, row_feat))

        return carry

    lax.fori_loop(0, 8, hello_far, 0)
    pl.semaphore_wait(bar, jnp.where(mine, 2 + 3 + 14, 2 + 3 + 16))

    def cot_copy(s):
        return pltpu.make_async_remote_copy(
            src_ref=cot_ref.at[s], dst_ref=cot_rx.at[blk], send_sem=cot_ss.at[s],
            recv_sem=cot_rs.at[blk],
            device_id=(2 * feat + lax.div(s, FEATS), lax.rem(s, FEATS)), device_id_type=MESH)

    def cot_wait(r):
        return pltpu.make_async_remote_copy(
            src_ref=cot_ref.at[0], dst_ref=cot_rx.at[r], send_sem=cot_ss.at[0],
            recv_sem=cot_rs.at[r], device_id=(r, row_feat), device_id_type=MESH)

    def far_not_me(s):
        return jnp.logical_or(2 * feat + lax.div(s, FEATS) != blk, lax.rem(s, FEATS) != feat)

    def near_not_me(r):
        return jnp.logical_or(r != blk, row_feat != feat)

    for c in range(8):
        for t in range(TOWERS):
            x[groups, t, c // SPAN, c % SPAN] = x_ref[c, t]

    run = jnp.int32(0)
    for q in range(PLACES):
        n = n_ref[RING_BLK[q]]
        k = jnp.clip(lax.div(n + (CHUNK - 1), CHUNK), 2, 8)
        first = lax.div(run + k + 1, 2) - lax.div(run + 1, 2)
        kd[q] = first
        kd[PLACES + q] = k - first
        nn[q] = n
        run = run + k

    def ring_unit_copy(d, m):
        return pltpu.make_async_remote_copy(
            src_ref=ring_tx.at[d, lax.rem(m, 4)], dst_ref=land.at[d, m],
            send_sem=ag_ss.at[d, lax.rem(m, 4)], recv_sem=ag_rs.at[d, m],
            device_id=(ring_to[d], feat), device_id_type=MESH)

    own_k = (kd[place], kd[PLACES + place])
    prev_k = tuple(kd[d * PLACES + ring_from[d]] for d in (0, 1))
    own_base = (0, own_k[0])
    for m in (0, 1):
        for d in (0, 1):
            c = own_base[d]
            ring_tx[d, m] = x[groups, m, lax.div(c, SPAN), lax.rem(c, SPAN)] if d else x[groups, m, 0, 0]
            ring_unit_copy(d, jnp.int32(m)).start()

    def cot_send(s, carry):
        @pl.when(far_not_me(s))
        def _():
            cot_copy(s).start()

        @pl.when(jnp.logical_not(far_not_me(s)))
        def _():
            cot_rx[blk] = cot_ref[s]

        return carry

    lax.fori_loop(0, 8, cot_send, 0)

    for d in (0, 1):
        run = jnp.int32(0)
        for h in range(1, PLACES + 1):
            at = lax.rem(place + (PLACES - h if d == 0 else h), PLACES)
            start[d * PLACES + at] = run
            run = run + kd[d * PLACES + at]
        tot[d] = run

        def fill(i, carry, d=d):
            h, c = carry
            hc = jnp.minimum(h, PLACES)
            at = lax.rem(place + (2 * PLACES - hc if d == 0 else hc), PLACES)
            chunk = jnp.minimum(c + (0 if d == 0 else kd[at]), 7)
            live = jnp.clip(nn[at] - CHUNK * chunk, 0, CHUNK)
            slot_rc[d * slots + i] = ring_blk(at) * 8 + chunk
            slot_live[d * slots + i] = jnp.where(h <= PLACES, live, 0)
            over = c + 1 >= kd[d * PLACES + at]
            return jnp.where(over, h + 1, h), jnp.where(over, 0, c + 1)

        lax.fori_loop(0, slots, fill, (jnp.int32(1), jnp.int32(0)))

    own_at = (tot[0] - own_k[0], tot[1] - own_k[1])
    held[...] = jnp.zeros_like(held)
    sog_acc[...] = jnp.zeros_like(sog_acc)
    w_copy.wait()

    def ex_copy(slot, g, o):
        to = lax.rem(feat + o, FEATS)
        return pltpu.make_async_remote_copy(
            src_ref=ex_tx.at[slot, to], dst_ref=ex_rx.at[g, feat], send_sem=ex_ss.at[slot, o - 1],
            recv_sem=ex_rs.at[g, feat], device_id=(blk, to), device_id_type=MESH)

    def ex_wait(g, o):
        src = lax.rem(feat + o, FEATS)
        return pltpu.make_async_remote_copy(
            src_ref=ex_tx.at[0, src], dst_ref=ex_rx.at[g, src], send_sem=ex_ss.at[0, o - 1],
            recv_sem=ex_rs.at[g, src], device_id=(blk, src), device_id_type=MESH)

    def gp_copy(g, o):
        to = lax.rem(feat + o, FEATS)
        return pltpu.make_async_remote_copy(
            src_ref=gp.at[g, feat], dst_ref=gp.at[g, feat], send_sem=gp_ss.at[g, o - 1],
            recv_sem=gp_rs.at[g, feat], device_id=(blk, to), device_id_type=MESH)

    def gp_wait(g, o):
        src = lax.rem(feat + o, FEATS)
        return pltpu.make_async_remote_copy(
            src_ref=gp.at[g, src], dst_ref=gp.at[g, src], send_sem=gp_ss.at[g, o - 1],
            recv_sem=gp_rs.at[g, src], device_id=(blk, src), device_id_type=MESH)

    def forward(g):
        slot = lax.rem(g, 2)

        @pl.when(g >= 2)
        def _():
            for o in range(1, FEATS):
                ex_copy(slot, g, o).wait_send()

        for t in range(TOWERS):
            rows = x[g, t].reshape(2 * SPAN * CHUNK, feats_dim)
            for h in range(2):
                out = lax.dot_general(
                    rows, w[t, 2 * h * quarter:2 * (h + 1) * quarter],
                    (((1,), (1,)), ((), ())), preferred_element_type=f32)
                for e in range(2):
                    ex_tx[slot, 2 * h + e, t] = out[:, e * quarter:(e + 1) * quarter].reshape(
                        2 * SPAN, CHUNK, quarter)
        for o in range(1, FEATS):
            ex_copy(slot, g, o).start()
        ex_rx[g, feat] = ex_tx[slot, feat]

    bias_here = bias_ref[:, pl.ds(pl.multiple_of(blk * units + feat * quarter, quarter), quarter)]

    def head(g):
        for o in range(1, FEATS):
            ex_wait(g, o).wait_recv()

        def one(s, carry):
            d, ci = lax.div(s, SPAN), lax.rem(s, SPAN)
            i = g * SPAN + ci
            rc = slot_rc[d * slots + i]
            live = slot_live[d * slots + i]
            mask = jnp.where(
                lax.broadcasted_iota(i32, (CHUNK, quarter), 0) < live, f32(1), f32(0))
            act, slope, cot = [], [], []
            for t in range(TOWERS):
                pre = ex_rx[g, 0, t, s]
                for q in range(1, FEATS):
                    pre = pre + ex_rx[g, q, t, s]
                pre = pre + bias_here[t:t + 1]
                square = pre * pre
                th = jnp.tanh(f32(0.7978845608028654) * (pre + f32(0.044715) * (square * pre)))
                cdf = f32(0.5) * (f32(1) + th)
                act.append(pre * cdf)
                slope.append(cdf + f32(0.5) * pre * (f32(1) - th * th) * (
                    f32(0.7978845608028654) * (f32(1) + f32(3 * 0.044715) * square)))
                cot.append(cot_rx[lax.div(rc, 8), lax.rem(rc, 8), t].astype(f32) * mask)
            for t in range(TOWERS):
                out = so_ref[2 * t:2 * t + 1] * act[0] + so_ref[2 * t + 1:2 * t + 2] * act[1]
                acts[i, d, t] = (out * mask).astype(bf16)
                for u in range(TOWERS):
                    sog_acc[2 * t + u] = sog_acc[2 * t + u] + cot[t] * act[u]
            for u in range(TOWERS):
                back = so_ref[u:u + 1] * cot[0] + so_ref[2 + u:3 + u] * cot[1]
                gp[g, feat, u, s] = (slope[u] * back).astype(bf16)
            return carry

        lax.fori_loop(0, 2 * SPAN, one, 0)
        for o in range(1, FEATS):
            gp_copy(g, o).start()

    tile = feats_dim // 3

    def backward(g):
        for o in range(1, FEATS):
            gp_wait(g, o).wait_recv()
        for t in range(TOWERS):
            rows = jnp.concatenate(
                [gp[g, q, t].reshape(2 * SPAN * CHUNK, quarter) for q in range(FEATS)], axis=1)
            for n in range(3):
                part[t, :, :, n * tile:(n + 1) * tile] = jnp.dot(
                    rows, w[t, :, n * tile:(n + 1) * tile],
                    preferred_element_type=f32).reshape(2 * SPAN, CHUNK, tile)

    wide = feats_dim // 6

    def wg_copy(q):
        return pltpu.make_async_copy(
            wg_tx.at[lax.rem(q, 2)],
            wg_hbm.at[lax.div(q, 6), :, pl.ds(pl.multiple_of(lax.rem(q, 6) * wide, 128), wide)],
            wg_sem.at[lax.rem(q, 2)])

    def weight_tile(q):
        t = lax.div(q, 6)
        cols = pl.ds(pl.multiple_of(lax.rem(q, 6) * wide, 128), wide)

        @pl.when(q >= 2)
        def _():
            wg_copy(q).wait()

        rows = x[0:groups, t, :, :, :, cols].reshape(groups * 2 * SPAN * CHUNK, wide)
        for e in range(FEATS):
            grads = gp[0:groups, e, t].reshape(groups * 2 * SPAN * CHUNK, quarter)
            wg_tx[lax.rem(q, 2), e * quarter:(e + 1) * quarter] = lax.dot_general(
                grads, rows, (((0,), (0,)), ((), ())), preferred_element_type=f32)
        wg_copy(q).start()

    def gather_unit(g, q):
        u = 2 * SPAN * g + q
        ci, t = lax.div(q, 2), lax.rem(q, 2)
        i = SPAN * g + ci
        for d in (0, 1):
            c = jnp.clip(i - own_at[d], 0, own_k[d] - 1) + own_base[d]
            own = x[groups, t, lax.div(c, SPAN), lax.rem(c, SPAN)]

            @pl.when(u < sent)
            def _(d=d, own=own):
                ring_unit_copy(d, u).wait_recv()
                x[g, t, d, ci] = jnp.where(i >= own_at[d], own, land[d, u])

            @pl.when(u >= sent)
            def _(d=d, own=own):
                x[g, t, d, ci] = own

        m = u + 2
        for d in (0, 1):
            @pl.when(m < sent)
            def _(d=d):
                @pl.when(m >= 4)
                def _():
                    ring_unit_copy(d, m).wait_send()

                im = i + 1
                here = im < own_k[d]
                cm = jnp.minimum(im, own_k[d] - 1) + own_base[d]
                src = jnp.maximum(im - own_k[d], 0)
                ring_tx[d, lax.rem(m, 4)] = x[
                    jnp.where(here, groups, lax.div(src, SPAN)), t,
                    jnp.where(here, lax.div(cm, SPAN), d),
                    jnp.where(here, lax.rem(cm, SPAN), lax.rem(src, SPAN))]
                ring_unit_copy(d, m).start()

    def sum_copy(d, v):
        return pltpu.make_async_remote_copy(
            src_ref=sums.at[d, v], dst_ref=sum_rx.at[d, v], send_sem=rs_ss.at[d, v],
            recv_sem=rs_rs.at[d, v], device_id=(ring_to[d], feat), device_id_type=MESH)

    def sum_unit(g, q):
        v = 2 * SPAN * g + q
        ci, t = lax.div(q, 2), lax.rem(q, 2)
        for d in (0, 1):
            @pl.when(jnp.logical_and(v >= 2, v - 2 < sent))
            def _(d=d):
                sum_copy(d, v - 2).wait_recv()
                held[d, lax.rem(v - 2, 8)] = sum_rx[d, v - 2]

            came = held[d, lax.rem(v - 2 * prev_k[d] + 8, 8)].astype(f32)
            value = part[t, d * SPAN + ci] + came * jnp.where(v >= 2 * prev_k[d], f32(1), f32(0))
            sums[d, v] = value.astype(bf16)

            @pl.when(v < sent)
            def _(d=d):
                sum_copy(d, v).start()

    def act_copy(r):
        return pltpu.make_async_remote_copy(
            src_ref=act_tx.at[r], dst_ref=act_rx.at[half_at], send_sem=act_ss.at[r],
            recv_sem=act_rs.at[half_at], device_id=(r, row_feat), device_id_type=MESH)

    def act_wait(s):
        return pltpu.make_async_remote_copy(
            src_ref=act_tx.at[0], dst_ref=act_rx.at[s], send_sem=act_ss.at[0],
            recv_sem=act_rs.at[s], device_id=(blk, feat), device_id_type=MESH)

    def sog_copy(r):
        return pltpu.make_async_remote_copy(
            src_ref=sog_tx, dst_ref=sog_rx.at[half_at], send_sem=sog_ss.at[r],
            recv_sem=sog_rs.at[half_at], device_id=(r, row_feat), device_id_type=MESH)

    def sog_wait(s):
        return pltpu.make_async_remote_copy(
            src_ref=sog_tx, dst_ref=sog_rx.at[s], send_sem=sog_ss.at[0],
            recv_sem=sog_rs.at[s], device_id=(blk, feat), device_id_type=MESH)

    def send_acts():
        sog_tx[...] = jnp.concatenate(
            [jnp.sum(sog_acc[e], axis=0, keepdims=True) for e in range(4)] * 2, axis=0)

        def pick(rc, carry):
            r, c = lax.div(rc, 8), lax.rem(rc, 8)
            at = ring_place(r)
            first, second = kd[at], kd[PLACES + at]
            d = jnp.where(c >= first, 1, 0)
            i = jnp.minimum(start[d * PLACES + at] + c - d * first, slots - 1)
            keep = jnp.where(c < first + second, f32(1), f32(0))
            for t in range(TOWERS):
                act_tx[r, c, t] = (acts[i, d, t].astype(f32) * keep).astype(bf16)
            return carry

        lax.fori_loop(0, PLACES * 8, pick, 0)

        def send(r, carry):
            @pl.when(near_not_me(r))
            def _():
                act_copy(r).start()
                sog_copy(r).start()

            @pl.when(jnp.logical_not(near_not_me(r)))
            def _():
                act_rx[half_at] = act_tx[r]
                sog_rx[half_at] = sog_tx[...]

            return carry

        lax.fori_loop(0, PLACES, send, 0)

    def iteration(it, carry):
        @pl.when(it >= 3)
        def _():
            backward(it - 3)

        @pl.when(it == 2)
        def _():
            def arrived(r, carry):
                @pl.when(near_not_me(r))
                def _():
                    cot_wait(r).wait_recv()

                return carry

            lax.fori_loop(0, PLACES, arrived, 0)

        @pl.when(jnp.logical_and(it >= 2, it < groups + 2))
        def _():
            head(it - 2)

        @pl.when(jnp.logical_and(it >= 1, it < groups + 1))
        def _():
            forward(it - 1)

        @pl.when(it == groups + 1)
        def _():
            send_acts()

        def unit(q, carry):
            @pl.when(it < groups)
            def _():
                gather_unit(it, q)

            @pl.when(it >= 3)
            def _():
                sum_unit(it - 3, q)

            @pl.when(jnp.logical_and(it == groups + 2, q < 6))
            def _():
                weight_tile(2 * q)
                weight_tile(2 * q + 1)

            return carry

        lax.fori_loop(0, 2 * SPAN, unit, 0)
        return carry

    lax.fori_loop(0, groups + 3, iteration, 0)

    for c in range(8):
        d = jnp.where(c >= own_k[0], 1, 0)
        i = jnp.where(c >= own_k[0], own_at[1] + c - own_k[0], own_at[0] + c)
        i = jnp.clip(i, 0, slots - 1)
        keep = jnp.where(c < own_k[0] + own_k[1], f32(1), f32(0))
        for t in range(TOWERS):
            gf_out[c, t] = (sums[d, 2 * i + t].astype(f32) * keep).astype(bf16)

    for e in range(FEATS):
        for t in range(TOWERS):
            def add(g, total, e=e, t=t):
                return total + jnp.sum(gp[g, e, t].astype(f32), axis=0)

            total = lax.fori_loop(0, groups, add, jnp.zeros((CHUNK, quarter), f32))
            bg_out[t:t + 1, e * quarter:(e + 1) * quarter] = jnp.sum(total, axis=0, keepdims=True)

    def finish(s, carry):
        @pl.when(far_not_me(s))
        def _():
            act_wait(s).wait_recv()
            sog_wait(s).wait_recv()
            cot_copy(s).wait_send()

        @pl.when(near_not_me(s))
        def _():
            act_copy(s).wait_send()
            sog_copy(s).wait_send()

        return carry

    lax.fori_loop(0, 8, finish, 0)
    act_out[...] = act_rx[...]
    sog_out[...] = sog_rx[...]

    def finish_sums(v, carry):
        for d in (0, 1):
            sum_copy(d, v).wait_send()
        return carry

    lax.fori_loop(0, sent, finish_sums, 0)
    for m in range(sent - 4, sent):
        for d in (0, 1):
            ring_unit_copy(d, jnp.int32(m)).wait_send()
    for o in range(1, FEATS):
        for g in (groups - 2, groups - 1):
            ex_copy(g % 2, g, o).wait_send()

        def finish_gp(g, carry, o=o):
            gp_copy(g, o).wait_send()
            return carry

        lax.fori_loop(0, groups, finish_gp, 0)
    for q in (10, 11):
        wg_copy(jnp.int32(q)).wait()


def fc_layer(steps, number, n, so, bias, x, cot, weight):
    units, feats_dim = weight.shape[1:]
    quarter = units // FEATS
    groups = -(-steps // SPAN)
    slots = groups * SPAN
    vm = pltpu.VMEM
    dma = pltpu.SemaphoreType.DMA
    sm = pltpu.SMEM
    unit = (CHUNK, feats_dim)
    vmem_spec = pl.BlockSpec(memory_space=pltpu.VMEM)
    any_spec = pl.BlockSpec(memory_space=pl.ANY)
    rows = 2 * slots * CHUNK
    return pl.pallas_call(
        functools.partial(fc_kernel, steps),
        out_shape=(
            jax.ShapeDtypeStruct((8, 8, TOWERS, CHUNK, quarter), bf16),
            jax.ShapeDtypeStruct((8, TOWERS) + unit, bf16),
            jax.ShapeDtypeStruct(weight.shape, f32),
            jax.ShapeDtypeStruct((TOWERS, units), f32),
            jax.ShapeDtypeStruct((8, 8, quarter), f32),
        ),
        in_specs=[pl.BlockSpec(memory_space=pltpu.SMEM)] + [vmem_spec] * 4 + [any_spec],
        out_specs=(vmem_spec, vmem_spec, any_spec, vmem_spec, vmem_spec),
        scratch_shapes=[
            vm(weight.shape, bf16),
            vm((groups + 1, TOWERS, 2, SPAN) + unit, bf16),
            vm((2, 2 * steps - 2) + unit, bf16),
            vm((2, 4) + unit, bf16),
            vm((2, FEATS, TOWERS, 2 * SPAN, CHUNK, quarter), f32),
            vm((groups, FEATS, TOWERS, 2 * SPAN, CHUNK, quarter), f32),
            vm((groups, FEATS, TOWERS, 2 * SPAN, CHUNK, quarter), bf16),
            vm((TOWERS, 2 * SPAN) + unit, f32),
            vm((2, 2 * steps - 2) + unit, bf16),
            vm((2, 8) + unit, bf16),
            vm((2, 2 * slots) + unit, bf16),
            vm((8, 8, TOWERS, CHUNK, quarter), bf16),
            vm((slots, 2, TOWERS, CHUNK, quarter), bf16),
            vm((8, 8, TOWERS, CHUNK, quarter), bf16),
            vm((8, 8, TOWERS, CHUNK, quarter), bf16),
            vm((4, CHUNK, quarter), f32),
            vm((8, quarter), f32),
            vm((8, 8, quarter), f32),
            vm((2, units, feats_dim // 6), f32),
            sm((2 * PLACES,), i32),
            sm((PLACES,), i32),
            sm((2 * PLACES,), i32),
            sm((2,), i32),
            sm((2 * slots,), i32),
            sm((2 * slots,), i32),
            dma,
            dma((2, 4)),
            dma((2, 2 * steps - 2)),
            dma((2, 2 * steps - 2)),
            dma((2, 2 * steps - 2)),
            dma((2, 3)),
            dma((groups, FEATS)),
            dma((groups, 3)),
            dma((groups, FEATS)),
            dma((8,)),
            dma((8,)),
            dma((8,)),
            dma((8,)),
            dma((8,)),
            dma((8,)),
            dma((2,)),
        ],
        cost_estimate=pl.CostEstimate(
            flops=6 * rows * TOWERS * units * feats_dim, bytes_accessed=30 << 20,
            transcendentals=rows * TOWERS * quarter),
        compiler_params=pltpu.CompilerParams(
            collective_id=number, has_side_effects=True, vmem_limit_bytes=60 << 20),
    )(n, so, bias, x, cot, weight)


def layout_matrix(chans):
    table = np.zeros((4 * 2 * chans, 4 * 2 * chans), np.float32)
    for q0 in range(4):
        for c in range(chans):
            for t in range(TOWERS):
                lane = 4 * ((9 * c) % 32) + q0
                table[q0 * 2 * chans + 2 * c + t, (2 * t + c // 32) * 128 + lane] = 1
    return table


def swap_pairs(value):
    lane = lax.broadcasted_iota(i32, value.shape, value.ndim - 1)
    return jnp.where(
        lax.rem(lane, 2) == 0, pltpu.roll(value, 127, value.ndim - 1),
        pltpu.roll(value, 1, value.ndim - 1))


def entry_kernel(
    cc_ref, so_ref, s_ref, perm_ref, conv_ref,
    feats_out, pooled_out, n_out, so_out,
    n_tx, n_rx, so_tx, so_rx, n_ss, n_rs, so_ss, so_rs,
):
    blk, feat = lax.axis_index("blk"), lax.axis_index("feat")
    step = pl.program_id(0)
    holds = lax.div(blk, 2) == feat

    def n_copy(o):
        to = lax.rem(blk + o, PLACES)
        return pltpu.make_async_remote_copy(
            src_ref=n_tx, dst_ref=n_rx.at[blk], send_sem=n_ss.at[o - 1], recv_sem=n_rs.at[blk],
            device_id=(to, feat), device_id_type=MESH)

    def n_wait(o):
        src = lax.rem(blk + o, PLACES)
        return pltpu.make_async_remote_copy(
            src_ref=n_tx, dst_ref=n_rx.at[src], send_sem=n_ss.at[o - 1], recv_sem=n_rs.at[src],
            device_id=(src, feat), device_id_type=MESH)

    def so_copy(o):
        to = lax.rem(feat + o, FEATS)
        return pltpu.make_async_remote_copy(
            src_ref=so_tx.at[to], dst_ref=so_rx, send_sem=so_ss.at[o - 1], recv_sem=so_rs,
            device_id=(blk, to), device_id_type=MESH)

    @pl.when(step == 0)
    def _():
        bar = pltpu.get_barrier_semaphore()
        for o in range(1, PLACES):
            pl.semaphore_signal(
                bar, inc=1, device_id=(lax.rem(blk + o, PLACES), feat), device_id_type=MESH)
        for o in range(1, FEATS):
            pl.semaphore_signal(
                bar, inc=1, device_id=(blk, lax.rem(feat + o, FEATS)), device_id_type=MESH)
        total = cc_ref[0]
        for e in range(1, cc_ref.shape[0]):
            total = total + cc_ref[e]
        n_tx[...] = jnp.full(n_tx.shape, total, i32)
        n_rx[blk] = n_tx[...]
        for q in range(FEATS):
            at = pl.ds(pl.multiple_of(lax.rem(blk, 2) * 512 + q * 128, 128), 128)
            for t in range(TOWERS):
                so_tx[q, 2 * t:2 * t + 2] = so_ref[t, :, at]
                so_tx[q, 4 + 2 * t:6 + 2 * t] = so_ref[t, :, at]
        pl.semaphore_wait(bar, PLACES - 1 + FEATS - 1)
        for o in range(1, PLACES):
            n_copy(o).start()

        @pl.when(holds)
        def _():
            so_rx[...] = so_tx[feat]
            for o in range(1, FEATS):
                so_copy(o).start()

    across = {}
    for row in range(MAP):
        line = [conv_ref[MAP * row + col].astype(f32) for col in range(MAP)]
        for v in range(GRID):
            across[row, v] = line[2 * v] + line[2 * v + 1] + line[2 * v + 2]
    own, other = s_ref[0:1], s_ref[1:2]
    parts = []
    for q1 in range(9):
        here = []
        for q0 in range(4):
            q = 4 * q1 + q0
            u, v = q // GRID, q % GRID
            pooled = (across[2 * u, v] + across[2 * u + 1, v] + across[2 * u + 2, v]) * f32(1 / 9)
            pooled_out[0, q] = pooled
            here.append((own * pooled + other * swap_pairs(pooled)).astype(bf16))
        parts.append(jnp.concatenate(here, axis=1))
    spread = jnp.dot(
        jnp.concatenate(parts, axis=0), perm_ref[...], preferred_element_type=f32)
    slot = lax.div(lax.broadcasted_iota(i32, (CHUNK, 128), 1), 4)
    for t in range(TOWERS):
        for half in range(2):
            at = (2 * t + half) * 128
            turned = [
                pltpu.roll(spread[q1 * CHUNK:(q1 + 1) * CHUNK, at:at + 128], 4 * q1, 1)
                if q1 else spread[0:CHUNK, at:at + 128] for q1 in range(9)]
            for j in range(9):
                source = lax.rem(slot + 32 * j, 9)
                tile = turned[0]
                for q1 in range(1, 9):
                    tile = jnp.where(source == q1, turned[q1], tile)
                feats_out[0, t, :, (9 * half + j) * 128:(9 * half + j + 1) * 128] = tile.astype(bf16)

    @pl.when(step == pl.num_programs(0) - 1)
    def _():
        for o in range(1, PLACES):
            n_wait(o).wait_recv()
            n_copy(o).wait_send()

        @pl.when(holds)
        def _():
            for o in range(1, FEATS):
                so_copy(o).wait_send()

        @pl.when(jnp.logical_not(holds))
        def _():
            so_copy(1).wait_recv()

        n_out[...] = n_rx[...]
        so_out[...] = so_rx[...]


def exit_kernel(
    s_ref, perm_ref, gf_ref, pooled_ref, wg_ref, conv_out, si_out, wg_out, acc,
):
    step = pl.program_id(0)

    @pl.when(step == 0)
    def _():
        acc[...] = jnp.zeros_like(acc)

    wg_out[...] = wg_ref[...]
    slot = lax.div(lax.broadcasted_iota(i32, (CHUNK, 128), 1), 4)
    columns = []
    for t in range(TOWERS):
        for half in range(2):
            tiles = [
                gf_ref[0, t, :, (9 * half + j) * 128:(9 * half + j + 1) * 128].astype(f32)
                for j in range(9)]
            turned = []
            for q1 in range(9):
                source = lax.rem(2 * (q1 - slot) + 72, 9)
                tile = tiles[0]
                for j in range(1, 9):
                    tile = jnp.where(source == j, tiles[j], tile)
                turned.append(pltpu.roll(tile, 128 - 4 * q1, 1) if q1 else tile)
            columns.append(jnp.concatenate(turned, axis=0).astype(bf16))
    grads = lax.dot_general(
        jnp.concatenate(columns, axis=1), perm_ref[...], (((1,), (1,)), ((), ())),
        preferred_element_type=f32)
    own, other = s_ref[0:1] * f32(1 / 9), s_ref[2:3] * f32(1 / 9)
    same = jnp.zeros((CHUNK, 128), f32)
    cross = jnp.zeros((CHUNK, 128), f32)
    back = {}
    for q in range(GRID * GRID):
        q1, q0 = q // 4, q % 4
        grad = grads[q1 * CHUNK:(q1 + 1) * CHUNK, q0 * 128:(q0 + 1) * 128]
        pooled = pooled_ref[0, q]
        swapped = swap_pairs(grad)
        same = same + grad * pooled
        cross = cross + swapped * pooled
        back[q // GRID, q % GRID] = own * grad + other * swapped
    acc[0] = acc[0] + same
    acc[1] = acc[1] + cross
    lines = []
    for u in range(GRID):
        line = []
        for col in range(MAP):
            v = col // 2
            if col % 2:
                line.append(back[u, v])
            elif col == 0:
                line.append(back[u, 0])
            elif col == MAP - 1:
                line.append(back[u, GRID - 1])
            else:
                line.append(back[u, v - 1] + back[u, v])
        lines.append(line)
    for row in range(MAP):
        u = row // 2
        for col in range(MAP):
            if row % 2 or row == 0:
                value = lines[u][col]
            elif row == MAP - 1:
                value = lines[GRID - 1][col]
            else:
                value = lines[u - 1][col] + lines[u][col]
            conv_out[MAP * row + col] = value.astype(bf16)

    @pl.when(step == pl.num_programs(0) - 1)
    def _():
        sums = [jnp.sum(acc[e], axis=0, keepdims=True) for e in range(2)]
        si_out[...] = jnp.concatenate(sums * 4, axis=0)


def total_kernel(x_ref, out, rx, ss, rs):
    blk, feat = lax.axis_index("blk"), lax.axis_index("feat")

    def copy(o):
        return pltpu.make_async_remote_copy(
            src_ref=x_ref, dst_ref=rx.at[blk], send_sem=ss.at[o - 1], recv_sem=rs.at[blk],
            device_id=(lax.rem(blk + o, PLACES), feat), device_id_type=MESH)

    def wait(o):
        src = lax.rem(blk + o, PLACES)
        return pltpu.make_async_remote_copy(
            src_ref=x_ref, dst_ref=rx.at[src], send_sem=ss.at[o - 1], recv_sem=rs.at[src],
            device_id=(src, feat), device_id_type=MESH)

    bar = pltpu.get_barrier_semaphore()
    for o in range(1, PLACES):
        pl.semaphore_signal(
            bar, inc=1, device_id=(lax.rem(blk + o, PLACES), feat), device_id_type=MESH)
    pl.semaphore_wait(bar, PLACES - 1)
    for o in range(1, PLACES):
        copy(o).start()
    rx[blk] = x_ref[...]
    for o in range(1, PLACES):
        wait(o).wait_recv()
    total = rx[0]
    for q in range(1, PLACES):
        total = total + rx[q]
    out[...] = total
    for o in range(1, PLACES):
        copy(o).wait_send()


def entry(counts, so, s_rows, conv):
    spots, rows, merged = conv.shape
    chunks = rows // CHUNK
    chans = merged // TOWERS
    wide = chans * GRID * GRID
    vm, dma = pltpu.VMEM, pltpu.SemaphoreType.DMA
    whole = pl.BlockSpec(memory_space=pltpu.VMEM)
    return pl.pallas_call(
        entry_kernel,
        grid=(chunks,),
        out_shape=(
            jax.ShapeDtypeStruct((chunks, TOWERS, CHUNK, wide), bf16),
            jax.ShapeDtypeStruct((chunks, GRID * GRID, CHUNK, merged), f32),
            jax.ShapeDtypeStruct((PLACES, 8, 128), i32),
            jax.ShapeDtypeStruct((8, 128), f32),
        ),
        in_specs=[pl.BlockSpec(memory_space=pltpu.SMEM)] + [whole] * 3 + [
            pl.BlockSpec((spots, CHUNK, merged), lambda c: (0, c, 0))],
        out_specs=(
            pl.BlockSpec((1, TOWERS, CHUNK, wide), lambda c: (c, 0, 0, 0)),
            pl.BlockSpec((1, GRID * GRID, CHUNK, merged), lambda c: (c, 0, 0, 0)),
            whole, whole,
        ),
        scratch_shapes=[
            vm((8, 128), i32), vm((PLACES, 8, 128), i32), vm((FEATS, 8, 128), f32), vm((8, 128), f32),
            dma((PLACES - 1,)), dma((PLACES,)), dma((FEATS - 1,)), dma,
        ],
        cost_estimate=pl.CostEstimate(flops=1 << 30, bytes_accessed=10 << 20, transcendentals=0),
        compiler_params=pltpu.CompilerParams(
            collective_id=8, has_side_effects=True, vmem_limit_bytes=40 << 20),
    )(counts, so, s_rows, jnp.asarray(layout_matrix(chans), bf16), conv)


def leave(s_rows, gf, pooled, weight_grad, spots):
    chunks, towers, _, wide = gf.shape
    merged = pooled.shape[-1]
    vm = pltpu.VMEM
    whole = pl.BlockSpec(memory_space=pltpu.VMEM)
    share = pl.BlockSpec(
        (towers, weight_grad.shape[1] // chunks, wide), lambda c: (0, c, 0))
    return pl.pallas_call(
        exit_kernel,
        grid=(chunks,),
        out_shape=(
            jax.ShapeDtypeStruct((spots, chunks * CHUNK, merged), bf16),
            jax.ShapeDtypeStruct((8, 128), f32),
            jax.ShapeDtypeStruct(weight_grad.shape, f32),
        ),
        in_specs=[whole] * 2 + [
            pl.BlockSpec((1, towers, CHUNK, wide), lambda c: (c, 0, 0, 0)),
            pl.BlockSpec((1, GRID * GRID, CHUNK, merged), lambda c: (c, 0, 0, 0)),
            share],
        out_specs=(
            pl.BlockSpec((spots, CHUNK, merged), lambda c: (0, c, 0)),
            whole, share,
        ),
        scratch_shapes=[vm((2, CHUNK, 128), f32)],
        cost_estimate=pl.CostEstimate(flops=1 << 30, bytes_accessed=30 << 20, transcendentals=0),
        compiler_params=pltpu.CompilerParams(vmem_limit_bytes=40 << 20),
    )(s_rows, jnp.asarray(layout_matrix(merged // TOWERS), bf16), gf, pooled, weight_grad)


def total_over_blk(value):
    whole = pl.BlockSpec(memory_space=pltpu.VMEM)
    dma = pltpu.SemaphoreType.DMA
    return pl.pallas_call(
        total_kernel,
        out_shape=jax.ShapeDtypeStruct(value.shape, f32),
        in_specs=[whole],
        out_specs=whole,
        scratch_shapes=[
            pltpu.VMEM((PLACES,) + value.shape, f32), dma((PLACES - 1,)), dma((PLACES,))],
        compiler_params=pltpu.CompilerParams(
            collective_id=9, has_side_effects=True, vmem_limit_bytes=16 << 20),
    )(value)


CLASSES = (20, 24)


def body_ring(conv_maps, crop_counts, fc_weight, fc_bias, stitch_in, stitch_out, cotangent):
    num_rows = conv_maps.shape[0]
    merged = conv_maps.shape[2]
    chans = merged // TOWERS
    units = fc_weight.shape[1]
    quarter = units // FEATS
    chunks = num_rows // CHUNK
    own = jnp.stack([stitch_in[0, 0], stitch_in[1, 1]], 1).reshape(1, -1)
    other = jnp.stack([stitch_in[0, 1], stitch_in[1, 0]], 1).reshape(1, -1)
    back = jnp.stack([stitch_in[1, 0], stitch_in[0, 1]], 1).reshape(1, -1)
    s_rows = jnp.concatenate([own, other, back, own], 0)
    feats, pooled, counts, so = entry(
        crop_counts, stitch_out, s_rows, conv_maps.transpose(1, 0, 2))
    n = counts[:, 0, 0]
    cot = cotangent.reshape(chunks, CHUNK, TOWERS, 8, quarter).transpose(3, 0, 2, 1, 4)
    need = lax.div(jnp.sum(lax.div(n + (CHUNK - 1), CHUNK)) + 1, 2)
    full = PLACES * chunks // 2
    kinds = CLASSES + (full,)
    pick = sum(((need > c).astype(i32) for c in CLASSES), jnp.int32(0))
    act, gf, weight_grad, bias_grad, sog = lax.switch(
        pick,
        [functools.partial(fc_layer, steps, at) for at, steps in enumerate(kinds)],
        n, so, fc_bias, feats, cot, fc_weight)
    activations = act.transpose(1, 3, 2, 0, 4).reshape(num_rows, TOWERS, -1)
    stitch_out_grad = sog[:, :4].transpose(1, 0, 2).reshape(TOWERS, TOWERS, -1)
    conv_grad, si, weight_grad = leave(s_rows, gf, pooled, weight_grad, conv_maps.shape[1])
    conv_grad = conv_grad.transpose(1, 0, 2)
    si = total_over_blk(si)
    same, cross = si[0].reshape(chans, TOWERS), si[1].reshape(chans, TOWERS)
    stitch_in_grad = jnp.stack(
        [jnp.stack([same[:, 0], cross[:, 1]]), jnp.stack([cross[:, 0], same[:, 1]])])
    return (activations, conv_grad, weight_grad, bias_grad, stitch_in_grad, stitch_out_grad)


def solution(mesh):
    ring = mesh.shape["blk"] == PLACES and mesh.shape["feat"] == FEATS
    return jax.shard_map(
        body_ring if ring else body_plain,
        mesh=mesh,
        in_specs=(
            P("blk", None, "feat"),
            P("blk"),
            P(None, "blk", "feat"),
            P(),
            P(None, None, "feat"),
            P(None, None, "feat"),
            P("blk", None, "feat"),
        ),
        out_specs=(
            P("blk", None, "feat"),
            P("blk", None, "feat"),
            P(None, "blk", "feat"),
            P(None, "blk"),
            P(None, None, "feat"),
            P(None, None, "feat"),
        ),
        check_vma=False,
    )
```

```python
import functools

import jax
import jax.numpy as jnp
import numpy as np
from jax import lax
from jax.experimental import pallas as pl
from jax.experimental.pallas import tpu as pltpu
from jax.sharding import PartitionSpec as P

MAP = 13
GRID = 6
TOWERS = 2
CHUNK = 16
SPAN = 2
PIECES = 4
HELD = 16
PLACES = 8
FEATS = 4
RING_BLK = (0, 2, 4, 6, 7, 5, 3, 1)
MESH = pl.DeviceIdType.MESH
f32 = jnp.float32
bf16 = jnp.bfloat16
i32 = jnp.int32


def pool_table(dtype):
    position = jnp.arange(MAP * MAP)
    row_pos = position // MAP
    col_pos = position % MAP
    cell = jnp.arange(GRID * GRID)
    row_cell = cell // GRID
    col_cell = cell % GRID
    down = row_pos[:, None] - 2 * row_cell[None, :]
    across = col_pos[:, None] - 2 * col_cell[None, :]
    inside = (down >= 0) & (down < 3) & (across >= 0) & (across < 3)
    return inside.astype(dtype)


def stitch_first(pooled, stitch_in):
    return jnp.einsum("tuc,rucq->rtcq", stitch_in, pooled, precision=lax.Precision.HIGHEST)


def stitch_head(pre, stitch_out):
    act = jax.nn.gelu(pre)
    return jnp.einsum("tuk,ruk->rtk", stitch_out, act, precision=lax.Precision.HIGHEST)


def body_plain(conv_maps, crop_counts, fc_weight, fc_bias, stitch_in, stitch_out, cotangent):
    num_rows = conv_maps.shape[0]
    merged = conv_maps.shape[2]
    chans = merged // TOWERS
    cols = fc_weight.shape[1]
    feat_idx = lax.axis_index("feat")
    blk_idx = lax.axis_index("blk")
    sums = jnp.einsum("rpm,pq->rqm", conv_maps, pool_table(bf16), preferred_element_type=f32)
    pooled = jnp.transpose(sums.reshape(num_rows, GRID * GRID, chans, TOWERS), (0, 3, 2, 1)) * (
        1.0 / 9.0
    )
    mixed, pull_first = jax.vjp(stitch_first, pooled, stitch_in)
    feats = mixed.astype(bf16).reshape(num_rows, TOWERS, -1)
    own_cols = jnp.einsum(
        "rtf,tnf->rtn",
        lax.all_gather(feats, "blk", axis=0, tiled=True),
        fc_weight,
        preferred_element_type=f32,
    )
    partial_value = lax.all_to_all(own_cols, "blk", split_axis=0, concat_axis=2, tiled=True)
    pre = lax.psum_scatter(partial_value, "feat", scatter_dimension=2, tiled=True)
    quarter = pre.shape[2]
    bias_part = lax.dynamic_slice_in_dim(fc_bias, feat_idx * quarter, quarter, 1)
    pre = pre + bias_part[None]
    live = (jnp.arange(num_rows) < jnp.sum(crop_counts)).astype(f32)
    stitched, pull_head = jax.vjp(stitch_head, pre, stitch_out)
    activations = (live[:, None, None] * stitched).astype(bf16)
    grad_out = live[:, None, None] * cotangent.astype(f32)
    grad_pre, grad_so = pull_head(grad_out)
    grad_low = grad_pre.astype(bf16)
    grad_all = lax.all_gather(grad_low, "feat", axis=2, tiled=True)
    bias_terms = jnp.sum(grad_all, axis=0, dtype=f32)
    grad_cols = lax.all_to_all(grad_all, "blk", split_axis=2, concat_axis=0, tiled=True)
    weight_grad = jnp.einsum(
        "rtf,rtn->tnf",
        lax.all_gather(feats, "blk", axis=0, tiled=True),
        grad_cols,
        preferred_element_type=f32,
    )
    grad_feats = jnp.einsum(
        "rtn,tnf->rtf",
        grad_all,
        lax.all_gather(fc_weight, "blk", axis=1, tiled=True),
        preferred_element_type=f32,
    )
    grad_mixed = grad_feats.reshape(num_rows, TOWERS, chans, -1)
    grad_pooled, grad_si = pull_first(grad_mixed)
    spread = jnp.einsum(
        "rtcq,pq->rpct", grad_pooled * (1.0 / 9.0), pool_table(f32), precision=lax.Precision.HIGHEST
    )
    conv_grad = spread.reshape(num_rows, MAP * MAP, merged).astype(bf16)
    stitch_in_grad, stitch_out_grad, bias_total = lax.psum((grad_si, grad_so, bias_terms), "blk")
    bias_grad = lax.dynamic_slice_in_dim(bias_total, blk_idx * cols, cols, 1)
    return (activations, conv_grad, weight_grad, bias_grad, stitch_in_grad, stitch_out_grad)


def ring_place(blk):
    z, x = lax.div(blk, 2), lax.rem(blk, 2)
    return z + x * (7 - 2 * z)


def ring_blk(place):
    x = lax.div(place, 4)
    return 2 * (place + x * (7 - 2 * place)) + x


def fc_kernel(
    steps,
    n_ref, so_ref, bias_ref, x_ref, cot_ref, relay_ref, w_hbm,
    act_out, gf_out, wg_hbm, bg_out, sog_out,
    w, x, land, ring_tx, ex_tx, ex_rx, gp, part, held, sums,
    cot_rx, acts, act_tx, act_rx, sog_acc, sog_tx, sog_rx, wg_acc,
    kd, nn, start, tot, slot_rc, slot_live,
    w_sem, ag_ss, ag_rs, rs_ss, rs_rs, ex_ss, ex_rs, gp_ss, gp_rs,
    cot_ss, cot_rs, act_ss, act_rs, sog_ss, sog_rs, wg_sem, free,
):
    blk, feat = lax.axis_index("blk"), lax.axis_index("feat")
    place = ring_place(blk)
    ring_to = (ring_blk(lax.rem(place + 1, 8)), ring_blk(lax.rem(place + 7, 8)))
    ring_from = (lax.rem(place + 7, 8), lax.rem(place + 1, 8))
    per = 2 * SPAN
    groups = x.shape[0] - 8 // per
    slots = groups * SPAN
    sent = PIECES * (steps - 1)
    part_dim = x.shape[-1]
    units = w.shape[1]
    quarter = units // FEATS
    row_feat = lax.div(blk, 2)
    half_at = lax.rem(blk, 2) * FEATS + feat
    mine = row_feat == feat
    side = 2 * lax.div(feat, 2)
    cot_feat = side + lax.rem(row_feat, 2)
    cot_mine = cot_feat == feat

    w_copy = pltpu.make_async_copy(w_hbm, w, w_sem)
    w_copy.start()

    bar = pltpu.get_barrier_semaphore()

    def hello(dev):
        pl.semaphore_signal(bar, inc=1, device_id=dev, device_id_type=MESH)

    for d in (0, 1):
        hello((ring_to[d], feat))
    for o in range(1, FEATS):
        hello((blk, lax.rem(feat + o, FEATS)))

    def cot_to(s):
        owner = lax.rem(feat + 2 * lax.div(s, 4), FEATS)
        return 2 * owner + lax.rem(lax.div(s, 2), 2), side + lax.rem(s, 2)

    def cot_not_me(s):
        to = cot_to(s)
        return jnp.logical_or(to[0] != blk, to[1] != feat)

    def hello_far(s, carry):
        to = (2 * feat + lax.div(s, FEATS), lax.rem(s, FEATS))

        @pl.when(jnp.logical_or(to[0] != blk, to[1] != feat))
        def _():
            hello(to)

        @pl.when(jnp.logical_or(s != blk, row_feat != feat))
        def _():
            hello((s, row_feat))

        @pl.when(cot_not_me(s))
        def _():
            hello(cot_to(s))

        @pl.when(jnp.logical_or(s != blk, cot_feat != feat))
        def _():
            hello((s, cot_feat))

        return carry

    lax.fori_loop(0, 8, hello_far, 0)
    pl.semaphore_wait(
        bar, jnp.where(mine, 2 + 3 + 14, 2 + 3 + 16) + jnp.where(cot_mine, 14, 16))

    def own_cot(s):
        return lax.div(s, 2) * FEATS + side + lax.rem(s, 2)

    def cot_copy(s, src):
        return pltpu.make_async_remote_copy(
            src_ref=src, dst_ref=cot_rx.at[blk], send_sem=cot_ss.at[s],
            recv_sem=cot_rs.at[blk], device_id=cot_to(s), device_id_type=MESH)

    def cot_wait(r):
        return pltpu.make_async_remote_copy(
            src_ref=cot_ref.at[0], dst_ref=cot_rx.at[r], send_sem=cot_ss.at[0],
            recv_sem=cot_rs.at[r], device_id=(r, cot_feat), device_id_type=MESH)

    def far_not_me(s):
        return jnp.logical_or(2 * feat + lax.div(s, FEATS) != blk, lax.rem(s, FEATS) != feat)

    def near_not_me(r):
        return jnp.logical_or(r != blk, row_feat != feat)

    for c in range(8):
        for t in range(TOWERS):
            for h in range(2):
                x[groups + c // per, t, h, c % per // SPAN, c % SPAN] = x_ref[
                    c, t, :, h * part_dim:(h + 1) * part_dim]

    run = jnp.int32(0)
    for q in range(PLACES):
        n = n_ref[RING_BLK[q]]
        k = jnp.clip(lax.div(n + (CHUNK - 1), CHUNK), 2, 8)
        first = lax.div(run + k + 1, 2) - lax.div(run + 1, 2)
        kd[q] = first
        kd[PLACES + q] = k - first
        nn[q] = n
        run = run + k

    def ring_unit_copy(d, m):
        return pltpu.make_async_remote_copy(
            src_ref=ring_tx.at[d, lax.rem(m, 8)], dst_ref=land.at[d, m],
            send_sem=ag_ss.at[d, lax.rem(m, 8)], recv_sem=ag_rs.at[d, m],
            device_id=(ring_to[d], feat), device_id_type=MESH)

    own_k = (kd[place], kd[PLACES + place])
    prev_k = tuple(kd[d * PLACES + ring_from[d]] for d in (0, 1))
    own_base = (0, own_k[0])

    def own_piece(c, t, h):
        return x[groups + lax.div(c, per), t, h, lax.div(lax.rem(c, per), SPAN), lax.rem(c, SPAN)]

    for m in range(PIECES):
        for d in (0, 1):
            ring_tx[d, m] = own_piece(jnp.int32(own_base[d]), m // 2, m % 2)
            ring_unit_copy(d, jnp.int32(m)).start()

    def cot_send(s, carry):
        @pl.when(cot_not_me(s))
        def _():
            cot_copy(s, cot_ref.at[own_cot(s)]).start()

        @pl.when(jnp.logical_not(cot_not_me(s)))
        def _():
            cot_rx[blk] = cot_ref[own_cot(s)]

        @pl.when(cot_not_me(s + 4))
        def _():
            cot_copy(s + 4, relay_ref.at[s]).start()

        @pl.when(jnp.logical_not(cot_not_me(s + 4)))
        def _():
            cot_rx[blk] = relay_ref[s]

        return carry

    lax.fori_loop(0, 4, cot_send, 0)

    for d in (0, 1):
        run = jnp.int32(0)
        for h in range(1, PLACES + 1):
            at = lax.rem(place + (PLACES - h if d == 0 else h), PLACES)
            start[d * PLACES + at] = run
            run = run + kd[d * PLACES + at]
        tot[d] = run

        def fill(i, carry, d=d):
            h, c = carry
            hc = jnp.minimum(h, PLACES)
            at = lax.rem(place + (2 * PLACES - hc if d == 0 else hc), PLACES)
            chunk = jnp.minimum(c + (0 if d == 0 else kd[at]), 7)
            live = jnp.clip(nn[at] - CHUNK * chunk, 0, CHUNK)
            slot_rc[d * slots + i] = ring_blk(at) * 8 + chunk
            slot_live[d * slots + i] = jnp.where(h <= PLACES, live, 0)
            over = c + 1 >= kd[d * PLACES + at]
            return jnp.where(over, h + 1, h), jnp.where(over, 0, c + 1)

        lax.fori_loop(0, slots, fill, (jnp.int32(1), jnp.int32(0)))

    own_at = (tot[0] - own_k[0], tot[1] - own_k[1])
    held[...] = jnp.zeros_like(held)
    sog_acc[...] = jnp.zeros_like(sog_acc)

    def ex_copy(slot, g, o):
        to = lax.rem(feat + o, FEATS)
        return pltpu.make_async_remote_copy(
            src_ref=ex_tx.at[slot, to], dst_ref=ex_rx.at[g, feat], send_sem=ex_ss.at[slot, o - 1],
            recv_sem=ex_rs.at[g, feat], device_id=(blk, to), device_id_type=MESH)

    def ex_wait(g, o):
        src = lax.rem(feat + o, FEATS)
        return pltpu.make_async_remote_copy(
            src_ref=ex_tx.at[0, src], dst_ref=ex_rx.at[g, src], send_sem=ex_ss.at[0, o - 1],
            recv_sem=ex_rs.at[g, src], device_id=(blk, src), device_id_type=MESH)

    def gp_copy(g, o):
        to = lax.rem(feat + o, FEATS)
        return pltpu.make_async_remote_copy(
            src_ref=gp.at[g, feat], dst_ref=gp.at[g, feat], send_sem=gp_ss.at[g, o - 1],
            recv_sem=gp_rs.at[g, feat], device_id=(blk, to), device_id_type=MESH)

    def gp_wait(g, o):
        src = lax.rem(feat + o, FEATS)
        return pltpu.make_async_remote_copy(
            src_ref=gp.at[g, src], dst_ref=gp.at[g, src], send_sem=gp_ss.at[g, o - 1],
            recv_sem=gp_rs.at[g, src], device_id=(blk, src), device_id_type=MESH)

    def forward(g):
        slot = lax.rem(g, 2)

        @pl.when(g >= 2)
        def _():
            for o in range(1, FEATS):
                ex_copy(slot, g, o).wait_send()

        for t in range(TOWERS):
            for n in range(2):
                out = sum(
                    lax.dot_general(
                        x[g, t, h].reshape(per * CHUNK, part_dim),
                        w[t, 2 * n * quarter:2 * (n + 1) * quarter, h * part_dim:(h + 1) * part_dim],
                        (((1,), (1,)), ((), ())), preferred_element_type=f32)
                    for h in range(2))
                for e in range(2):
                    ex_tx[slot, 2 * n + e, t] = out[:, e * quarter:(e + 1) * quarter].reshape(
                        per, CHUNK, quarter)
        for o in range(1, FEATS):
            ex_copy(slot, g, o).start()
        ex_rx[g, feat] = ex_tx[slot, feat]

    bias_here = bias_ref[:, pl.ds(pl.multiple_of(blk * units + feat * quarter, quarter), quarter)]

    def head(g):
        for o in range(1, FEATS):
            ex_wait(g, o).wait_recv()

        def one(s, carry):
            d, ci = lax.div(s, SPAN), lax.rem(s, SPAN)
            i = g * SPAN + ci
            rc = slot_rc[d * slots + i]
            live = slot_live[d * slots + i]
            mask = jnp.where(
                lax.broadcasted_iota(i32, (CHUNK, quarter), 0) < live, f32(1), f32(0))
            act, slope, cot = [], [], []
            for t in range(TOWERS):
                pre = ex_rx[g, 0, t, s]
                for q in range(1, FEATS):
                    pre = pre + ex_rx[g, q, t, s]
                pre = pre + bias_here[t:t + 1]
                square = pre * pre
                th = jnp.tanh(f32(0.7978845608028654) * (pre + f32(0.044715) * (square * pre)))
                cdf = f32(0.5) * (f32(1) + th)
                act.append(pre * cdf)
                slope.append(cdf + f32(0.5) * pre * (f32(1) - th * th) * (
                    f32(0.7978845608028654) * (f32(1) + f32(3 * 0.044715) * square)))
                cot.append(cot_rx[lax.div(rc, 8), lax.rem(rc, 8), t].astype(f32) * mask)
            for t in range(TOWERS):
                out = so_ref[2 * t:2 * t + 1] * act[0] + so_ref[2 * t + 1:2 * t + 2] * act[1]
                acts[i, d, t] = (out * mask).astype(bf16)
                for u in range(TOWERS):
                    sog_acc[2 * t + u] = sog_acc[2 * t + u] + cot[t] * act[u]
            for u in range(TOWERS):
                back = so_ref[u:u + 1] * cot[0] + so_ref[2 + u:3 + u] * cot[1]
                gp[g, feat, u, s] = (slope[u] * back).astype(bf16)
            return carry

        lax.fori_loop(0, per, one, 0)
        for o in range(1, FEATS):
            gp_copy(g, o).start()

    tile = part_dim // 3

    def backward(g):
        for o in range(1, FEATS):
            gp_wait(g, o).wait_recv()
        for t in range(TOWERS):
            rows = jnp.concatenate(
                [gp[g, q, t].reshape(per * CHUNK, quarter) for q in range(FEATS)], axis=1)
            for h in range(2):
                part[t, h] = jnp.dot(
                    rows, w[t, :, h * part_dim:(h + 1) * part_dim],
                    preferred_element_type=f32).reshape(per, CHUNK, part_dim)

    def tile_at(q):
        t, n = lax.div(q, 6), lax.rem(q, 6)
        return t, lax.div(n, 3), pl.multiple_of(n * tile, 128), pl.multiple_of(lax.rem(n, 3) * tile, 128)

    def wg_copy(q):
        t, _, whole_at, _ = tile_at(q)
        cols = pl.ds(whole_at, tile)
        return pltpu.make_async_copy(wg_acc.at[t, :, cols], wg_hbm.at[t, :, cols], wg_sem.at[q])

    def weight_tile(q, first, count):
        t, h, whole_at, part_at = tile_at(q)
        rows = x[first:first + count, t, h, :, :, :, pl.ds(part_at, tile)].reshape(
            count * per * CHUNK, tile)
        for e in range(FEATS):
            grads = gp[first:first + count, e, t].reshape(count * per * CHUNK, quarter)
            value = lax.dot_general(
                grads, rows, (((0,), (0,)), ((), ())), preferred_element_type=f32)
            at = (t, pl.ds(e * quarter, quarter), pl.ds(whole_at, tile))
            wg_acc[at] = value + wg_acc[at] if first else value

    def gather_unit(g, q):
        u = PIECES * SPAN * g + q
        ci, t, h = lax.div(q, PIECES), lax.rem(lax.div(q, 2), 2), lax.rem(q, 2)
        i = SPAN * g + ci
        for d in (0, 1):
            own = own_piece(jnp.clip(i - own_at[d], 0, own_k[d] - 1) + own_base[d], t, h)

            @pl.when(u < sent)
            def _(d=d, own=own):
                ring_unit_copy(d, u).wait_recv()
                x[g, t, h, d, ci] = jnp.where(i >= own_at[d], own, land[d, u])

            @pl.when(u >= sent)
            def _(d=d, own=own):
                x[g, t, h, d, ci] = own

            m = u + PIECES

            @pl.when(m < sent)
            def _(d=d):
                @pl.when(m >= 8)
                def _():
                    ring_unit_copy(d, m).wait_send()

                here = i + 1 < own_k[d]
                c = jnp.minimum(i + 1, own_k[d] - 1) + own_base[d]
                src = jnp.maximum(i + 1 - own_k[d], 0)
                ring_tx[d, lax.rem(m, 8)] = x[
                    jnp.where(here, groups + lax.div(c, per), lax.div(src, SPAN)), t, h,
                    jnp.where(here, lax.div(lax.rem(c, per), SPAN), d),
                    jnp.where(here, lax.rem(c, SPAN), lax.rem(src, SPAN))]
                ring_unit_copy(d, m).start()

    def sum_copy(d, v):
        return pltpu.make_async_remote_copy(
            src_ref=sums.at[d, v], dst_ref=land.at[d, v], send_sem=rs_ss.at[d, lax.rem(v, HELD)],
            recv_sem=rs_rs.at[d, v], device_id=(ring_to[d], feat), device_id_type=MESH)

    def sum_unit(g, q):
        v = PIECES * SPAN * g + q
        ci, t, h = lax.div(q, PIECES), lax.rem(lax.div(q, 2), 2), lax.rem(q, 2)
        before = v - PIECES
        for d in (0, 1):
            @pl.when(jnp.logical_and(before >= 0, before < sent))
            def _(d=d):
                sum_copy(d, before).wait_recv()
                held[d, lax.rem(before, HELD)] = land[d, before]

            came = held[d, lax.rem(v - PIECES * prev_k[d] + HELD, HELD)].astype(f32)
            value = part[t, h, d * SPAN + ci] + came * jnp.where(
                v >= PIECES * prev_k[d], f32(1), f32(0))
            sums[d, v] = value.astype(bf16)

            @pl.when(v < sent)
            def _(d=d):
                @pl.when(v >= HELD)
                def _():
                    sum_copy(d, v).wait_send()

                sum_copy(d, v).start()

    def act_copy(r):
        return pltpu.make_async_remote_copy(
            src_ref=act_tx.at[r], dst_ref=act_rx.at[half_at], send_sem=act_ss.at[r],
            recv_sem=act_rs.at[half_at], device_id=(r, row_feat), device_id_type=MESH)

    def act_wait(s):
        return pltpu.make_async_remote_copy(
            src_ref=act_tx.at[0], dst_ref=act_rx.at[s], send_sem=act_ss.at[0],
            recv_sem=act_rs.at[s], device_id=(blk, feat), device_id_type=MESH)

    def sog_copy(r):
        return pltpu.make_async_remote_copy(
            src_ref=sog_tx, dst_ref=sog_rx.at[half_at], send_sem=sog_ss.at[r],
            recv_sem=sog_rs.at[half_at], device_id=(r, row_feat), device_id_type=MESH)

    def sog_wait(s):
        return pltpu.make_async_remote_copy(
            src_ref=sog_tx, dst_ref=sog_rx.at[s], send_sem=sog_ss.at[0],
            recv_sem=sog_rs.at[s], device_id=(blk, feat), device_id_type=MESH)

    def send_acts():
        sog_tx[...] = jnp.concatenate(
            [jnp.sum(sog_acc[e], axis=0, keepdims=True) for e in range(4)] * 2, axis=0)

        def pick(rc, carry):
            r, c = lax.div(rc, 8), lax.rem(rc, 8)
            at = ring_place(r)
            first, second = kd[at], kd[PLACES + at]
            d = jnp.where(c >= first, 1, 0)
            i = jnp.minimum(start[d * PLACES + at] + c - d * first, slots - 1)
            keep = jnp.where(c < first + second, f32(1), f32(0))
            for t in range(TOWERS):
                act_tx[r, c, t] = (acts[i, d, t].astype(f32) * keep).astype(bf16)
            return carry

        lax.fori_loop(0, PLACES * 8, pick, 0)

        def send(r, carry):
            @pl.when(near_not_me(r))
            def _():
                act_copy(r).start()
                sog_copy(r).start()

            @pl.when(jnp.logical_not(near_not_me(r)))
            def _():
                act_rx[half_at] = act_tx[r]
                sog_rx[half_at] = sog_tx[...]

            return carry

        lax.fori_loop(0, PLACES, send, 0)

    def add_bias():
        for e in range(FEATS):
            for t in range(TOWERS):
                def add(g, total, e=e, t=t):
                    return total + jnp.sum(gp[g, e, t].astype(f32), axis=0)

                total = lax.fori_loop(0, groups, add, jnp.zeros((CHUNK, quarter), f32))
                bg_out[t:t + 1, e * quarter:(e + 1) * quarter] = jnp.sum(
                    total, axis=0, keepdims=True)

    early = groups - 2

    def iteration(it, carry):
        @pl.when(it >= 3)
        def _():
            backward(it - 3)

        @pl.when(it == groups + 2)
        def _():
            add_bias()

        @pl.when(it == 1)
        def _():
            w_copy.wait()

        @pl.when(it == 2)
        def _():
            def arrived(r, carry):
                @pl.when(jnp.logical_or(r != blk, cot_feat != feat))
                def _():
                    cot_wait(r).wait_recv()

                return carry

            lax.fori_loop(0, PLACES, arrived, 0)

        @pl.when(jnp.logical_and(it >= 2, it < groups + 2))
        def _():
            head(it - 2)

        @pl.when(jnp.logical_and(it >= 1, it < groups + 1))
        def _():
            forward(it - 1)

        @pl.when(it == groups + 1)
        def _():
            send_acts()

        @pl.when(it >= 3)
        def _():
            for d in (0, 1):
                pl.semaphore_wait(free.at[d], 1)

        def unit(q, carry):
            @pl.when(it < groups)
            def _():
                gather_unit(it, q)

            @pl.when(it >= 3)
            def _():
                sum_unit(it - 3, q)

            @pl.when(jnp.logical_and(it == groups, q < 6))
            def _():
                weight_tile(q, 0, early)

            @pl.when(jnp.logical_and(it == groups + 1, q < 6))
            def _():
                weight_tile(q + 6, 0, early)

            @pl.when(jnp.logical_and(it == groups + 2, q < 6))
            def _():
                for e in range(2):
                    weight_tile(2 * q + e, early, 2)
                    wg_copy(2 * q + e).start()

            return carry

        lax.fori_loop(0, PIECES * SPAN, unit, 0)

        @pl.when(it < groups)
        def _():
            for d in (0, 1):
                pl.semaphore_signal(
                    free.at[d], inc=1, device_id=(ring_blk(ring_from[d]), feat), device_id_type=MESH)

        return carry

    lax.fori_loop(0, groups + 3, iteration, 0)

    for c in range(8):
        d = jnp.where(c >= own_k[0], 1, 0)
        i = jnp.where(c >= own_k[0], own_at[1] + c - own_k[0], own_at[0] + c)
        i = jnp.clip(i, 0, slots - 1)
        keep = jnp.where(c < own_k[0] + own_k[1], f32(1), f32(0))
        for t in range(TOWERS):
            for h in range(2):
                gf_out[c, t, :, h * part_dim:(h + 1) * part_dim] = (
                    sums[d, PIECES * i + 2 * t + h].astype(f32) * keep).astype(bf16)

    def finish(s, carry):
        @pl.when(far_not_me(s))
        def _():
            act_wait(s).wait_recv()
            sog_wait(s).wait_recv()

        @pl.when(cot_not_me(s))
        def _():
            cot_copy(s, cot_ref.at[0]).wait_send()

        @pl.when(near_not_me(s))
        def _():
            act_copy(s).wait_send()
            sog_copy(s).wait_send()

        return carry

    lax.fori_loop(0, 8, finish, 0)
    act_out[...] = act_rx[...]
    sog_out[...] = sog_rx[...]

    def finish_sums(v, carry):
        for d in (0, 1):
            sum_copy(d, v).wait_send()
        return carry

    lax.fori_loop(sent - HELD, sent, finish_sums, 0)
    for m in range(sent - 8, sent):
        for d in (0, 1):
            ring_unit_copy(d, jnp.int32(m)).wait_send()
    for o in range(1, FEATS):
        for g in (groups - 2, groups - 1):
            ex_copy(g % 2, g, o).wait_send()

        def finish_gp(g, carry, o=o):
            gp_copy(g, o).wait_send()
            return carry

        lax.fori_loop(0, groups, finish_gp, 0)
    for q in range(12):
        wg_copy(jnp.int32(q)).wait()


def fc_layer(steps, number, n, so, bias, x, cot, relay, weight):
    units, feats_dim = weight.shape[1:]
    quarter = units // FEATS
    groups = -(-steps // SPAN)
    slots = groups * SPAN
    vm = pltpu.VMEM
    dma = pltpu.SemaphoreType.DMA
    sm = pltpu.SMEM
    unit = (CHUNK, feats_dim // 2)
    vmem_spec = pl.BlockSpec(memory_space=pltpu.VMEM)
    any_spec = pl.BlockSpec(memory_space=pl.ANY)
    rows = 2 * slots * CHUNK
    return pl.pallas_call(
        functools.partial(fc_kernel, steps),
        out_shape=(
            jax.ShapeDtypeStruct((8, 8, TOWERS, CHUNK, quarter), bf16),
            jax.ShapeDtypeStruct((8, TOWERS, CHUNK, feats_dim), bf16),
            jax.ShapeDtypeStruct(weight.shape, f32),
            jax.ShapeDtypeStruct((TOWERS, units), f32),
            jax.ShapeDtypeStruct((8, 8, quarter), f32),
        ),
        in_specs=[pl.BlockSpec(memory_space=pltpu.SMEM)] + [vmem_spec] * 5 + [any_spec],
        out_specs=(vmem_spec, vmem_spec, any_spec, vmem_spec, vmem_spec),
        scratch_shapes=[
            vm(weight.shape, bf16),
            vm((groups + 8 // (2 * SPAN), TOWERS, 2, 2, SPAN) + unit, bf16),
            vm((2, PIECES * (steps - 1)) + unit, bf16),
            vm((2, 8) + unit, bf16),
            vm((2, FEATS, TOWERS, 2 * SPAN, CHUNK, quarter), f32),
            vm((groups, FEATS, TOWERS, 2 * SPAN, CHUNK, quarter), f32),
            vm((groups, FEATS, TOWERS, 2 * SPAN, CHUNK, quarter), bf16),
            vm((TOWERS, 2, 2 * SPAN) + unit, f32),
            vm((2, HELD) + unit, bf16),
            vm((2, PIECES * slots) + unit, bf16),
            vm((8, 8, TOWERS, CHUNK, quarter), bf16),
            vm((slots, 2, TOWERS, CHUNK, quarter), bf16),
            vm((8, 8, TOWERS, CHUNK, quarter), bf16),
            vm((8, 8, TOWERS, CHUNK, quarter), bf16),
            vm((4, CHUNK, quarter), f32),
            vm((8, quarter), f32),
            vm((8, 8, quarter), f32),
            vm(weight.shape, f32),
            sm((2 * PLACES,), i32),
            sm((PLACES,), i32),
            sm((2 * PLACES,), i32),
            sm((2,), i32),
            sm((2 * slots,), i32),
            sm((2 * slots,), i32),
            dma,
            dma((2, 8)),
            dma((2, PIECES * (steps - 1))),
            dma((2, HELD)),
            dma((2, PIECES * (steps - 1))),
            dma((2, 3)),
            dma((groups, FEATS)),
            dma((groups, 3)),
            dma((groups, FEATS)),
            dma((8,)),
            dma((8,)),
            dma((8,)),
            dma((8,)),
            dma((8,)),
            dma((8,)),
            dma((12,)),
            pltpu.SemaphoreType.REGULAR((2,)),
        ],
        cost_estimate=pl.CostEstimate(
            flops=6 * rows * TOWERS * units * feats_dim, bytes_accessed=30 << 20,
            transcendentals=rows * TOWERS * quarter),
        compiler_params=pltpu.CompilerParams(
            collective_id=number, has_side_effects=True, vmem_limit_bytes=60 << 20),
    )(n, so, bias, x, cot, relay, weight)


def layout_matrix(chans):
    table = np.zeros((4 * 2 * chans, 4 * 2 * chans), np.float32)
    for q0 in range(4):
        for c in range(chans):
            for t in range(TOWERS):
                lane = 4 * ((9 * c) % 32) + q0
                table[q0 * 2 * chans + 2 * c + t, (2 * t + c // 32) * 128 + lane] = 1
    return table


def swap_pairs(value):
    lane = lax.broadcasted_iota(i32, value.shape, value.ndim - 1)
    return jnp.where(
        lax.rem(lane, 2) == 0, pltpu.roll(value, 127, value.ndim - 1),
        pltpu.roll(value, 1, value.ndim - 1))


def entry_kernel(
    cc_ref, so_ref, s_ref, perm_ref, cot_ref, conv_ref,
    feats_out, pooled_out, n_out, so_out, relay_out,
    n_tx, n_rx, so_tx, so_rx, relay_rx, n_ss, n_rs, so_ss, so_rs, relay_ss, relay_rs,
):
    blk, feat = lax.axis_index("blk"), lax.axis_index("feat")
    step = pl.program_id(0)
    holds = lax.div(blk, 2) == feat

    def n_copy(o):
        to = lax.rem(blk + o, PLACES)
        return pltpu.make_async_remote_copy(
            src_ref=n_tx, dst_ref=n_rx.at[blk], send_sem=n_ss.at[o - 1], recv_sem=n_rs.at[blk],
            device_id=(to, feat), device_id_type=MESH)

    def n_wait(o):
        src = lax.rem(blk + o, PLACES)
        return pltpu.make_async_remote_copy(
            src_ref=n_tx, dst_ref=n_rx.at[src], send_sem=n_ss.at[o - 1], recv_sem=n_rs.at[src],
            device_id=(src, feat), device_id_type=MESH)

    def so_copy(o):
        to = lax.rem(feat + o, FEATS)
        return pltpu.make_async_remote_copy(
            src_ref=so_tx.at[to], dst_ref=so_rx, send_sem=so_ss.at[o - 1], recv_sem=so_rs,
            device_id=(blk, to), device_id_type=MESH)

    across_y = lax.rem(feat + 2, FEATS)

    def relay_copy(s):
        return pltpu.make_async_remote_copy(
            src_ref=cot_ref.at[s // 2 * FEATS + 2 * lax.div(across_y, 2) + s % 2],
            dst_ref=relay_rx.at[s], send_sem=relay_ss.at[s], recv_sem=relay_rs.at[s],
            device_id=(blk, across_y), device_id_type=MESH)

    @pl.when(step == 0)
    def _():
        bar = pltpu.get_barrier_semaphore()
        for o in range(1, PLACES):
            pl.semaphore_signal(
                bar, inc=1, device_id=(lax.rem(blk + o, PLACES), feat), device_id_type=MESH)
        for o in range(1, FEATS):
            pl.semaphore_signal(
                bar, inc=1, device_id=(blk, lax.rem(feat + o, FEATS)), device_id_type=MESH)
        total = cc_ref[0]
        for e in range(1, cc_ref.shape[0]):
            total = total + cc_ref[e]
        n_tx[...] = jnp.full(n_tx.shape, total, i32)
        n_rx[blk] = n_tx[...]
        for q in range(FEATS):
            at = pl.ds(pl.multiple_of(lax.rem(blk, 2) * 512 + q * 128, 128), 128)
            for t in range(TOWERS):
                so_tx[q, 2 * t:2 * t + 2] = so_ref[t, :, at]
                so_tx[q, 4 + 2 * t:6 + 2 * t] = so_ref[t, :, at]
        pl.semaphore_wait(bar, PLACES - 1 + FEATS - 1)
        for o in range(1, PLACES):
            n_copy(o).start()
        for s in range(4):
            relay_copy(s).start()

        @pl.when(holds)
        def _():
            so_rx[...] = so_tx[feat]
            for o in range(1, FEATS):
                so_copy(o).start()

    across = {}
    for row in range(MAP):
        line = [conv_ref[MAP * row + col].astype(f32) for col in range(MAP)]
        for v in range(GRID):
            across[row, v] = line[2 * v] + line[2 * v + 1] + line[2 * v + 2]
    own, other = s_ref[0:1], s_ref[1:2]
    parts = []
    for q1 in range(9):
        here = []
        for q0 in range(4):
            q = 4 * q1 + q0
            u, v = q // GRID, q % GRID
            pooled = (across[2 * u, v] + across[2 * u + 1, v] + across[2 * u + 2, v]) * f32(1 / 9)
            pooled_out[0, q] = pooled
            here.append((own * pooled + other * swap_pairs(pooled)).astype(bf16))
        parts.append(jnp.concatenate(here, axis=1))
    spread = jnp.dot(
        jnp.concatenate(parts, axis=0), perm_ref[...], preferred_element_type=f32)
    slot = lax.div(lax.broadcasted_iota(i32, (CHUNK, 128), 1), 4)
    for t in range(TOWERS):
        for half in range(2):
            at = (2 * t + half) * 128
            turned = [
                pltpu.roll(spread[q1 * CHUNK:(q1 + 1) * CHUNK, at:at + 128], 4 * q1, 1)
                if q1 else spread[0:CHUNK, at:at + 128] for q1 in range(9)]
            for j in range(9):
                source = lax.rem(slot + 32 * j, 9)
                tile = turned[0]
                for q1 in range(1, 9):
                    tile = jnp.where(source == q1, turned[q1], tile)
                feats_out[0, t, :, (9 * half + j) * 128:(9 * half + j + 1) * 128] = tile.astype(bf16)

    @pl.when(step == pl.num_programs(0) - 1)
    def _():
        for o in range(1, PLACES):
            n_wait(o).wait_recv()
            n_copy(o).wait_send()

        @pl.when(holds)
        def _():
            for o in range(1, FEATS):
                so_copy(o).wait_send()

        @pl.when(jnp.logical_not(holds))
        def _():
            so_copy(1).wait_recv()

        for s in range(4):
            relay_copy(s).wait()
        n_out[...] = n_rx[...]
        so_out[...] = so_rx[...]
        relay_out[...] = relay_rx[...]


def exit_kernel(
    s_ref, perm_ref, gf_ref, pooled_ref, wg_ref, conv_out, si_out, wg_out, acc,
):
    step = pl.program_id(0)

    @pl.when(step == 0)
    def _():
        acc[...] = jnp.zeros_like(acc)

    wg_out[...] = wg_ref[...]
    slot = lax.div(lax.broadcasted_iota(i32, (CHUNK, 128), 1), 4)
    columns = []
    for t in range(TOWERS):
        for half in range(2):
            tiles = [
                gf_ref[0, t, :, (9 * half + j) * 128:(9 * half + j + 1) * 128].astype(f32)
                for j in range(9)]
            turned = []
            for q1 in range(9):
                source = lax.rem(2 * (q1 - slot) + 72, 9)
                tile = tiles[0]
                for j in range(1, 9):
                    tile = jnp.where(source == j, tiles[j], tile)
                turned.append(pltpu.roll(tile, 128 - 4 * q1, 1) if q1 else tile)
            columns.append(jnp.concatenate(turned, axis=0).astype(bf16))
    grads = lax.dot_general(
        jnp.concatenate(columns, axis=1), perm_ref[...], (((1,), (1,)), ((), ())),
        preferred_element_type=f32)
    own, other = s_ref[0:1] * f32(1 / 9), s_ref[2:3] * f32(1 / 9)
    same = jnp.zeros((CHUNK, 128), f32)
    cross = jnp.zeros((CHUNK, 128), f32)
    back = {}
    for q in range(GRID * GRID):
        q1, q0 = q // 4, q % 4
        grad = grads[q1 * CHUNK:(q1 + 1) * CHUNK, q0 * 128:(q0 + 1) * 128]
        pooled = pooled_ref[0, q]
        swapped = swap_pairs(grad)
        same = same + grad * pooled
        cross = cross + swapped * pooled
        back[q // GRID, q % GRID] = own * grad + other * swapped
    acc[0] = acc[0] + same
    acc[1] = acc[1] + cross
    lines = []
    for u in range(GRID):
        line = []
        for col in range(MAP):
            v = col // 2
            if col % 2:
                line.append(back[u, v])
            elif col == 0:
                line.append(back[u, 0])
            elif col == MAP - 1:
                line.append(back[u, GRID - 1])
            else:
                line.append(back[u, v - 1] + back[u, v])
        lines.append(line)
    for row in range(MAP):
        u = row // 2
        for col in range(MAP):
            if row % 2 or row == 0:
                value = lines[u][col]
            elif row == MAP - 1:
                value = lines[GRID - 1][col]
            else:
                value = lines[u - 1][col] + lines[u][col]
            conv_out[MAP * row + col] = value.astype(bf16)

    @pl.when(step == pl.num_programs(0) - 1)
    def _():
        sums = [jnp.sum(acc[e], axis=0, keepdims=True) for e in range(2)]
        si_out[...] = jnp.concatenate(sums * 4, axis=0)


def total_kernel(x_ref, out, rx, ss, rs):
    blk, feat = lax.axis_index("blk"), lax.axis_index("feat")

    def copy(o):
        return pltpu.make_async_remote_copy(
            src_ref=x_ref, dst_ref=rx.at[blk], send_sem=ss.at[o - 1], recv_sem=rs.at[blk],
            device_id=(lax.rem(blk + o, PLACES), feat), device_id_type=MESH)

    def wait(o):
        src = lax.rem(blk + o, PLACES)
        return pltpu.make_async_remote_copy(
            src_ref=x_ref, dst_ref=rx.at[src], send_sem=ss.at[o - 1], recv_sem=rs.at[src],
            device_id=(src, feat), device_id_type=MESH)

    bar = pltpu.get_barrier_semaphore()
    for o in range(1, PLACES):
        pl.semaphore_signal(
            bar, inc=1, device_id=(lax.rem(blk + o, PLACES), feat), device_id_type=MESH)
    pl.semaphore_wait(bar, PLACES - 1)
    for o in range(1, PLACES):
        copy(o).start()
    rx[blk] = x_ref[...]
    for o in range(1, PLACES):
        wait(o).wait_recv()
    total = rx[0]
    for q in range(1, PLACES):
        total = total + rx[q]
    out[...] = total
    for o in range(1, PLACES):
        copy(o).wait_send()


def entry(counts, so, s_rows, cot, conv):
    spots, rows, merged = conv.shape
    chunks = rows // CHUNK
    chans = merged // TOWERS
    wide = chans * GRID * GRID
    vm, dma = pltpu.VMEM, pltpu.SemaphoreType.DMA
    whole = pl.BlockSpec(memory_space=pltpu.VMEM)
    return pl.pallas_call(
        entry_kernel,
        grid=(chunks,),
        out_shape=(
            jax.ShapeDtypeStruct((chunks, TOWERS, CHUNK, wide), bf16),
            jax.ShapeDtypeStruct((chunks, GRID * GRID, CHUNK, merged), f32),
            jax.ShapeDtypeStruct((PLACES, 8, 128), i32),
            jax.ShapeDtypeStruct((8, 128), f32),
            jax.ShapeDtypeStruct((4,) + cot.shape[1:], bf16),
        ),
        in_specs=[pl.BlockSpec(memory_space=pltpu.SMEM)] + [whole] * 4 + [
            pl.BlockSpec((spots, CHUNK, merged), lambda c: (0, c, 0))],
        out_specs=(
            pl.BlockSpec((1, TOWERS, CHUNK, wide), lambda c: (c, 0, 0, 0)),
            pl.BlockSpec((1, GRID * GRID, CHUNK, merged), lambda c: (c, 0, 0, 0)),
            whole, whole, whole,
        ),
        scratch_shapes=[
            vm((8, 128), i32), vm((PLACES, 8, 128), i32), vm((FEATS, 8, 128), f32), vm((8, 128), f32),
            vm((4,) + cot.shape[1:], bf16),
            dma((PLACES - 1,)), dma((PLACES,)), dma((FEATS - 1,)), dma, dma((4,)), dma((4,)),
        ],
        cost_estimate=pl.CostEstimate(flops=1 << 30, bytes_accessed=10 << 20, transcendentals=0),
        compiler_params=pltpu.CompilerParams(
            collective_id=20, has_side_effects=True, vmem_limit_bytes=60 << 20),
    )(counts, so, s_rows, jnp.asarray(layout_matrix(chans), bf16), cot, conv)


def leave(s_rows, gf, pooled, weight_grad, spots):
    chunks, towers, _, wide = gf.shape
    merged = pooled.shape[-1]
    vm = pltpu.VMEM
    whole = pl.BlockSpec(memory_space=pltpu.VMEM)
    share = pl.BlockSpec(
        (towers, weight_grad.shape[1] // chunks, wide), lambda c: (0, c, 0))
    return pl.pallas_call(
        exit_kernel,
        grid=(chunks,),
        out_shape=(
            jax.ShapeDtypeStruct((spots, chunks * CHUNK, merged), bf16),
            jax.ShapeDtypeStruct((8, 128), f32),
            jax.ShapeDtypeStruct(weight_grad.shape, f32),
        ),
        in_specs=[whole] * 2 + [
            pl.BlockSpec((1, towers, CHUNK, wide), lambda c: (c, 0, 0, 0)),
            pl.BlockSpec((1, GRID * GRID, CHUNK, merged), lambda c: (c, 0, 0, 0)),
            share],
        out_specs=(
            pl.BlockSpec((spots, CHUNK, merged), lambda c: (0, c, 0)),
            whole, share,
        ),
        scratch_shapes=[vm((2, CHUNK, 128), f32)],
        cost_estimate=pl.CostEstimate(flops=1 << 30, bytes_accessed=30 << 20, transcendentals=0),
        compiler_params=pltpu.CompilerParams(vmem_limit_bytes=60 << 20),
    )(s_rows, jnp.asarray(layout_matrix(merged // TOWERS), bf16), gf, pooled, weight_grad)


def total_over_blk(value):
    whole = pl.BlockSpec(memory_space=pltpu.VMEM)
    dma = pltpu.SemaphoreType.DMA
    return pl.pallas_call(
        total_kernel,
        out_shape=jax.ShapeDtypeStruct(value.shape, f32),
        in_specs=[whole],
        out_specs=whole,
        scratch_shapes=[
            pltpu.VMEM((PLACES,) + value.shape, f32), dma((PLACES - 1,)), dma((PLACES,))],
        compiler_params=pltpu.CompilerParams(
            collective_id=21, has_side_effects=True, vmem_limit_bytes=16 << 20),
    )(value)


CLASSES = (19, 20, 21, 22, 24)


def body_ring(conv_maps, crop_counts, fc_weight, fc_bias, stitch_in, stitch_out, cotangent):
    num_rows = conv_maps.shape[0]
    merged = conv_maps.shape[2]
    chans = merged // TOWERS
    units = fc_weight.shape[1]
    quarter = units // FEATS
    chunks = num_rows // CHUNK
    own = jnp.stack([stitch_in[0, 0], stitch_in[1, 1]], 1).reshape(1, -1)
    other = jnp.stack([stitch_in[0, 1], stitch_in[1, 0]], 1).reshape(1, -1)
    back = jnp.stack([stitch_in[1, 0], stitch_in[0, 1]], 1).reshape(1, -1)
    s_rows = jnp.concatenate([own, other, back, own], 0)
    cot = cotangent.reshape(chunks, CHUNK, TOWERS, 8, quarter).transpose(3, 0, 2, 1, 4)
    feats, pooled, counts, so, relay = entry(
        crop_counts, stitch_out, s_rows, cot, conv_maps.transpose(1, 0, 2))
    n = counts[:, 0, 0]
    need = lax.div(jnp.sum(lax.div(n + (CHUNK - 1), CHUNK)) + 1, 2)
    full = PLACES * chunks // 2
    kinds = CLASSES + (full,)
    pick = sum(((need > c).astype(i32) for c in CLASSES), jnp.int32(0))
    act, gf, weight_grad, bias_grad, sog = lax.switch(
        pick,
        [functools.partial(fc_layer, steps, at) for at, steps in enumerate(kinds)],
        n, so, fc_bias, feats, cot, relay, fc_weight)
    activations = act.transpose(1, 3, 2, 0, 4).reshape(num_rows, TOWERS, -1)
    stitch_out_grad = sog[:, :4].transpose(1, 0, 2).reshape(TOWERS, TOWERS, -1)
    conv_grad, si, weight_grad = leave(s_rows, gf, pooled, weight_grad, conv_maps.shape[1])
    conv_grad = conv_grad.transpose(1, 0, 2)
    si = total_over_blk(si)
    same, cross = si[0].reshape(chans, TOWERS), si[1].reshape(chans, TOWERS)
    stitch_in_grad = jnp.stack(
        [jnp.stack([same[:, 0], cross[:, 1]]), jnp.stack([cross[:, 0], same[:, 1]])])
    return (activations, conv_grad, weight_grad, bias_grad, stitch_in_grad, stitch_out_grad)


def solution(mesh):
    ring = mesh.shape["blk"] == PLACES and mesh.shape["feat"] == FEATS
    return jax.shard_map(
        body_ring if ring else body_plain,
        mesh=mesh,
        in_specs=(
            P("blk", None, "feat"),
            P("blk"),
            P(None, "blk", "feat"),
            P(),
            P(None, None, "feat"),
            P(None, None, "feat"),
            P("blk", None, "feat"),
        ),
        out_specs=(
            P("blk", None, "feat"),
            P("blk", None, "feat"),
            P(None, "blk", "feat"),
            P(None, "blk"),
            P(None, None, "feat"),
            P(None, None, "feat"),
        ),
        check_vma=False,
    )
```

```python
import functools

import jax
import jax.numpy as jnp
import numpy as np
from jax import lax
from jax.experimental import pallas as pl
from jax.experimental.pallas import tpu as pltpu
from jax.sharding import PartitionSpec as P

MAP = 13
GRID = 6
TOWERS = 2
CHUNK = 16
SPAN = 2
PIECES = 4
HELD = 16
PLACES = 8
FEATS = 4
RING_BLK = (0, 2, 4, 6, 7, 5, 3, 1)
MESH = pl.DeviceIdType.MESH
f32 = jnp.float32
bf16 = jnp.bfloat16
i32 = jnp.int32


def pool_table(dtype):
    position = jnp.arange(MAP * MAP)
    row_pos = position // MAP
    col_pos = position % MAP
    cell = jnp.arange(GRID * GRID)
    row_cell = cell // GRID
    col_cell = cell % GRID
    down = row_pos[:, None] - 2 * row_cell[None, :]
    across = col_pos[:, None] - 2 * col_cell[None, :]
    inside = (down >= 0) & (down < 3) & (across >= 0) & (across < 3)
    return inside.astype(dtype)


def stitch_first(pooled, stitch_in):
    return jnp.einsum("tuc,rucq->rtcq", stitch_in, pooled, precision=lax.Precision.HIGHEST)


def stitch_head(pre, stitch_out):
    act = jax.nn.gelu(pre)
    return jnp.einsum("tuk,ruk->rtk", stitch_out, act, precision=lax.Precision.HIGHEST)


def body_plain(conv_maps, crop_counts, fc_weight, fc_bias, stitch_in, stitch_out, cotangent):
    num_rows = conv_maps.shape[0]
    merged = conv_maps.shape[2]
    chans = merged // TOWERS
    cols = fc_weight.shape[1]
    feat_idx = lax.axis_index("feat")
    blk_idx = lax.axis_index("blk")
    sums = jnp.einsum("rpm,pq->rqm", conv_maps, pool_table(bf16), preferred_element_type=f32)
    pooled = jnp.transpose(sums.reshape(num_rows, GRID * GRID, chans, TOWERS), (0, 3, 2, 1)) * (
        1.0 / 9.0
    )
    mixed, pull_first = jax.vjp(stitch_first, pooled, stitch_in)
    feats = mixed.astype(bf16).reshape(num_rows, TOWERS, -1)
    own_cols = jnp.einsum(
        "rtf,tnf->rtn",
        lax.all_gather(feats, "blk", axis=0, tiled=True),
        fc_weight,
        preferred_element_type=f32,
    )
    partial_value = lax.all_to_all(own_cols, "blk", split_axis=0, concat_axis=2, tiled=True)
    pre = lax.psum_scatter(partial_value, "feat", scatter_dimension=2, tiled=True)
    quarter = pre.shape[2]
    bias_part = lax.dynamic_slice_in_dim(fc_bias, feat_idx * quarter, quarter, 1)
    pre = pre + bias_part[None]
    live = (jnp.arange(num_rows) < jnp.sum(crop_counts)).astype(f32)
    stitched, pull_head = jax.vjp(stitch_head, pre, stitch_out)
    activations = (live[:, None, None] * stitched).astype(bf16)
    grad_out = live[:, None, None] * cotangent.astype(f32)
    grad_pre, grad_so = pull_head(grad_out)
    grad_low = grad_pre.astype(bf16)
    grad_all = lax.all_gather(grad_low, "feat", axis=2, tiled=True)
    bias_terms = jnp.sum(grad_all, axis=0, dtype=f32)
    grad_cols = lax.all_to_all(grad_all, "blk", split_axis=2, concat_axis=0, tiled=True)
    weight_grad = jnp.einsum(
        "rtf,rtn->tnf",
        lax.all_gather(feats, "blk", axis=0, tiled=True),
        grad_cols,
        preferred_element_type=f32,
    )
    grad_feats = jnp.einsum(
        "rtn,tnf->rtf",
        grad_all,
        lax.all_gather(fc_weight, "blk", axis=1, tiled=True),
        preferred_element_type=f32,
    )
    grad_mixed = grad_feats.reshape(num_rows, TOWERS, chans, -1)
    grad_pooled, grad_si = pull_first(grad_mixed)
    spread = jnp.einsum(
        "rtcq,pq->rpct", grad_pooled * (1.0 / 9.0), pool_table(f32), precision=lax.Precision.HIGHEST
    )
    conv_grad = spread.reshape(num_rows, MAP * MAP, merged).astype(bf16)
    stitch_in_grad, stitch_out_grad, bias_total = lax.psum((grad_si, grad_so, bias_terms), "blk")
    bias_grad = lax.dynamic_slice_in_dim(bias_total, blk_idx * cols, cols, 1)
    return (activations, conv_grad, weight_grad, bias_grad, stitch_in_grad, stitch_out_grad)


def ring_place(blk):
    z, x = lax.div(blk, 2), lax.rem(blk, 2)
    return z + x * (7 - 2 * z)


def ring_blk(place):
    x = lax.div(place, 4)
    return 2 * (place + x * (7 - 2 * place)) + x


def fc_kernel(
    steps,
    n_ref, so_ref, bias_ref, x_ref, first_ref, cot_ref, relay_ref, w_hbm,
    act_out, gf_out, wg_hbm, bg_out, sog_out,
    w, x, land, ring_tx, ex_tx, ex_rx, gp, part, held, sums,
    cot_rx, acts, act_tx, act_rx, sog_acc, sog_tx, sog_rx, wg_acc,
    kd, nn, start, tot, slot_rc, slot_live,
    w_sem, ag_ss, ag_rs, rs_ss, rs_rs, ex_ss, ex_rs, gp_ss, gp_rs,
    cot_ss, cot_rs, act_ss, act_rs, sog_ss, sog_rs, wg_sem, free,
):
    blk, feat = lax.axis_index("blk"), lax.axis_index("feat")
    place = ring_place(blk)
    ring_to = (ring_blk(lax.rem(place + 1, 8)), ring_blk(lax.rem(place + 7, 8)))
    ring_from = (lax.rem(place + 7, 8), lax.rem(place + 1, 8))
    per = 2 * SPAN
    groups = x.shape[0] - 8 // per
    slots = groups * SPAN
    sent = PIECES * (steps - 1)
    part_dim = x.shape[-1]
    units = w.shape[1]
    quarter = units // FEATS
    row_feat = lax.div(blk, 2)
    half_at = lax.rem(blk, 2) * FEATS + feat
    mine = row_feat == feat
    side = 2 * lax.div(feat, 2)
    cot_feat = side + lax.rem(row_feat, 2)
    cot_mine = cot_feat == feat

    w_copy = pltpu.make_async_copy(w_hbm, w, w_sem)
    w_copy.start()

    bar = pltpu.get_barrier_semaphore()

    def hello(dev):
        pl.semaphore_signal(bar, inc=1, device_id=dev, device_id_type=MESH)

    for d in (0, 1):
        hello((ring_to[d], feat))
    for o in range(1, FEATS):
        hello((blk, lax.rem(feat + o, FEATS)))

    def cot_to(s):
        owner = lax.rem(feat + 2 * lax.div(s, 4), FEATS)
        return 2 * owner + lax.rem(lax.div(s, 2), 2), side + lax.rem(s, 2)

    def cot_not_me(s):
        to = cot_to(s)
        return jnp.logical_or(to[0] != blk, to[1] != feat)

    def hello_far(s, carry):
        to = (2 * feat + lax.div(s, FEATS), lax.rem(s, FEATS))

        @pl.when(jnp.logical_or(to[0] != blk, to[1] != feat))
        def _():
            hello(to)

        @pl.when(jnp.logical_or(s != blk, row_feat != feat))
        def _():
            hello((s, row_feat))

        @pl.when(cot_not_me(s))
        def _():
            hello(cot_to(s))

        @pl.when(jnp.logical_or(s != blk, cot_feat != feat))
        def _():
            hello((s, cot_feat))

        return carry

    lax.fori_loop(0, 8, hello_far, 0)

    for d in (0, 1):
        for m in range(PIECES):
            land[d, m] = first_ref[d, m]

    def own_cot(s):
        return lax.div(s, 2) * FEATS + side + lax.rem(s, 2)

    def cot_copy(s, src):
        return pltpu.make_async_remote_copy(
            src_ref=src, dst_ref=cot_rx.at[blk], send_sem=cot_ss.at[s],
            recv_sem=cot_rs.at[blk], device_id=cot_to(s), device_id_type=MESH)

    def cot_wait(r):
        return pltpu.make_async_remote_copy(
            src_ref=cot_ref.at[0], dst_ref=cot_rx.at[r], send_sem=cot_ss.at[0],
            recv_sem=cot_rs.at[r], device_id=(r, cot_feat), device_id_type=MESH)

    def far_not_me(s):
        return jnp.logical_or(2 * feat + lax.div(s, FEATS) != blk, lax.rem(s, FEATS) != feat)

    def near_not_me(r):
        return jnp.logical_or(r != blk, row_feat != feat)

    for c in range(8):
        for t in range(TOWERS):
            for h in range(2):
                x[groups + c // per, t, h, c % per // SPAN, c % SPAN] = x_ref[
                    c, t, :, h * part_dim:(h + 1) * part_dim]

    run = jnp.int32(0)
    for q in range(PLACES):
        n = n_ref[RING_BLK[q]]
        k = jnp.clip(lax.div(n + (CHUNK - 1), CHUNK), 2, 8)
        first = lax.div(run + k + 1, 2) - lax.div(run + 1, 2)
        kd[q] = first
        kd[PLACES + q] = k - first
        nn[q] = n
        run = run + k

    def ring_unit_copy(d, m):
        return pltpu.make_async_remote_copy(
            src_ref=ring_tx.at[d, lax.rem(m, 8)], dst_ref=land.at[d, m],
            send_sem=ag_ss.at[d, lax.rem(m, 8)], recv_sem=ag_rs.at[d, m],
            device_id=(ring_to[d], feat), device_id_type=MESH)

    own_k = (kd[place], kd[PLACES + place])
    prev_k = tuple(kd[d * PLACES + ring_from[d]] for d in (0, 1))

    def chunk_of(d, c, first):
        return jnp.where(c == 0, d, (c + 1 if d == 0 else first + c))

    def own_piece(d, pos, t, h):
        c = chunk_of(d, pos, own_k[0])
        return x[groups + lax.div(c, per), t, h, lax.div(lax.rem(c, per), SPAN), lax.rem(c, SPAN)]

    def cot_send(s, carry):
        @pl.when(cot_not_me(s))
        def _():
            cot_copy(s, cot_ref.at[own_cot(s)]).start()

        @pl.when(jnp.logical_not(cot_not_me(s)))
        def _():
            cot_rx[blk] = cot_ref[own_cot(s)]

        @pl.when(cot_not_me(s + 4))
        def _():
            cot_copy(s + 4, relay_ref.at[s]).start()

        @pl.when(jnp.logical_not(cot_not_me(s + 4)))
        def _():
            cot_rx[blk] = relay_ref[s]

        return carry


    for d in (0, 1):
        run = jnp.int32(0)
        for h in range(1, PLACES + 1):
            at = lax.rem(place + (PLACES - h if d == 0 else h), PLACES)
            start[d * PLACES + at] = run
            run = run + kd[d * PLACES + at]
        tot[d] = run

        def fill(i, carry, d=d):
            h, c = carry
            hc = jnp.minimum(h, PLACES)
            at = lax.rem(place + (2 * PLACES - hc if d == 0 else hc), PLACES)
            chunk = jnp.minimum(chunk_of(d, c, kd[at]), 7)
            live = jnp.clip(nn[at] - CHUNK * chunk, 0, CHUNK)
            slot_rc[d * slots + i] = ring_blk(at) * 8 + chunk
            slot_live[d * slots + i] = jnp.where(h <= PLACES, live, 0)
            over = c + 1 >= kd[d * PLACES + at]
            return jnp.where(over, h + 1, h), jnp.where(over, 0, c + 1)

        lax.fori_loop(0, slots, fill, (jnp.int32(1), jnp.int32(0)))

    own_at = (tot[0] - own_k[0], tot[1] - own_k[1])
    held[...] = jnp.zeros_like(held)
    sog_acc[...] = jnp.zeros_like(sog_acc)
    pl.semaphore_wait(
        bar, jnp.where(mine, 2 + 3 + 14, 2 + 3 + 16) + jnp.where(cot_mine, 14, 16))
    lax.fori_loop(0, 4, cot_send, 0)

    def ex_copy(slot, g, o):
        to = lax.rem(feat + o, FEATS)
        return pltpu.make_async_remote_copy(
            src_ref=ex_tx.at[slot, to], dst_ref=ex_rx.at[g, feat], send_sem=ex_ss.at[slot, o - 1],
            recv_sem=ex_rs.at[g, feat], device_id=(blk, to), device_id_type=MESH)

    def ex_wait(g, o):
        src = lax.rem(feat + o, FEATS)
        return pltpu.make_async_remote_copy(
            src_ref=ex_tx.at[0, src], dst_ref=ex_rx.at[g, src], send_sem=ex_ss.at[0, o - 1],
            recv_sem=ex_rs.at[g, src], device_id=(blk, src), device_id_type=MESH)

    def gp_copy(g, o):
        to = lax.rem(feat + o, FEATS)
        return pltpu.make_async_remote_copy(
            src_ref=gp.at[g, feat], dst_ref=gp.at[g, feat], send_sem=gp_ss.at[g, o - 1],
            recv_sem=gp_rs.at[g, feat], device_id=(blk, to), device_id_type=MESH)

    def gp_wait(g, o):
        src = lax.rem(feat + o, FEATS)
        return pltpu.make_async_remote_copy(
            src_ref=gp.at[g, src], dst_ref=gp.at[g, src], send_sem=gp_ss.at[g, o - 1],
            recv_sem=gp_rs.at[g, src], device_id=(blk, src), device_id_type=MESH)

    def forward(g):
        slot = lax.rem(g, 2)

        @pl.when(g >= 2)
        def _():
            for o in range(1, FEATS):
                ex_copy(slot, g, o).wait_send()

        for t in range(TOWERS):
            for n in range(2):
                out = sum(
                    lax.dot_general(
                        x[g, t, h].reshape(per * CHUNK, part_dim),
                        w[t, 2 * n * quarter:2 * (n + 1) * quarter, h * part_dim:(h + 1) * part_dim],
                        (((1,), (1,)), ((), ())), preferred_element_type=f32)
                    for h in range(2))
                for e in range(2):
                    ex_tx[slot, 2 * n + e, t] = out[:, e * quarter:(e + 1) * quarter].reshape(
                        per, CHUNK, quarter)
        for o in range(1, FEATS):
            ex_copy(slot, g, o).start()
        ex_rx[g, feat] = ex_tx[slot, feat]

    bias_here = bias_ref[:, pl.ds(pl.multiple_of(blk * units + feat * quarter, quarter), quarter)]

    def head(g):
        for o in range(1, FEATS):
            ex_wait(g, o).wait_recv()

        def one(s, carry):
            d, ci = lax.div(s, SPAN), lax.rem(s, SPAN)
            i = g * SPAN + ci
            rc = slot_rc[d * slots + i]
            live = slot_live[d * slots + i]
            mask = jnp.where(
                lax.broadcasted_iota(i32, (CHUNK, quarter), 0) < live, f32(1), f32(0))
            act, slope, cot = [], [], []
            for t in range(TOWERS):
                pre = ex_rx[g, 0, t, s]
                for q in range(1, FEATS):
                    pre = pre + ex_rx[g, q, t, s]
                pre = pre + bias_here[t:t + 1]
                square = pre * pre
                th = jnp.tanh(f32(0.7978845608028654) * (pre + f32(0.044715) * (square * pre)))
                cdf = f32(0.5) * (f32(1) + th)
                act.append(pre * cdf)
                slope.append(cdf + f32(0.5) * pre * (f32(1) - th * th) * (
                    f32(0.7978845608028654) * (f32(1) + f32(3 * 0.044715) * square)))
                cot.append(cot_rx[lax.div(rc, 8), lax.rem(rc, 8), t].astype(f32) * mask)
            for t in range(TOWERS):
                out = so_ref[2 * t:2 * t + 1] * act[0] + so_ref[2 * t + 1:2 * t + 2] * act[1]
                acts[i, d, t] = (out * mask).astype(bf16)
                for u in range(TOWERS):
                    sog_acc[2 * t + u] = sog_acc[2 * t + u] + cot[t] * act[u]
            for u in range(TOWERS):
                back = so_ref[u:u + 1] * cot[0] + so_ref[2 + u:3 + u] * cot[1]
                gp[g, feat, u, s] = (slope[u] * back).astype(bf16)
            return carry

        lax.fori_loop(0, per, one, 0)
        for o in range(1, FEATS):
            gp_copy(g, o).start()

    tile = part_dim // 3

    def backward(g):
        for o in range(1, FEATS):
            gp_wait(g, o).wait_recv()
        for t in range(TOWERS):
            rows = jnp.concatenate(
                [gp[g, q, t].reshape(per * CHUNK, quarter) for q in range(FEATS)], axis=1)
            for h in range(2):
                part[t, h] = jnp.dot(
                    rows, w[t, :, h * part_dim:(h + 1) * part_dim],
                    preferred_element_type=f32).reshape(per, CHUNK, part_dim)

    def tile_at(q):
        t, n = lax.div(q, 6), lax.rem(q, 6)
        return t, lax.div(n, 3), pl.multiple_of(n * tile, 128), pl.multiple_of(lax.rem(n, 3) * tile, 128)

    def wg_copy(q):
        t, _, whole_at, _ = tile_at(q)
        cols = pl.ds(whole_at, tile)
        return pltpu.make_async_copy(wg_acc.at[t, :, cols], wg_hbm.at[t, :, cols], wg_sem.at[q])

    def weight_tile(q, first, count):
        t, h, whole_at, part_at = tile_at(q)
        rows = x[first:first + count, t, h, :, :, :, pl.ds(part_at, tile)].reshape(
            count * per * CHUNK, tile)
        for e in range(FEATS):
            grads = gp[first:first + count, e, t].reshape(count * per * CHUNK, quarter)
            value = lax.dot_general(
                grads, rows, (((0,), (0,)), ((), ())), preferred_element_type=f32)
            at = (t, pl.ds(e * quarter, quarter), pl.ds(whole_at, tile))
            wg_acc[at] = value + wg_acc[at] if first else value

    def gather_unit(g, q):
        u = PIECES * SPAN * g + q
        ci, t, h = lax.div(q, PIECES), lax.rem(lax.div(q, 2), 2), lax.rem(q, 2)
        i = SPAN * g + ci
        for d in (0, 1):
            own = own_piece(d, jnp.clip(i - own_at[d], 0, own_k[d] - 1), t, h)

            @pl.when(u < sent)
            def _(d=d, own=own):
                @pl.when(u >= PIECES)
                def _():
                    ring_unit_copy(d, u).wait_recv()

                x[g, t, h, d, ci] = jnp.where(i >= own_at[d], own, land[d, u])

            @pl.when(u >= sent)
            def _(d=d, own=own):
                x[g, t, h, d, ci] = own

            m = u + PIECES

            @pl.when(m < sent)
            def _(d=d):
                @pl.when(m >= 8 + PIECES)
                def _():
                    ring_unit_copy(d, m).wait_send()

                here = i + 1 < own_k[d]
                c = chunk_of(d, jnp.minimum(i + 1, own_k[d] - 1), own_k[0])
                src = jnp.maximum(i + 1 - own_k[d], 0)
                ring_tx[d, lax.rem(m, 8)] = x[
                    jnp.where(here, groups + lax.div(c, per), lax.div(src, SPAN)), t, h,
                    jnp.where(here, lax.div(lax.rem(c, per), SPAN), d),
                    jnp.where(here, lax.rem(c, SPAN), lax.rem(src, SPAN))]
                ring_unit_copy(d, m).start()

    def sum_copy(d, v):
        return pltpu.make_async_remote_copy(
            src_ref=sums.at[d, v], dst_ref=land.at[d, v], send_sem=rs_ss.at[d, lax.rem(v, HELD)],
            recv_sem=rs_rs.at[d, v], device_id=(ring_to[d], feat), device_id_type=MESH)

    def sum_unit(g, q):
        v = PIECES * SPAN * g + q
        ci, t, h = lax.div(q, PIECES), lax.rem(lax.div(q, 2), 2), lax.rem(q, 2)
        before = v - PIECES
        for d in (0, 1):
            @pl.when(jnp.logical_and(before >= 0, before < sent))
            def _(d=d):
                sum_copy(d, before).wait_recv()
                held[d, lax.rem(before, HELD)] = land[d, before]

            came = held[d, lax.rem(v - PIECES * prev_k[d] + HELD, HELD)].astype(f32)
            value = part[t, h, d * SPAN + ci] + came * jnp.where(
                v >= PIECES * prev_k[d], f32(1), f32(0))
            sums[d, v] = value.astype(bf16)

            @pl.when(v < sent)
            def _(d=d):
                @pl.when(v >= HELD)
                def _():
                    sum_copy(d, v).wait_send()

                sum_copy(d, v).start()

    def act_copy(r):
        return pltpu.make_async_remote_copy(
            src_ref=act_tx.at[r], dst_ref=act_rx.at[half_at], send_sem=act_ss.at[r],
            recv_sem=act_rs.at[half_at], device_id=(r, row_feat), device_id_type=MESH)

    def act_wait(s):
        return pltpu.make_async_remote_copy(
            src_ref=act_tx.at[0], dst_ref=act_rx.at[s], send_sem=act_ss.at[0],
            recv_sem=act_rs.at[s], device_id=(blk, feat), device_id_type=MESH)

    def sog_copy(r):
        return pltpu.make_async_remote_copy(
            src_ref=sog_tx, dst_ref=sog_rx.at[half_at], send_sem=sog_ss.at[r],
            recv_sem=sog_rs.at[half_at], device_id=(r, row_feat), device_id_type=MESH)

    def sog_wait(s):
        return pltpu.make_async_remote_copy(
            src_ref=sog_tx, dst_ref=sog_rx.at[s], send_sem=sog_ss.at[0],
            recv_sem=sog_rs.at[s], device_id=(blk, feat), device_id_type=MESH)

    def send_acts():
        sog_tx[...] = jnp.concatenate(
            [jnp.sum(sog_acc[e], axis=0, keepdims=True) for e in range(4)] * 2, axis=0)

        def pick(rc, carry):
            r, c = lax.div(rc, 8), lax.rem(rc, 8)
            at = ring_place(r)
            first, second = kd[at], kd[PLACES + at]
            d = jnp.where(jnp.logical_or(c == 1, c > first), 1, 0)
            pos = jnp.where(c < 2, 0, jnp.where(c > first, c - first, c - 1))
            i = jnp.minimum(start[d * PLACES + at] + pos, slots - 1)
            keep = jnp.where(c < first + second, f32(1), f32(0))
            for t in range(TOWERS):
                act_tx[r, c, t] = (acts[i, d, t].astype(f32) * keep).astype(bf16)
            return carry

        lax.fori_loop(0, PLACES * 8, pick, 0)

        def send(r, carry):
            @pl.when(near_not_me(r))
            def _():
                act_copy(r).start()
                sog_copy(r).start()

            @pl.when(jnp.logical_not(near_not_me(r)))
            def _():
                act_rx[half_at] = act_tx[r]
                sog_rx[half_at] = sog_tx[...]

            return carry

        lax.fori_loop(0, PLACES, send, 0)

    def add_bias():
        for e in range(FEATS):
            for t in range(TOWERS):
                def add(g, total, e=e, t=t):
                    return total + jnp.sum(gp[g, e, t].astype(f32), axis=0)

                total = lax.fori_loop(0, groups, add, jnp.zeros((CHUNK, quarter), f32))
                bg_out[t:t + 1, e * quarter:(e + 1) * quarter] = jnp.sum(
                    total, axis=0, keepdims=True)

    early = groups - 2

    def iteration(it, carry):
        @pl.when(it >= 3)
        def _():
            backward(it - 3)

        @pl.when(it == groups + 2)
        def _():
            add_bias()

        @pl.when(it == 1)
        def _():
            w_copy.wait()

        @pl.when(it == 2)
        def _():
            def arrived(r, carry):
                @pl.when(jnp.logical_or(r != blk, cot_feat != feat))
                def _():
                    cot_wait(r).wait_recv()

                return carry

            lax.fori_loop(0, PLACES, arrived, 0)

        @pl.when(jnp.logical_and(it >= 2, it < groups + 2))
        def _():
            head(it - 2)

        @pl.when(jnp.logical_and(it >= 1, it < groups + 1))
        def _():
            forward(it - 1)

        @pl.when(it == groups + 1)
        def _():
            send_acts()

        @pl.when(it >= 3)
        def _():
            for d in (0, 1):
                pl.semaphore_wait(free.at[d], 1)

        def unit(q, carry):
            @pl.when(it < groups)
            def _():
                gather_unit(it, q)

            @pl.when(it >= 3)
            def _():
                sum_unit(it - 3, q)

            @pl.when(jnp.logical_and(it == groups, q < 6))
            def _():
                weight_tile(q, 0, early)

            @pl.when(jnp.logical_and(it == groups + 1, q < 6))
            def _():
                weight_tile(q + 6, 0, early)

            @pl.when(jnp.logical_and(it == groups + 2, q < 6))
            def _():
                for e in range(2):
                    weight_tile(2 * q + e, early, 2)
                    wg_copy(2 * q + e).start()

            return carry

        lax.fori_loop(0, PIECES * SPAN, unit, 0)

        @pl.when(it < groups)
        def _():
            for d in (0, 1):
                pl.semaphore_signal(
                    free.at[d], inc=1, device_id=(ring_blk(ring_from[d]), feat), device_id_type=MESH)

        return carry

    lax.fori_loop(0, groups + 3, iteration, 0)

    for c in range(8):
        late = c > own_k[0]
        d = jnp.where(late, 1, 0) if c > 1 else c
        i = jnp.where(late, own_at[1] + c - own_k[0], own_at[0] + c - 1) if c > 1 else own_at[c]
        i = jnp.clip(i, 0, slots - 1)
        keep = jnp.where(c < own_k[0] + own_k[1], f32(1), f32(0))
        for t in range(TOWERS):
            for h in range(2):
                gf_out[c, t, :, h * part_dim:(h + 1) * part_dim] = (
                    sums[d, PIECES * i + 2 * t + h].astype(f32) * keep).astype(bf16)

    def finish(s, carry):
        @pl.when(far_not_me(s))
        def _():
            act_wait(s).wait_recv()
            sog_wait(s).wait_recv()

        @pl.when(cot_not_me(s))
        def _():
            cot_copy(s, cot_ref.at[0]).wait_send()

        @pl.when(near_not_me(s))
        def _():
            act_copy(s).wait_send()
            sog_copy(s).wait_send()

        return carry

    lax.fori_loop(0, 8, finish, 0)
    act_out[...] = act_rx[...]
    sog_out[...] = sog_rx[...]

    def finish_sums(v, carry):
        for d in (0, 1):
            sum_copy(d, v).wait_send()
        return carry

    lax.fori_loop(sent - HELD, sent, finish_sums, 0)
    for m in range(sent - 8, sent):
        for d in (0, 1):
            ring_unit_copy(d, jnp.int32(m)).wait_send()
    for o in range(1, FEATS):
        for g in (groups - 2, groups - 1):
            ex_copy(g % 2, g, o).wait_send()

        def finish_gp(g, carry, o=o):
            gp_copy(g, o).wait_send()
            return carry

        lax.fori_loop(0, groups, finish_gp, 0)
    for q in range(12):
        wg_copy(jnp.int32(q)).wait()


def fc_layer(steps, number, n, so, bias, x, first, cot, relay, weight):
    units, feats_dim = weight.shape[1:]
    quarter = units // FEATS
    groups = -(-steps // SPAN)
    slots = groups * SPAN
    vm = pltpu.VMEM
    dma = pltpu.SemaphoreType.DMA
    sm = pltpu.SMEM
    unit = (CHUNK, feats_dim // 2)
    vmem_spec = pl.BlockSpec(memory_space=pltpu.VMEM)
    any_spec = pl.BlockSpec(memory_space=pl.ANY)
    rows = 2 * slots * CHUNK
    return pl.pallas_call(
        functools.partial(fc_kernel, steps),
        out_shape=(
            jax.ShapeDtypeStruct((8, 8, TOWERS, CHUNK, quarter), bf16),
            jax.ShapeDtypeStruct((8, TOWERS, CHUNK, feats_dim), bf16),
            jax.ShapeDtypeStruct(weight.shape, f32),
            jax.ShapeDtypeStruct((TOWERS, units), f32),
            jax.ShapeDtypeStruct((8, 8, quarter), f32),
        ),
        in_specs=[pl.BlockSpec(memory_space=pltpu.SMEM)] + [vmem_spec] * 6 + [any_spec],
        out_specs=(vmem_spec, vmem_spec, any_spec, vmem_spec, vmem_spec),
        scratch_shapes=[
            vm(weight.shape, bf16),
            vm((groups + 8 // (2 * SPAN), TOWERS, 2, 2, SPAN) + unit, bf16),
            vm((2, PIECES * (steps - 1)) + unit, bf16),
            vm((2, 8) + unit, bf16),
            vm((2, FEATS, TOWERS, 2 * SPAN, CHUNK, quarter), f32),
            vm((groups, FEATS, TOWERS, 2 * SPAN, CHUNK, quarter), f32),
            vm((groups, FEATS, TOWERS, 2 * SPAN, CHUNK, quarter), bf16),
            vm((TOWERS, 2, 2 * SPAN) + unit, f32),
            vm((2, HELD) + unit, bf16),
            vm((2, PIECES * slots) + unit, bf16),
            vm((8, 8, TOWERS, CHUNK, quarter), bf16),
            vm((slots, 2, TOWERS, CHUNK, quarter), bf16),
            vm((8, 8, TOWERS, CHUNK, quarter), bf16),
            vm((8, 8, TOWERS, CHUNK, quarter), bf16),
            vm((4, CHUNK, quarter), f32),
            vm((8, quarter), f32),
            vm((8, 8, quarter), f32),
            vm(weight.shape, f32),
            sm((2 * PLACES,), i32),
            sm((PLACES,), i32),
            sm((2 * PLACES,), i32),
            sm((2,), i32),
            sm((2 * slots,), i32),
            sm((2 * slots,), i32),
            dma,
            dma((2, 8)),
            dma((2, PIECES * (steps - 1))),
            dma((2, HELD)),
            dma((2, PIECES * (steps - 1))),
            dma((2, 3)),
            dma((groups, FEATS)),
            dma((groups, 3)),
            dma((groups, FEATS)),
            dma((8,)),
            dma((8,)),
            dma((8,)),
            dma((8,)),
            dma((8,)),
            dma((8,)),
            dma((12,)),
            pltpu.SemaphoreType.REGULAR((2,)),
        ],
        cost_estimate=pl.CostEstimate(
            flops=6 * rows * TOWERS * units * feats_dim, bytes_accessed=30 << 20,
            transcendentals=rows * TOWERS * quarter),
        compiler_params=pltpu.CompilerParams(
            collective_id=number, has_side_effects=True, vmem_limit_bytes=60 << 20),
    )(n, so, bias, x, first, cot, relay, weight)


def layout_matrix(chans):
    table = np.zeros((4 * 2 * chans, 4 * 2 * chans), np.float32)
    for q0 in range(4):
        for c in range(chans):
            for t in range(TOWERS):
                lane = 4 * ((9 * c) % 32) + q0
                table[q0 * 2 * chans + 2 * c + t, (2 * t + c // 32) * 128 + lane] = 1
    return table


def lane_sources():
    slot = np.arange(128) // 4
    rows = [(slot + 32 * j) % 9 for j in range(9)] + [(2 * (q1 - slot)) % 9 for q1 in range(9)]
    return np.broadcast_to(np.stack(rows)[:, None, :], (18, CHUNK, 128)).astype(np.int32)


def lane_pairs(chans):
    shape = (chans, TOWERS * chans)
    lane, chan = lax.broadcasted_iota(i32, shape, 1), lax.broadcasted_iota(i32, shape, 0)
    return tuple((lane == 2 * chan + t).astype(f32) for t in range(TOWERS))


def exact_dot(a, b, dims):
    return lax.dot_general(
        a, b, (dims, ((), ())), precision=lax.Precision.HIGHEST, preferred_element_type=f32)


def pair_swap():
    even = (lax.broadcasted_iota(i32, (CHUNK, 128), 1) & 1) == 0

    def swap(value):
        return jnp.where(even, pltpu.roll(value, 127, 1), pltpu.roll(value, 1, 1))

    return swap


BATCH = 2


def entry_kernel(
    cc_ref, so_ref, si_ref, perm_ref, source_ref, cot_ref, conv_ref,
    feats_out, pooled_out, n_out, so_out, relay_out, first_out, s_out,
    n_tx, n_rx, so_tx, so_rx, relay_rx, first_tx, first_rx, s_ref,
    n_ss, n_rs, so_ss, so_rs, relay_ss, relay_rs, first_ss, first_rs,
):
    blk, feat = lax.axis_index("blk"), lax.axis_index("feat")
    step = pl.program_id(0)
    holds = lax.div(blk, 2) == feat

    def n_copy(o):
        to = lax.rem(blk + o, PLACES)
        return pltpu.make_async_remote_copy(
            src_ref=n_tx, dst_ref=n_rx.at[blk], send_sem=n_ss.at[o - 1], recv_sem=n_rs.at[blk],
            device_id=(to, feat), device_id_type=MESH)

    def n_wait(o):
        src = lax.rem(blk + o, PLACES)
        return pltpu.make_async_remote_copy(
            src_ref=n_tx, dst_ref=n_rx.at[src], send_sem=n_ss.at[o - 1], recv_sem=n_rs.at[src],
            device_id=(src, feat), device_id_type=MESH)

    def so_copy(o):
        to = lax.rem(feat + o, FEATS)
        return pltpu.make_async_remote_copy(
            src_ref=so_tx.at[to], dst_ref=so_rx, send_sem=so_ss.at[o - 1], recv_sem=so_rs,
            device_id=(blk, to), device_id_type=MESH)

    across_y = lax.rem(feat + 2, FEATS)
    place = ring_place(blk)
    half = feats_out.shape[-1] // 2

    def first_copy(d, m):
        return pltpu.make_async_remote_copy(
            src_ref=first_tx.at[d, m], dst_ref=first_rx.at[d, m], send_sem=first_ss.at[d, m],
            recv_sem=first_rs.at[d, m],
            device_id=(ring_blk(lax.rem(place + (7 if d else 1), 8)), feat), device_id_type=MESH)

    def relay_copy(s):
        return pltpu.make_async_remote_copy(
            src_ref=cot_ref.at[s // 2 * FEATS + 2 * lax.div(across_y, 2) + s % 2],
            dst_ref=relay_rx.at[s], send_sem=relay_ss.at[s], recv_sem=relay_rs.at[s],
            device_id=(blk, across_y), device_id_type=MESH)

    @pl.when(step == 0)
    def _():
        bar = pltpu.get_barrier_semaphore()
        for o in range(1, PLACES):
            pl.semaphore_signal(
                bar, inc=1, device_id=(lax.rem(blk + o, PLACES), feat), device_id_type=MESH)
        for o in range(1, FEATS):
            pl.semaphore_signal(
                bar, inc=1, device_id=(blk, lax.rem(feat + o, FEATS)), device_id_type=MESH)
        total = cc_ref[0]
        for e in range(1, cc_ref.shape[0]):
            total = total + cc_ref[e]
        n_tx[...] = jnp.full(n_tx.shape, total, i32)
        n_rx[blk] = n_tx[...]
        for q in range(FEATS):
            at = pl.ds(pl.multiple_of(lax.rem(blk, 2) * 512 + q * 128, 128), 128)
            for t in range(TOWERS):
                so_tx[q, 2 * t:2 * t + 2] = so_ref[t, :, at]
                so_tx[q, 4 + 2 * t:6 + 2 * t] = so_ref[t, :, at]
        even, odd = lane_pairs(si_ref.shape[-1])
        rows = [[exact_dot(si_ref[t], v, ((1,), (0,))) for v in (even, odd)] for t in range(TOWERS)]
        s_ref[0:1] = rows[0][0][0:1] + rows[1][1][1:2]
        s_ref[1:2] = rows[0][0][1:2] + rows[1][1][0:1]
        s_ref[2:3] = rows[1][0][0:1] + rows[0][1][1:2]
        s_ref[3:8] = jnp.zeros((5, s_ref.shape[1]), f32)
        pl.semaphore_wait(bar, PLACES - 1 + FEATS - 1)
        for o in range(1, PLACES):
            n_copy(o).start()
        for s in range(4):
            relay_copy(s).start()

        @pl.when(holds)
        def _():
            so_rx[...] = so_tx[feat]
            for o in range(1, FEATS):
                so_copy(o).start()

    def chunk(e, carry):
        swap = pair_swap()
        at_row = pl.ds(pl.multiple_of(e * CHUNK, CHUNK), CHUNK)
        across = {}
        for row in range(MAP):
            line = [conv_ref[MAP * row + col, at_row].astype(f32) for col in range(MAP)]
            for v in range(GRID):
                across[row, v] = line[2 * v] + line[2 * v + 1] + line[2 * v + 2]
        own, other = s_ref[0:1], s_ref[1:2]
        parts = []
        for q1 in range(9):
            here = []
            for q0 in range(4):
                q = 4 * q1 + q0
                u, v = q // GRID, q % GRID
                pooled = (across[2 * u, v] + across[2 * u + 1, v] + across[2 * u + 2, v]) * f32(1 / 9)
                pooled_out[e, q] = pooled
                here.append((own * pooled + other * swap(pooled)).astype(bf16))
            parts.append(jnp.concatenate(here, axis=1))
        spread = jnp.dot(
            jnp.concatenate(parts, axis=0), perm_ref[...], preferred_element_type=f32)
        turned = [
            pltpu.roll(spread[q1 * CHUNK:(q1 + 1) * CHUNK, at:at + 128], 4 * q1, 1)
            if q1 else spread[0:CHUNK, at:at + 128] for q1 in range(9) for at in range(0, 512, 128)]
        for j in range(9):
            source = source_ref[j]
            tiles = turned[0:4]
            for q1 in range(1, 9):
                here = source == q1
                tiles = [jnp.where(here, turned[4 * q1 + k], tiles[k]) for k in range(4)]
            for k in range(4):
                n = 9 * (k % 2) + j
                feats_out[e, k // 2, :, n * 128:(n + 1) * 128] = tiles[k].astype(bf16)
        return carry

    lax.fori_loop(0, BATCH, chunk, 0)

    @pl.when(step == 0)
    def _():
        for m in range(PIECES):
            for d in range(2):
                first_tx[d, m] = feats_out[d, m // 2, :, m % 2 * half:(m % 2 + 1) * half]
                first_copy(d, m).start()

    @pl.when(step == pl.num_programs(0) - 1)
    def _():
        for m in range(PIECES):
            for d in range(2):
                first_copy(d, m).wait()
        first_out[...] = first_rx[...]
        s_out[...] = s_ref[...]
        for o in range(1, PLACES):
            n_wait(o).wait_recv()
            n_copy(o).wait_send()

        @pl.when(holds)
        def _():
            for o in range(1, FEATS):
                so_copy(o).wait_send()

        @pl.when(jnp.logical_not(holds))
        def _():
            so_copy(1).wait_recv()

        for s in range(4):
            relay_copy(s).wait()
        n_out[...] = n_rx[...]
        so_out[...] = so_rx[...]
        relay_out[...] = relay_rx[...]


def exit_kernel(
    s_ref, perm_ref, source_ref, gf_ref, pooled_ref, wg_ref, conv_out, si_out, wg_out, acc,
):
    step = pl.program_id(0)

    @pl.when(step == 0)
    def _():
        acc[...] = jnp.zeros_like(acc)

    wg_out[...] = wg_ref[...]
    def chunk(e, carry):
        swap = pair_swap()
        at_row = pl.ds(pl.multiple_of(e * CHUNK, CHUNK), CHUNK)
        tiles = [
            gf_ref[e, k // 2, :, (9 * (k % 2) + j) * 128:(9 * (k % 2) + j + 1) * 128].astype(f32)
            for j in range(9) for k in range(4)]
        rows = []
        for q1 in range(9):
            source = source_ref[9 + q1]
            here = tiles[0:4]
            for j in range(1, 9):
                mask = source == j
                here = [jnp.where(mask, tiles[4 * j + k], here[k]) for k in range(4)]
            rows.append(jnp.concatenate(
                [pltpu.roll(v, 128 - 4 * q1, 1) if q1 else v for v in here], axis=1).astype(bf16))
        grads = lax.dot_general(
            jnp.concatenate(rows, axis=0), perm_ref[...], (((1,), (1,)), ((), ())),
            preferred_element_type=f32)
        own, other = s_ref[0:1] * f32(1 / 9), s_ref[2:3] * f32(1 / 9)
        same = acc[0]
        cross = acc[1]
        back = {}
        for q in range(GRID * GRID):
            q1, q0 = q // 4, q % 4
            grad = grads[q1 * CHUNK:(q1 + 1) * CHUNK, q0 * 128:(q0 + 1) * 128]
            pooled = pooled_ref[e, q]
            swapped = swap(grad)
            same = same + grad * pooled
            cross = cross + swapped * pooled
            back[q // GRID, q % GRID] = own * grad + other * swapped
        acc[0] = same
        acc[1] = cross
        lines = []
        for u in range(GRID):
            line = []
            for col in range(MAP):
                v = col // 2
                if col % 2:
                    line.append(back[u, v])
                elif col == 0:
                    line.append(back[u, 0])
                elif col == MAP - 1:
                    line.append(back[u, GRID - 1])
                else:
                    line.append(back[u, v - 1] + back[u, v])
            lines.append(line)
        for row in range(MAP):
            u = row // 2
            for col in range(MAP):
                if row % 2 or row == 0:
                    value = lines[u][col]
                elif row == MAP - 1:
                    value = lines[GRID - 1][col]
                else:
                    value = lines[u - 1][col] + lines[u][col]
                conv_out[MAP * row + col, at_row] = value.astype(bf16)
        return carry

    lax.fori_loop(0, BATCH, chunk, 0)

    @pl.when(step == pl.num_programs(0) - 1)
    def _():
        sums = [jnp.sum(acc[e], axis=0, keepdims=True) for e in range(2)]
        si_out[...] = jnp.concatenate(sums * 4, axis=0)


def total_kernel(x_ref, out, rx, ss, rs):
    blk, feat = lax.axis_index("blk"), lax.axis_index("feat")

    def copy(o):
        return pltpu.make_async_remote_copy(
            src_ref=x_ref, dst_ref=rx.at[blk], send_sem=ss.at[o - 1], recv_sem=rs.at[blk],
            device_id=(lax.rem(blk + o, PLACES), feat), device_id_type=MESH)

    def wait(o):
        src = lax.rem(blk + o, PLACES)
        return pltpu.make_async_remote_copy(
            src_ref=x_ref, dst_ref=rx.at[src], send_sem=ss.at[o - 1], recv_sem=rs.at[src],
            device_id=(src, feat), device_id_type=MESH)

    bar = pltpu.get_barrier_semaphore()
    for o in range(1, PLACES):
        pl.semaphore_signal(
            bar, inc=1, device_id=(lax.rem(blk + o, PLACES), feat), device_id_type=MESH)
    pl.semaphore_wait(bar, PLACES - 1)
    for o in range(1, PLACES):
        copy(o).start()
    rx[blk] = x_ref[...]
    for o in range(1, PLACES):
        wait(o).wait_recv()
    total = rx[0]
    for q in range(1, PLACES):
        total = total + rx[q]
    even, odd = (
        exact_dot(total, v, ((1,), (1,))) for v in lane_pairs(out.shape[-1]))
    out[0] = jnp.concatenate([even[0:1], odd[1:2]], axis=0)
    out[1] = jnp.concatenate([even[1:2], odd[0:1]], axis=0)
    for o in range(1, PLACES):
        copy(o).wait_send()


def entry(counts, so, stitch, cot, conv):
    spots, rows, merged = conv.shape
    chunks = rows // CHUNK
    chans = merged // TOWERS
    wide = chans * GRID * GRID
    vm, dma = pltpu.VMEM, pltpu.SemaphoreType.DMA
    whole = pl.BlockSpec(memory_space=pltpu.VMEM)
    return pl.pallas_call(
        entry_kernel,
        grid=(chunks // BATCH,),
        out_shape=(
            jax.ShapeDtypeStruct((chunks, TOWERS, CHUNK, wide), bf16),
            jax.ShapeDtypeStruct((chunks, GRID * GRID, CHUNK, merged), f32),
            jax.ShapeDtypeStruct((PLACES, 8, 128), i32),
            jax.ShapeDtypeStruct((8, 128), f32),
            jax.ShapeDtypeStruct((4,) + cot.shape[1:], bf16),
            jax.ShapeDtypeStruct((2, PIECES, CHUNK, wide // 2), bf16),
            jax.ShapeDtypeStruct((8, merged), f32),
        ),
        in_specs=[pl.BlockSpec(memory_space=pltpu.SMEM)] + [whole] * 5 + [
            pl.BlockSpec((spots, BATCH * CHUNK, merged), lambda c: (0, c, 0))],
        out_specs=(
            pl.BlockSpec((BATCH, TOWERS, CHUNK, wide), lambda c: (c, 0, 0, 0)),
            pl.BlockSpec((BATCH, GRID * GRID, CHUNK, merged), lambda c: (c, 0, 0, 0)),
            whole, whole, whole, whole, whole,
        ),
        scratch_shapes=[
            vm((8, 128), i32), vm((PLACES, 8, 128), i32), vm((FEATS, 8, 128), f32), vm((8, 128), f32),
            vm((4,) + cot.shape[1:], bf16), vm((2, PIECES, CHUNK, wide // 2), bf16),
            vm((2, PIECES, CHUNK, wide // 2), bf16), vm((8, merged), f32),
            dma((PLACES - 1,)), dma((PLACES,)), dma((FEATS - 1,)), dma, dma((4,)), dma((4,)),
            dma((2, PIECES)), dma((2, PIECES)),
        ],
        cost_estimate=pl.CostEstimate(flops=1 << 30, bytes_accessed=10 << 20, transcendentals=0),
        compiler_params=pltpu.CompilerParams(
            collective_id=20, has_side_effects=True, vmem_limit_bytes=60 << 20),
    )(counts, so, stitch, jnp.asarray(layout_matrix(chans), bf16), jnp.asarray(lane_sources()), cot, conv)


def leave(s_rows, gf, pooled, weight_grad, spots):
    chunks, towers, _, wide = gf.shape
    merged = pooled.shape[-1]
    vm = pltpu.VMEM
    whole = pl.BlockSpec(memory_space=pltpu.VMEM)
    share = pl.BlockSpec(
        (towers, weight_grad.shape[1] * BATCH // chunks, wide), lambda c: (0, c, 0))
    return pl.pallas_call(
        exit_kernel,
        grid=(chunks // BATCH,),
        out_shape=(
            jax.ShapeDtypeStruct((spots, chunks * CHUNK, merged), bf16),
            jax.ShapeDtypeStruct((8, 128), f32),
            jax.ShapeDtypeStruct(weight_grad.shape, f32),
        ),
        in_specs=[whole] * 3 + [
            pl.BlockSpec((BATCH, towers, CHUNK, wide), lambda c: (c, 0, 0, 0)),
            pl.BlockSpec((BATCH, GRID * GRID, CHUNK, merged), lambda c: (c, 0, 0, 0)),
            share],
        out_specs=(
            pl.BlockSpec((spots, BATCH * CHUNK, merged), lambda c: (0, c, 0)),
            whole, share,
        ),
        scratch_shapes=[vm((2, CHUNK, 128), f32)],
        cost_estimate=pl.CostEstimate(flops=1 << 30, bytes_accessed=30 << 20, transcendentals=0),
        compiler_params=pltpu.CompilerParams(vmem_limit_bytes=60 << 20),
    )(s_rows, jnp.asarray(layout_matrix(merged // TOWERS), bf16),
      jnp.asarray(lane_sources()), gf, pooled, weight_grad)


def total_over_blk(value):
    whole = pl.BlockSpec(memory_space=pltpu.VMEM)
    dma = pltpu.SemaphoreType.DMA
    return pl.pallas_call(
        total_kernel,
        out_shape=jax.ShapeDtypeStruct((TOWERS, TOWERS, value.shape[1] // TOWERS), f32),
        in_specs=[whole],
        out_specs=whole,
        scratch_shapes=[
            pltpu.VMEM((PLACES,) + value.shape, f32), dma((PLACES - 1,)), dma((PLACES,))],
        compiler_params=pltpu.CompilerParams(
            collective_id=21, has_side_effects=True, vmem_limit_bytes=16 << 20),
    )(value)


CLASSES = (19, 20, 21, 22, 24)


def body_ring(conv_maps, crop_counts, fc_weight, fc_bias, stitch_in, stitch_out, cotangent):
    num_rows = conv_maps.shape[0]
    units = fc_weight.shape[1]
    quarter = units // FEATS
    chunks = num_rows // CHUNK
    cot = cotangent.reshape(chunks, CHUNK, TOWERS, 8, quarter).transpose(3, 0, 2, 1, 4)
    feats, pooled, counts, so, relay, first, s_rows = entry(
        crop_counts, stitch_out, stitch_in, cot, conv_maps.transpose(1, 0, 2))
    n = counts[:, 0, 0]
    need = lax.div(jnp.sum(lax.div(n + (CHUNK - 1), CHUNK)) + 1, 2)
    full = PLACES * chunks // 2
    kinds = CLASSES + (full,)
    pick = sum(((need > c).astype(i32) for c in CLASSES), jnp.int32(0))
    act, gf, weight_grad, bias_grad, sog = lax.switch(
        pick,
        [functools.partial(fc_layer, steps, at) for at, steps in enumerate(kinds)],
        n, so, fc_bias, feats, first, cot, relay, fc_weight)
    activations = act.transpose(1, 3, 2, 0, 4).reshape(num_rows, TOWERS, -1)
    stitch_out_grad = sog[:, :4].transpose(1, 0, 2).reshape(TOWERS, TOWERS, -1)
    conv_grad, si, weight_grad = leave(s_rows, gf, pooled, weight_grad, conv_maps.shape[1])
    conv_grad = conv_grad.transpose(1, 0, 2)
    stitch_in_grad = total_over_blk(si)
    return (activations, conv_grad, weight_grad, bias_grad, stitch_in_grad, stitch_out_grad)


def solution(mesh):
    ring = mesh.shape["blk"] == PLACES and mesh.shape["feat"] == FEATS
    return jax.shard_map(
        body_ring if ring else body_plain,
        mesh=mesh,
        in_specs=(
            P("blk", None, "feat"),
            P("blk"),
            P(None, "blk", "feat"),
            P(),
            P(None, None, "feat"),
            P(None, None, "feat"),
            P("blk", None, "feat"),
        ),
        out_specs=(
            P("blk", None, "feat"),
            P("blk", None, "feat"),
            P(None, "blk", "feat"),
            P(None, "blk"),
            P(None, None, "feat"),
            P(None, None, "feat"),
        ),
        check_vma=False,
    )
```

```python
import functools

import jax
import jax.numpy as jnp
import numpy as np
from jax import lax
from jax.experimental import pallas as pl
from jax.experimental.pallas import tpu as pltpu
from jax.sharding import PartitionSpec as P

MAP = 13
GRID = 6
TOWERS = 2
CHUNK = 16
CLASSES = (19, 20, 21, 22, 24)
SPAN = 2
PIECES = 4
HELD = 16
PLACES = 8
FEATS = 4
RING_BLK = (0, 2, 4, 6, 7, 5, 3, 1)
MESH = pl.DeviceIdType.MESH
f32 = jnp.float32
bf16 = jnp.bfloat16
i32 = jnp.int32


def pool_table(dtype):
    position = jnp.arange(MAP * MAP)
    row_pos = position // MAP
    col_pos = position % MAP
    cell = jnp.arange(GRID * GRID)
    row_cell = cell // GRID
    col_cell = cell % GRID
    down = row_pos[:, None] - 2 * row_cell[None, :]
    across = col_pos[:, None] - 2 * col_cell[None, :]
    inside = (down >= 0) & (down < 3) & (across >= 0) & (across < 3)
    return inside.astype(dtype)


def stitch_first(pooled, stitch_in):
    return jnp.einsum("tuc,rucq->rtcq", stitch_in, pooled, precision=lax.Precision.HIGHEST)


def stitch_head(pre, stitch_out):
    act = jax.nn.gelu(pre)
    return jnp.einsum("tuk,ruk->rtk", stitch_out, act, precision=lax.Precision.HIGHEST)


def body_plain(conv_maps, crop_counts, fc_weight, fc_bias, stitch_in, stitch_out, cotangent):
    num_rows = conv_maps.shape[0]
    merged = conv_maps.shape[2]
    chans = merged // TOWERS
    cols = fc_weight.shape[1]
    feat_idx = lax.axis_index("feat")
    blk_idx = lax.axis_index("blk")
    sums = jnp.einsum("rpm,pq->rqm", conv_maps, pool_table(bf16), preferred_element_type=f32)
    pooled = jnp.transpose(sums.reshape(num_rows, GRID * GRID, chans, TOWERS), (0, 3, 2, 1)) * (
        1.0 / 9.0
    )
    mixed, pull_first = jax.vjp(stitch_first, pooled, stitch_in)
    feats = mixed.astype(bf16).reshape(num_rows, TOWERS, -1)
    own_cols = jnp.einsum(
        "rtf,tnf->rtn",
        lax.all_gather(feats, "blk", axis=0, tiled=True),
        fc_weight,
        preferred_element_type=f32,
    )
    partial_value = lax.all_to_all(own_cols, "blk", split_axis=0, concat_axis=2, tiled=True)
    pre = lax.psum_scatter(partial_value, "feat", scatter_dimension=2, tiled=True)
    quarter = pre.shape[2]
    bias_part = lax.dynamic_slice_in_dim(fc_bias, feat_idx * quarter, quarter, 1)
    pre = pre + bias_part[None]
    live = (jnp.arange(num_rows) < jnp.sum(crop_counts)).astype(f32)
    stitched, pull_head = jax.vjp(stitch_head, pre, stitch_out)
    activations = (live[:, None, None] * stitched).astype(bf16)
    grad_out = live[:, None, None] * cotangent.astype(f32)
    grad_pre, grad_so = pull_head(grad_out)
    grad_low = grad_pre.astype(bf16)
    grad_all = lax.all_gather(grad_low, "feat", axis=2, tiled=True)
    bias_terms = jnp.sum(grad_all, axis=0, dtype=f32)
    grad_cols = lax.all_to_all(grad_all, "blk", split_axis=2, concat_axis=0, tiled=True)
    weight_grad = jnp.einsum(
        "rtf,rtn->tnf",
        lax.all_gather(feats, "blk", axis=0, tiled=True),
        grad_cols,
        preferred_element_type=f32,
    )
    grad_feats = jnp.einsum(
        "rtn,tnf->rtf",
        grad_all,
        lax.all_gather(fc_weight, "blk", axis=1, tiled=True),
        preferred_element_type=f32,
    )
    grad_mixed = grad_feats.reshape(num_rows, TOWERS, chans, -1)
    grad_pooled, grad_si = pull_first(grad_mixed)
    spread = jnp.einsum(
        "rtcq,pq->rpct", grad_pooled * (1.0 / 9.0), pool_table(f32), precision=lax.Precision.HIGHEST
    )
    conv_grad = spread.reshape(num_rows, MAP * MAP, merged).astype(bf16)
    stitch_in_grad, stitch_out_grad, bias_total = lax.psum((grad_si, grad_so, bias_terms), "blk")
    bias_grad = lax.dynamic_slice_in_dim(bias_total, blk_idx * cols, cols, 1)
    return (activations, conv_grad, weight_grad, bias_grad, stitch_in_grad, stitch_out_grad)


def ring_place(blk):
    z, x = lax.div(blk, 2), lax.rem(blk, 2)
    return z + x * (7 - 2 * z)


def ring_blk(place):
    x = lax.div(place, 4)
    return 2 * (place + x * (7 - 2 * place)) + x


def fc_kernel(
    steps,
    n_ref, so_ref, bias_ref, x_ref, first_ref, cot_ref, relay_ref, w_hbm,
    act_out, gf_out, wg_hbm, bg_out, sog_out,
    w, x, land, ring_tx, ex_tx, ex_rx, gp, part, held, sums,
    cot_rx, acts, act_tx, act_rx, sog_acc, sog_tx, sog_rx, wg_acc,
    kd, nn, start, tot, slot_rc, slot_live,
    w_sem, ag_ss, ag_rs, rs_ss, rs_rs, ex_ss, ex_rs, gp_ss, gp_rs,
    cot_ss, cot_rs, act_ss, act_rs, sog_ss, sog_rs, wg_sem, free,
):
    blk, feat = lax.axis_index("blk"), lax.axis_index("feat")
    place = ring_place(blk)
    ring_to = (ring_blk(lax.rem(place + 1, 8)), ring_blk(lax.rem(place + 7, 8)))
    ring_from = (lax.rem(place + 7, 8), lax.rem(place + 1, 8))
    per = 2 * SPAN
    groups = x.shape[0] - 8 // per
    slots = groups * SPAN
    sent = PIECES * (steps - 1)
    part_dim = x.shape[-1]
    units = w.shape[1]
    quarter = units // FEATS
    row_feat = lax.div(blk, 2)
    half_at = lax.rem(blk, 2) * FEATS + feat
    mine = row_feat == feat
    side = 2 * lax.div(feat, 2)
    cot_feat = side + lax.rem(row_feat, 2)
    cot_mine = cot_feat == feat

    w_copy = pltpu.make_async_copy(w_hbm, w, w_sem)
    w_copy.start()

    bar = pltpu.get_barrier_semaphore()

    def hello(dev):
        pl.semaphore_signal(bar, inc=1, device_id=dev, device_id_type=MESH)

    for d in (0, 1):
        hello((ring_to[d], feat))
    for o in range(1, FEATS):
        hello((blk, lax.rem(feat + o, FEATS)))

    def cot_to(s):
        owner = lax.rem(feat + 2 * lax.div(s, 4), FEATS)
        return 2 * owner + lax.rem(lax.div(s, 2), 2), side + lax.rem(s, 2)

    def cot_not_me(s):
        to = cot_to(s)
        return jnp.logical_or(to[0] != blk, to[1] != feat)

    def hello_far(s, carry):
        to = (2 * feat + lax.div(s, FEATS), lax.rem(s, FEATS))

        @pl.when(jnp.logical_or(to[0] != blk, to[1] != feat))
        def _():
            hello(to)

        @pl.when(jnp.logical_or(s != blk, row_feat != feat))
        def _():
            hello((s, row_feat))

        @pl.when(cot_not_me(s))
        def _():
            hello(cot_to(s))

        @pl.when(jnp.logical_or(s != blk, cot_feat != feat))
        def _():
            hello((s, cot_feat))

        return carry

    lax.fori_loop(0, 8, hello_far, 0)

    for d in (0, 1):
        for m in range(PIECES):
            land[d, m] = first_ref[d, m]

    def own_cot(s):
        return lax.div(s, 2) * FEATS + side + lax.rem(s, 2)

    def cot_copy(s, src):
        return pltpu.make_async_remote_copy(
            src_ref=src, dst_ref=cot_rx.at[blk], send_sem=cot_ss.at[s],
            recv_sem=cot_rs.at[blk], device_id=cot_to(s), device_id_type=MESH)

    def cot_wait(r):
        return pltpu.make_async_remote_copy(
            src_ref=cot_ref.at[0], dst_ref=cot_rx.at[r], send_sem=cot_ss.at[0],
            recv_sem=cot_rs.at[r], device_id=(r, cot_feat), device_id_type=MESH)

    def far_not_me(s):
        return jnp.logical_or(2 * feat + lax.div(s, FEATS) != blk, lax.rem(s, FEATS) != feat)

    def near_not_me(r):
        return jnp.logical_or(r != blk, row_feat != feat)

    for c in range(8):
        for t in range(TOWERS):
            for h in range(2):
                x[groups + c // per, t, h, c % per // SPAN, c % SPAN] = x_ref[
                    c, t, :, h * part_dim:(h + 1) * part_dim]

    run = jnp.int32(0)
    for q in range(PLACES):
        n = n_ref[RING_BLK[q]]
        k = jnp.clip(lax.div(n + (CHUNK - 1), CHUNK), 2, 8)
        first = lax.div(run + k + 1, 2) - lax.div(run + 1, 2)
        kd[q] = first
        kd[PLACES + q] = k - first
        nn[q] = n
        run = run + k

    def ring_unit_copy(d, m):
        return pltpu.make_async_remote_copy(
            src_ref=ring_tx.at[d, lax.rem(m, 8)], dst_ref=land.at[d, m],
            send_sem=ag_ss.at[d, lax.rem(m, 8)], recv_sem=ag_rs.at[d, m],
            device_id=(ring_to[d], feat), device_id_type=MESH)

    own_k = (kd[place], kd[PLACES + place])
    prev_k = tuple(kd[d * PLACES + ring_from[d]] for d in (0, 1))

    def chunk_of(d, c, first):
        return jnp.where(c == 0, d, (c + 1 if d == 0 else first + c))

    def own_piece(d, pos, t, h):
        c = chunk_of(d, pos, own_k[0])
        return x[groups + lax.div(c, per), t, h, lax.div(lax.rem(c, per), SPAN), lax.rem(c, SPAN)]

    def cot_send(s, carry):
        @pl.when(cot_not_me(s))
        def _():
            cot_copy(s, cot_ref.at[own_cot(s)]).start()

        @pl.when(jnp.logical_not(cot_not_me(s)))
        def _():
            cot_rx[blk] = cot_ref[own_cot(s)]

        @pl.when(cot_not_me(s + 4))
        def _():
            cot_copy(s + 4, relay_ref.at[s]).start()

        @pl.when(jnp.logical_not(cot_not_me(s + 4)))
        def _():
            cot_rx[blk] = relay_ref[s]

        return carry


    for d in (0, 1):
        run = jnp.int32(0)
        for h in range(1, PLACES + 1):
            at = lax.rem(place + (PLACES - h if d == 0 else h), PLACES)
            start[d * PLACES + at] = run
            run = run + kd[d * PLACES + at]
        tot[d] = run

        def fill(i, carry, d=d):
            h, c = carry
            hc = jnp.minimum(h, PLACES)
            at = lax.rem(place + (2 * PLACES - hc if d == 0 else hc), PLACES)
            chunk = jnp.minimum(chunk_of(d, c, kd[at]), 7)
            live = jnp.clip(nn[at] - CHUNK * chunk, 0, CHUNK)
            slot_rc[d * slots + i] = ring_blk(at) * 8 + chunk
            slot_live[d * slots + i] = jnp.where(h <= PLACES, live, 0)
            over = c + 1 >= kd[d * PLACES + at]
            return jnp.where(over, h + 1, h), jnp.where(over, 0, c + 1)

        lax.fori_loop(0, slots, fill, (jnp.int32(1), jnp.int32(0)))

    own_at = (tot[0] - own_k[0], tot[1] - own_k[1])
    held[...] = jnp.zeros_like(held)
    sog_acc[...] = jnp.zeros_like(sog_acc)
    pl.semaphore_wait(
        bar, jnp.where(mine, 2 + 3 + 14, 2 + 3 + 16) + jnp.where(cot_mine, 14, 16))
    lax.fori_loop(0, 4, cot_send, 0)

    def ex_copy(slot, g, o):
        to = lax.rem(feat + o, FEATS)
        return pltpu.make_async_remote_copy(
            src_ref=ex_tx.at[slot, to], dst_ref=ex_rx.at[g, feat], send_sem=ex_ss.at[slot, o - 1],
            recv_sem=ex_rs.at[g, feat], device_id=(blk, to), device_id_type=MESH)

    def ex_wait(g, o):
        src = lax.rem(feat + o, FEATS)
        return pltpu.make_async_remote_copy(
            src_ref=ex_tx.at[0, src], dst_ref=ex_rx.at[g, src], send_sem=ex_ss.at[0, o - 1],
            recv_sem=ex_rs.at[g, src], device_id=(blk, src), device_id_type=MESH)

    def gp_copy(g, o):
        to = lax.rem(feat + o, FEATS)
        return pltpu.make_async_remote_copy(
            src_ref=gp.at[g, feat], dst_ref=gp.at[g, feat], send_sem=gp_ss.at[g, o - 1],
            recv_sem=gp_rs.at[g, feat], device_id=(blk, to), device_id_type=MESH)

    def gp_wait(g, o):
        src = lax.rem(feat + o, FEATS)
        return pltpu.make_async_remote_copy(
            src_ref=gp.at[g, src], dst_ref=gp.at[g, src], send_sem=gp_ss.at[g, o - 1],
            recv_sem=gp_rs.at[g, src], device_id=(blk, src), device_id_type=MESH)

    def forward(g, t):
        slot = lax.rem(g, 2)

        @pl.when(jnp.logical_and(g >= 2, t == 0))
        def _():
            for o in range(1, FEATS):
                ex_copy(slot, g, o).wait_send()

        for n in range(2):
            out = sum(
                lax.dot_general(
                    x[g, t, h].reshape(per * CHUNK, part_dim),
                    w[t, 2 * n * quarter:2 * (n + 1) * quarter, h * part_dim:(h + 1) * part_dim],
                    (((1,), (1,)), ((), ())), preferred_element_type=f32)
                for h in range(2))
            for e in range(2):
                ex_tx[slot, 2 * n + e, t] = out[:, e * quarter:(e + 1) * quarter].reshape(
                    per, CHUNK, quarter)

        @pl.when(t == 1)
        def _():
            for o in range(1, FEATS):
                ex_copy(slot, g, o).start()
            ex_rx[g, feat] = ex_tx[slot, feat]

    bias_here = bias_ref[:, pl.ds(pl.multiple_of(blk * units + feat * quarter, quarter), quarter)]

    def head(g):
        for o in range(1, FEATS):
            ex_wait(g, o).wait_recv()

        def one(s, carry):
            d, ci = lax.div(s, SPAN), lax.rem(s, SPAN)
            i = g * SPAN + ci
            rc = slot_rc[d * slots + i]
            live = slot_live[d * slots + i]
            mask = jnp.where(
                lax.broadcasted_iota(i32, (CHUNK, quarter), 0) < live, f32(1), f32(0))
            act, slope, cot = [], [], []
            for t in range(TOWERS):
                pre = ex_rx[g, 0, t, s]
                for q in range(1, FEATS):
                    pre = pre + ex_rx[g, q, t, s]
                pre = pre + bias_here[t:t + 1]
                square = pre * pre
                th = jnp.tanh(f32(0.7978845608028654) * (pre + f32(0.044715) * (square * pre)))
                cdf = f32(0.5) * (f32(1) + th)
                act.append(pre * cdf)
                slope.append(cdf + f32(0.5) * pre * (f32(1) - th * th) * (
                    f32(0.7978845608028654) * (f32(1) + f32(3 * 0.044715) * square)))
                cot.append(cot_rx[lax.div(rc, 8), lax.rem(rc, 8), t].astype(f32) * mask)
            for t in range(TOWERS):
                out = so_ref[2 * t:2 * t + 1] * act[0] + so_ref[2 * t + 1:2 * t + 2] * act[1]
                acts[i, d, t] = (out * mask).astype(bf16)
                for u in range(TOWERS):
                    sog_acc[2 * t + u] = sog_acc[2 * t + u] + cot[t] * act[u]
            for u in range(TOWERS):
                back = so_ref[u:u + 1] * cot[0] + so_ref[2 + u:3 + u] * cot[1]
                gp[g, feat, u, s] = (slope[u] * back).astype(bf16)
            return carry

        lax.fori_loop(0, per, one, 0)
        for o in range(1, FEATS):
            gp_copy(g, o).start()

    tile = part_dim // 3

    def backward(g, t):
        rows = jnp.concatenate(
            [gp[g, q, t].reshape(per * CHUNK, quarter) for q in range(FEATS)], axis=1)
        for h in range(2):
            part[t, h] = jnp.dot(
                rows, w[t, :, h * part_dim:(h + 1) * part_dim],
                preferred_element_type=f32).reshape(per, CHUNK, part_dim)

    def tile_at(q):
        t, n = lax.div(q, 6), lax.rem(q, 6)
        return t, lax.div(n, 3), pl.multiple_of(n * tile, 128), pl.multiple_of(lax.rem(n, 3) * tile, 128)

    def wg_copy(q):
        t, _, whole_at, _ = tile_at(q)
        cols = pl.ds(whole_at, tile)
        return pltpu.make_async_copy(wg_acc.at[t, :, cols], wg_hbm.at[t, :, cols], wg_sem.at[q])

    def weight_tile(q, first, count):
        t, h, whole_at, part_at = tile_at(q)
        rows = x[first:first + count, t, h, :, :, :, pl.ds(part_at, tile)].reshape(
            count * per * CHUNK, tile)
        for e in range(FEATS):
            grads = gp[first:first + count, e, t].reshape(count * per * CHUNK, quarter)
            value = lax.dot_general(
                grads, rows, (((0,), (0,)), ((), ())), preferred_element_type=f32)
            at = (t, pl.ds(e * quarter, quarter), pl.ds(whole_at, tile))
            wg_acc[at] = value + wg_acc[at] if first else value

    def gather_unit(g, q):
        u = PIECES * SPAN * g + q
        ci, t, h = lax.div(q, PIECES), lax.rem(lax.div(q, 2), 2), lax.rem(q, 2)
        i = SPAN * g + ci
        for d in (0, 1):
            own = own_piece(d, jnp.clip(i - own_at[d], 0, own_k[d] - 1), t, h)

            @pl.when(u < sent)
            def _(d=d, own=own):
                @pl.when(u >= PIECES)
                def _():
                    ring_unit_copy(d, u).wait_recv()

                x[g, t, h, d, ci] = jnp.where(i >= own_at[d], own, land[d, u])

            @pl.when(u >= sent)
            def _(d=d, own=own):
                x[g, t, h, d, ci] = own

            m = u + PIECES

            @pl.when(m < sent)
            def _(d=d):
                @pl.when(m >= 8 + PIECES)
                def _():
                    ring_unit_copy(d, m).wait_send()

                here = i + 1 < own_k[d]
                c = chunk_of(d, jnp.minimum(i + 1, own_k[d] - 1), own_k[0])
                src = jnp.maximum(i + 1 - own_k[d], 0)
                ring_tx[d, lax.rem(m, 8)] = x[
                    jnp.where(here, groups + lax.div(c, per), lax.div(src, SPAN)), t, h,
                    jnp.where(here, lax.div(lax.rem(c, per), SPAN), d),
                    jnp.where(here, lax.rem(c, SPAN), lax.rem(src, SPAN))]
                ring_unit_copy(d, m).start()

    def sum_copy(d, v):
        return pltpu.make_async_remote_copy(
            src_ref=sums.at[d, v], dst_ref=land.at[d, v], send_sem=rs_ss.at[d, lax.rem(v, HELD)],
            recv_sem=rs_rs.at[d, v], device_id=(ring_to[d], feat), device_id_type=MESH)

    def sum_unit(g, q):
        v = PIECES * SPAN * g + q
        ci, t, h = lax.div(q, PIECES), lax.rem(lax.div(q, 2), 2), lax.rem(q, 2)
        before = v - PIECES
        for d in (0, 1):
            @pl.when(jnp.logical_and(before >= 0, before < sent))
            def _(d=d):
                sum_copy(d, before).wait_recv()
                held[d, lax.rem(before, HELD)] = land[d, before]

            came = held[d, lax.rem(v - PIECES * prev_k[d] + HELD, HELD)].astype(f32)
            value = part[t, h, d * SPAN + ci] + came * jnp.where(
                v >= PIECES * prev_k[d], f32(1), f32(0))
            sums[d, v] = value.astype(bf16)

            @pl.when(v < sent)
            def _(d=d):
                @pl.when(v >= HELD)
                def _():
                    sum_copy(d, v).wait_send()

                sum_copy(d, v).start()

    def act_copy(r):
        return pltpu.make_async_remote_copy(
            src_ref=act_tx.at[r], dst_ref=act_rx.at[half_at], send_sem=act_ss.at[r],
            recv_sem=act_rs.at[half_at], device_id=(r, row_feat), device_id_type=MESH)

    def act_wait(s):
        return pltpu.make_async_remote_copy(
            src_ref=act_tx.at[0], dst_ref=act_rx.at[s], send_sem=act_ss.at[0],
            recv_sem=act_rs.at[s], device_id=(blk, feat), device_id_type=MESH)

    def sog_copy(r):
        return pltpu.make_async_remote_copy(
            src_ref=sog_tx, dst_ref=sog_rx.at[half_at], send_sem=sog_ss.at[r],
            recv_sem=sog_rs.at[half_at], device_id=(r, row_feat), device_id_type=MESH)

    def sog_wait(s):
        return pltpu.make_async_remote_copy(
            src_ref=sog_tx, dst_ref=sog_rx.at[s], send_sem=sog_ss.at[0],
            recv_sem=sog_rs.at[s], device_id=(blk, feat), device_id_type=MESH)

    def send_acts(r):
        at = ring_place(r)
        first, second = kd[at], kd[PLACES + at]
        for c in range(8):
            late = c > first
            d = jnp.where(late, 1, 0) if c > 1 else c
            pos = jnp.where(late, c - first, c - 1) if c > 1 else 0
            i = jnp.minimum(start[d * PLACES + at] + pos, slots - 1)
            keep = jnp.where(c < first + second, f32(1), f32(0))
            for t in range(TOWERS):
                act_tx[r, c, t] = (acts[i, d, t].astype(f32) * keep).astype(bf16)

        @pl.when(near_not_me(r))
        def _():
            act_copy(r).start()
            sog_copy(r).start()

        @pl.when(jnp.logical_not(near_not_me(r)))
        def _():
            act_rx[half_at] = act_tx[r]
            sog_rx[half_at] = sog_tx[...]

    def add_bias():
        for e in range(FEATS):
            for t in range(TOWERS):
                def add(g, total, e=e, t=t):
                    return total + jnp.sum(gp[g, e, t].astype(f32), axis=0)

                total = lax.fori_loop(0, groups, add, jnp.zeros((CHUNK, quarter), f32))
                bg_out[t:t + 1, e * quarter:(e + 1) * quarter] = jnp.sum(
                    total, axis=0, keepdims=True)

    early = groups - 2

    def iteration(it, carry):
        @pl.when(it >= 3)
        def _():
            for o in range(1, FEATS):
                gp_wait(it - 3, o).wait_recv()
            backward(it - 3, 0)

        @pl.when(it == 1)
        def _():
            w_copy.wait()

        @pl.when(it == 2)
        def _():
            def arrived(r, carry):
                @pl.when(jnp.logical_or(r != blk, cot_feat != feat))
                def _():
                    cot_wait(r).wait_recv()

                return carry

            lax.fori_loop(0, PLACES, arrived, 0)

        @pl.when(jnp.logical_and(it >= 2, it < groups + 2))
        def _():
            head(it - 2)

        @pl.when(it == groups + 1)
        def _():
            sog_tx[...] = jnp.concatenate(
                [jnp.sum(sog_acc[e], axis=0, keepdims=True) for e in range(4)] * 2, axis=0)

        @pl.when(it >= 3)
        def _():
            for d in (0, 1):
                pl.semaphore_wait(free.at[d], 1)

        def unit(q, carry):
            @pl.when(it < groups)
            def _():
                gather_unit(it, q)

            @pl.when(it >= 3)
            def _():
                sum_unit(it - 3, q)

            @pl.when(jnp.logical_and(
                lax.rem(q, 2) == 0, jnp.logical_and(q < 4, jnp.logical_and(it >= 1, it < groups + 1))))
            def _():
                forward(it - 1, lax.div(q, 2))

            @pl.when(jnp.logical_and(it >= 3, q == 1))
            def _():
                backward(it - 3, 1)

            @pl.when(it == groups + 1)
            def _():
                send_acts(q)

            @pl.when(jnp.logical_and(it == groups + 2, q == 3))
            def _():
                add_bias()

            @pl.when(jnp.logical_and(it == groups, q < 6))
            def _():
                weight_tile(q, 0, early)

            @pl.when(jnp.logical_and(it == groups + 1, q < 6))
            def _():
                weight_tile(q + 6, 0, early)

            @pl.when(jnp.logical_and(it == groups + 2, q < 6))
            def _():
                for e in range(2):
                    weight_tile(2 * q + e, early, 2)
                    wg_copy(2 * q + e).start()

            return carry

        lax.fori_loop(0, PIECES * SPAN, unit, 0)

        @pl.when(it < groups)
        def _():
            for d in (0, 1):
                pl.semaphore_signal(
                    free.at[d], inc=1, device_id=(ring_blk(ring_from[d]), feat), device_id_type=MESH)

        return carry

    lax.fori_loop(0, groups + 3, iteration, 0)

    for c in range(8):
        late = c > own_k[0]
        d = jnp.where(late, 1, 0) if c > 1 else c
        i = jnp.where(late, own_at[1] + c - own_k[0], own_at[0] + c - 1) if c > 1 else own_at[c]
        i = jnp.clip(i, 0, slots - 1)
        keep = jnp.where(c < own_k[0] + own_k[1], f32(1), f32(0))
        for t in range(TOWERS):
            for h in range(2):
                gf_out[c, t, :, h * part_dim:(h + 1) * part_dim] = (
                    sums[d, PIECES * i + 2 * t + h].astype(f32) * keep).astype(bf16)

    def finish(s, carry):
        @pl.when(far_not_me(s))
        def _():
            act_wait(s).wait_recv()
            sog_wait(s).wait_recv()

        @pl.when(cot_not_me(s))
        def _():
            cot_copy(s, cot_ref.at[0]).wait_send()

        @pl.when(near_not_me(s))
        def _():
            act_copy(s).wait_send()
            sog_copy(s).wait_send()

        return carry

    lax.fori_loop(0, 8, finish, 0)
    act_out[...] = act_rx[...]
    sog_out[...] = sog_rx[...]

    def finish_sums(v, carry):
        for d in (0, 1):
            sum_copy(d, v).wait_send()
        return carry

    lax.fori_loop(sent - HELD, sent, finish_sums, 0)
    for m in range(sent - 8, sent):
        for d in (0, 1):
            ring_unit_copy(d, jnp.int32(m)).wait_send()
    for o in range(1, FEATS):
        for g in (groups - 2, groups - 1):
            ex_copy(g % 2, g, o).wait_send()

        def finish_gp(g, carry, o=o):
            gp_copy(g, o).wait_send()
            return carry

        lax.fori_loop(0, groups, finish_gp, 0)
    for q in range(12):
        wg_copy(jnp.int32(q)).wait()


def fc_layer(steps, number, n, so, bias, x, first, cot, relay, weight):
    units, feats_dim = weight.shape[1:]
    quarter = units // FEATS
    groups = -(-steps // SPAN)
    slots = groups * SPAN
    vm = pltpu.VMEM
    dma = pltpu.SemaphoreType.DMA
    sm = pltpu.SMEM
    unit = (CHUNK, feats_dim // 2)
    vmem_spec = pl.BlockSpec(memory_space=pltpu.VMEM)
    any_spec = pl.BlockSpec(memory_space=pl.ANY)
    rows = 2 * slots * CHUNK
    return pl.pallas_call(
        functools.partial(fc_kernel, steps),
        out_shape=(
            jax.ShapeDtypeStruct((8, 8, TOWERS, CHUNK, quarter), bf16),
            jax.ShapeDtypeStruct((8, TOWERS, CHUNK, feats_dim), bf16),
            jax.ShapeDtypeStruct(weight.shape, f32),
            jax.ShapeDtypeStruct((TOWERS, units), f32),
            jax.ShapeDtypeStruct((8, 8, quarter), f32),
        ),
        in_specs=[pl.BlockSpec(memory_space=pltpu.SMEM)] + [vmem_spec] * 6 + [any_spec],
        out_specs=(vmem_spec, vmem_spec, any_spec, vmem_spec, vmem_spec),
        scratch_shapes=[
            vm(weight.shape, bf16),
            vm((groups + 8 // (2 * SPAN), TOWERS, 2, 2, SPAN) + unit, bf16),
            vm((2, PIECES * (steps - 1)) + unit, bf16),
            vm((2, 8) + unit, bf16),
            vm((2, FEATS, TOWERS, 2 * SPAN, CHUNK, quarter), f32),
            vm((groups, FEATS, TOWERS, 2 * SPAN, CHUNK, quarter), f32),
            vm((groups, FEATS, TOWERS, 2 * SPAN, CHUNK, quarter), bf16),
            vm((TOWERS, 2, 2 * SPAN) + unit, f32),
            vm((2, HELD) + unit, bf16),
            vm((2, PIECES * slots) + unit, bf16),
            vm((8, 8, TOWERS, CHUNK, quarter), bf16),
            vm((slots, 2, TOWERS, CHUNK, quarter), bf16),
            vm((8, 8, TOWERS, CHUNK, quarter), bf16),
            vm((8, 8, TOWERS, CHUNK, quarter), bf16),
            vm((4, CHUNK, quarter), f32),
            vm((8, quarter), f32),
            vm((8, 8, quarter), f32),
            vm(weight.shape, f32),
            sm((2 * PLACES,), i32),
            sm((PLACES,), i32),
            sm((2 * PLACES,), i32),
            sm((2,), i32),
            sm((2 * slots,), i32),
            sm((2 * slots,), i32),
            dma,
            dma((2, 8)),
            dma((2, PIECES * (steps - 1))),
            dma((2, HELD)),
            dma((2, PIECES * (steps - 1))),
            dma((2, 3)),
            dma((groups, FEATS)),
            dma((groups, 3)),
            dma((groups, FEATS)),
            dma((8,)),
            dma((8,)),
            dma((8,)),
            dma((8,)),
            dma((8,)),
            dma((8,)),
            dma((12,)),
            pltpu.SemaphoreType.REGULAR((2,)),
        ],
        cost_estimate=pl.CostEstimate(
            flops=6 * rows * TOWERS * units * feats_dim, bytes_accessed=30 << 20,
            transcendentals=rows * TOWERS * quarter),
        compiler_params=pltpu.CompilerParams(
            collective_id=number, has_side_effects=True, vmem_limit_bytes=60 << 20),
    )(n, so, bias, x, first, cot, relay, weight)


def layout_matrix(chans):
    table = np.zeros((4 * 2 * chans, 4 * 2 * chans), np.float32)
    for q0 in range(4):
        for c in range(chans):
            for t in range(TOWERS):
                lane = 4 * ((9 * c) % 32) + q0
                table[q0 * 2 * chans + 2 * c + t, (2 * t + c // 32) * 128 + lane] = 1
    return table


def lane_sources():
    slot = np.arange(128) // 4
    rows = [(slot + 32 * j) % 9 for j in range(9)] + [(2 * (q1 - slot)) % 9 for q1 in range(9)]
    return np.broadcast_to(np.stack(rows)[:, None, :], (18, CHUNK, 128)).astype(np.int32)


def lane_pairs(chans):
    shape = (chans, TOWERS * chans)
    lane, chan = lax.broadcasted_iota(i32, shape, 1), lax.broadcasted_iota(i32, shape, 0)
    return tuple((lane == 2 * chan + t).astype(f32) for t in range(TOWERS))


def exact_dot(a, b, dims):
    return lax.dot_general(
        a, b, (dims, ((), ())), precision=lax.Precision.HIGHEST, preferred_element_type=f32)


def pair_swap():
    even = (lax.broadcasted_iota(i32, (CHUNK, 128), 1) & 1) == 0

    def swap(value):
        return jnp.where(even, pltpu.roll(value, 127, 1), pltpu.roll(value, 1, 1))

    return swap


BATCH = 2
LAST = 4


def entry_kernel(
    cc_ref, so_ref, si_ref, perm_ref, source_ref, cot_ref, conv_ref,
    feats_out, pooled_out, n_out, pick_out, so_out, relay_out, first_out, s_out,
    n_tx, n_rx, so_tx, so_rx, relay_rx, first_tx, first_rx, s_ref,
    n_ss, n_rs, so_ss, so_rs, relay_ss, relay_rs, first_ss, first_rs,
):
    blk, feat = lax.axis_index("blk"), lax.axis_index("feat")
    step = pl.program_id(0)
    holds = lax.div(blk, 2) == feat

    def n_copy(o):
        to = lax.rem(blk + o, PLACES)
        return pltpu.make_async_remote_copy(
            src_ref=n_tx, dst_ref=n_rx.at[blk], send_sem=n_ss.at[o - 1], recv_sem=n_rs.at[blk],
            device_id=(to, feat), device_id_type=MESH)

    def n_wait(o):
        src = lax.rem(blk + o, PLACES)
        return pltpu.make_async_remote_copy(
            src_ref=n_tx, dst_ref=n_rx.at[src], send_sem=n_ss.at[o - 1], recv_sem=n_rs.at[src],
            device_id=(src, feat), device_id_type=MESH)

    def so_copy(o):
        to = lax.rem(feat + o, FEATS)
        return pltpu.make_async_remote_copy(
            src_ref=so_tx.at[to], dst_ref=so_rx, send_sem=so_ss.at[o - 1], recv_sem=so_rs,
            device_id=(blk, to), device_id_type=MESH)

    across_y = lax.rem(feat + 2, FEATS)
    place = ring_place(blk)
    half = feats_out.shape[-1] // 2

    def first_copy(d, m):
        return pltpu.make_async_remote_copy(
            src_ref=first_tx.at[d, m], dst_ref=first_rx.at[d, m], send_sem=first_ss.at[d, m],
            recv_sem=first_rs.at[d, m],
            device_id=(ring_blk(lax.rem(place + (7 if d else 1), 8)), feat), device_id_type=MESH)

    def relay_copy(s):
        return pltpu.make_async_remote_copy(
            src_ref=cot_ref.at[s // 2 * FEATS + 2 * lax.div(across_y, 2) + s % 2],
            dst_ref=relay_rx.at[s], send_sem=relay_ss.at[s], recv_sem=relay_rs.at[s],
            device_id=(blk, across_y), device_id_type=MESH)

    @pl.when(step == 0)
    def _():
        bar = pltpu.get_barrier_semaphore()
        for o in range(1, PLACES):
            pl.semaphore_signal(
                bar, inc=1, device_id=(lax.rem(blk + o, PLACES), feat), device_id_type=MESH)
        for o in range(1, FEATS):
            pl.semaphore_signal(
                bar, inc=1, device_id=(blk, lax.rem(feat + o, FEATS)), device_id_type=MESH)
        total = cc_ref[0]
        for e in range(1, cc_ref.shape[0]):
            total = total + cc_ref[e]
        n_tx[...] = jnp.full(n_tx.shape, total, i32)
        n_rx[blk] = n_tx[...]
        for q in range(FEATS):
            at = pl.ds(pl.multiple_of(lax.rem(blk, 2) * 512 + q * 128, 128), 128)
            for t in range(TOWERS):
                so_tx[q, 2 * t:2 * t + 2] = so_ref[t, :, at]
                so_tx[q, 4 + 2 * t:6 + 2 * t] = so_ref[t, :, at]
        even, odd = lane_pairs(si_ref.shape[-1])
        rows = [[exact_dot(si_ref[t], v, ((1,), (0,))) for v in (even, odd)] for t in range(TOWERS)]
        s_ref[0:1] = rows[0][0][0:1] + rows[1][1][1:2]
        s_ref[1:2] = rows[0][0][1:2] + rows[1][1][0:1]
        s_ref[2:3] = rows[1][0][0:1] + rows[0][1][1:2]
        s_ref[3:8] = jnp.zeros((5, s_ref.shape[1]), f32)
        pl.semaphore_wait(bar, PLACES - 1 + FEATS - 1)
        for o in range(1, PLACES):
            n_copy(o).start()
        for s in range(4):
            relay_copy(s).start()

        @pl.when(holds)
        def _():
            so_rx[...] = so_tx[feat]
            for o in range(1, FEATS):
                so_copy(o).start()

    def chunk(e, carry):
        swap = pair_swap()
        at_row = pl.ds(pl.multiple_of(e * CHUNK, CHUNK), CHUNK)
        across = {}
        for row in range(MAP):
            line = [conv_ref[MAP * row + col, at_row].astype(f32) for col in range(MAP)]
            for v in range(GRID):
                across[row, v] = line[2 * v] + line[2 * v + 1] + line[2 * v + 2]
        own, other = s_ref[0:1], s_ref[1:2]
        parts = []
        for q1 in range(9):
            here = []
            for q0 in range(4):
                q = 4 * q1 + q0
                u, v = q // GRID, q % GRID
                pooled = (across[2 * u, v] + across[2 * u + 1, v] + across[2 * u + 2, v]) * f32(1 / 9)
                pooled_out[e, q] = pooled
                here.append((own * pooled + other * swap(pooled)).astype(bf16))
            parts.append(jnp.concatenate(here, axis=1))
        spread = jnp.dot(
            jnp.concatenate(parts, axis=0), perm_ref[...], preferred_element_type=f32)
        turned = [
            pltpu.roll(spread[q1 * CHUNK:(q1 + 1) * CHUNK, at:at + 128], 4 * q1, 1)
            if q1 else spread[0:CHUNK, at:at + 128] for q1 in range(9) for at in range(0, 512, 128)]
        for j in range(9):
            source = source_ref[j]
            tiles = turned[0:4]
            for q1 in range(1, 9):
                here = source == q1
                tiles = [jnp.where(here, turned[4 * q1 + k], tiles[k]) for k in range(4)]
            for k in range(4):
                n = 9 * (k % 2) + j
                feats_out[e, k // 2, :, n * 128:(n + 1) * 128] = tiles[k].astype(bf16)
        return carry

    lax.fori_loop(0, BATCH, chunk, 0)

    @pl.when(step == 0)
    def _():
        for m in range(PIECES):
            for d in range(2):
                first_tx[d, m] = feats_out[d, m // 2, :, m % 2 * half:(m % 2 + 1) * half]
                first_copy(d, m).start()

    @pl.when(step == pl.num_programs(0) - 1)
    def _():
        for m in range(PIECES):
            for d in range(2):
                first_copy(d, m).wait()
        first_out[...] = first_rx[...]
        s_out[...] = s_ref[...]
        for o in range(1, PLACES):
            n_wait(o).wait_recv()
            n_copy(o).wait_send()

        @pl.when(holds)
        def _():
            for o in range(1, FEATS):
                so_copy(o).wait_send()

        @pl.when(jnp.logical_not(holds))
        def _():
            so_copy(1).wait_recv()

        for s in range(4):
            relay_copy(s).wait()
        chunks = jnp.int32(0)
        for q in range(PLACES):
            n = jnp.max(n_rx[q])
            n_out[q] = n
            chunks = chunks + lax.div(n + (CHUNK - 1), CHUNK)
        need = lax.div(chunks + 1, 2)
        pick_out[0] = sum(((need > c).astype(i32) for c in CLASSES), jnp.int32(0))
        so_out[...] = so_rx[...]
        relay_out[...] = relay_rx[...]


def exit_kernel(
    s_ref, perm_ref, source_ref, bg_ref, sog_ref, gf_ref, pooled_ref, wg_ref,
    conv_out, si_out, bg_out, sog_out, wg_out, acc,
):
    step = pl.program_id(0)

    @pl.when(step == 0)
    def _():
        acc[...] = jnp.zeros_like(acc)

    wg_out[...] = wg_ref[...]
    def chunk(e, carry):
        swap = pair_swap()
        at_row = pl.ds(pl.multiple_of(e * CHUNK, CHUNK), CHUNK)
        tiles = [
            gf_ref[e, k // 2, :, (9 * (k % 2) + j) * 128:(9 * (k % 2) + j + 1) * 128].astype(f32)
            for j in range(9) for k in range(4)]
        rows = []
        for q1 in range(9):
            source = source_ref[9 + q1]
            here = tiles[0:4]
            for j in range(1, 9):
                mask = source == j
                here = [jnp.where(mask, tiles[4 * j + k], here[k]) for k in range(4)]
            rows.append(jnp.concatenate(
                [pltpu.roll(v, 128 - 4 * q1, 1) if q1 else v for v in here], axis=1).astype(bf16))
        grads = lax.dot_general(
            jnp.concatenate(rows, axis=0), perm_ref[...], (((1,), (1,)), ((), ())),
            preferred_element_type=f32)
        own, other = s_ref[0:1] * f32(1 / 9), s_ref[2:3] * f32(1 / 9)
        same = acc[0]
        cross = acc[1]
        back = {}
        for q in range(GRID * GRID):
            q1, q0 = q // 4, q % 4
            grad = grads[q1 * CHUNK:(q1 + 1) * CHUNK, q0 * 128:(q0 + 1) * 128]
            pooled = pooled_ref[e, q]
            swapped = swap(grad)
            same = same + grad * pooled
            cross = cross + swapped * pooled
            back[q // GRID, q % GRID] = own * grad + other * swapped
        acc[0] = same
        acc[1] = cross
        lines = []
        for u in range(GRID):
            line = []
            for col in range(MAP):
                v = col // 2
                if col % 2:
                    line.append(back[u, v])
                elif col == 0:
                    line.append(back[u, 0])
                elif col == MAP - 1:
                    line.append(back[u, GRID - 1])
                else:
                    line.append(back[u, v - 1] + back[u, v])
            lines.append(line)
        for row in range(MAP):
            u = row // 2
            for col in range(MAP):
                if row % 2 or row == 0:
                    value = lines[u][col]
                elif row == MAP - 1:
                    value = lines[GRID - 1][col]
                else:
                    value = lines[u - 1][col] + lines[u][col]
                conv_out[MAP * row + col, at_row] = value.astype(bf16)
        return carry

    lax.fori_loop(0, LAST, chunk, 0)

    @pl.when(step == pl.num_programs(0) - 1)
    def _():
        sums = jnp.concatenate(
            [jnp.sum(acc[e], axis=0, keepdims=True) for e in range(2)] * 4, axis=0)
        chans = sums.shape[1] // TOWERS
        even, odd = (exact_dot(sums, v, ((1,), (1,))) for v in lane_pairs(chans))
        si_out[...] = jnp.zeros_like(si_out)
        si_out[0:1, 0:chans] = even[0:1]
        si_out[1:2, 0:chans] = odd[1:2]
        si_out[2:3, 0:chans] = even[1:2]
        si_out[3:4, 0:chans] = odd[0:1]
        bg_out[...] = bg_ref[...]
        for e in range(8):
            for t in range(TOWERS):
                sog_out[t, :, e * 128:(e + 1) * 128] = sog_ref[e, TOWERS * t:TOWERS * (t + 1)]


def total_kernel(x_ref, out, rx, ss, rs):
    blk, feat = lax.axis_index("blk"), lax.axis_index("feat")

    def copy(o):
        return pltpu.make_async_remote_copy(
            src_ref=x_ref, dst_ref=rx.at[blk], send_sem=ss.at[o - 1], recv_sem=rs.at[blk],
            device_id=(lax.rem(blk + o, PLACES), feat), device_id_type=MESH)

    def wait(o):
        src = lax.rem(blk + o, PLACES)
        return pltpu.make_async_remote_copy(
            src_ref=x_ref, dst_ref=rx.at[src], send_sem=ss.at[o - 1], recv_sem=rs.at[src],
            device_id=(src, feat), device_id_type=MESH)

    bar = pltpu.get_barrier_semaphore()
    for o in range(1, PLACES):
        pl.semaphore_signal(
            bar, inc=1, device_id=(lax.rem(blk + o, PLACES), feat), device_id_type=MESH)
    pl.semaphore_wait(bar, PLACES - 1)
    for o in range(1, PLACES):
        copy(o).start()
    rx[blk] = x_ref[...]
    for o in range(1, PLACES):
        wait(o).wait_recv()
    total = rx[0]
    for q in range(1, PLACES):
        total = total + rx[q]
    for t in range(TOWERS):
        out[t] = total[TOWERS * t:TOWERS * (t + 1), 0:out.shape[-1]]
    for o in range(1, PLACES):
        copy(o).wait_send()


def entry(counts, so, stitch, cot, conv):
    spots, rows, merged = conv.shape
    chunks = rows // CHUNK
    chans = merged // TOWERS
    wide = chans * GRID * GRID
    vm, dma = pltpu.VMEM, pltpu.SemaphoreType.DMA
    whole = pl.BlockSpec(memory_space=pltpu.VMEM)
    scalars = pl.BlockSpec(memory_space=pltpu.SMEM)
    return pl.pallas_call(
        entry_kernel,
        grid=(chunks // BATCH,),
        out_shape=(
            jax.ShapeDtypeStruct((chunks, TOWERS, CHUNK, wide), bf16),
            jax.ShapeDtypeStruct((chunks, GRID * GRID, CHUNK, merged), f32),
            jax.ShapeDtypeStruct((PLACES,), i32),
            jax.ShapeDtypeStruct((1,), i32),
            jax.ShapeDtypeStruct((8, 128), f32),
            jax.ShapeDtypeStruct((4,) + cot.shape[1:], bf16),
            jax.ShapeDtypeStruct((2, PIECES, CHUNK, wide // 2), bf16),
            jax.ShapeDtypeStruct((8, merged), f32),
        ),
        in_specs=[scalars] + [whole] * 5 + [
            pl.BlockSpec((spots, BATCH * CHUNK, merged), lambda c: (0, c, 0))],
        out_specs=(
            pl.BlockSpec((BATCH, TOWERS, CHUNK, wide), lambda c: (c, 0, 0, 0)),
            pl.BlockSpec((BATCH, GRID * GRID, CHUNK, merged), lambda c: (c, 0, 0, 0)),
            scalars, scalars, whole, whole, whole, whole,
        ),
        scratch_shapes=[
            vm((8, 128), i32), vm((PLACES, 8, 128), i32), vm((FEATS, 8, 128), f32), vm((8, 128), f32),
            vm((4,) + cot.shape[1:], bf16), vm((2, PIECES, CHUNK, wide // 2), bf16),
            vm((2, PIECES, CHUNK, wide // 2), bf16), vm((8, merged), f32),
            dma((PLACES - 1,)), dma((PLACES,)), dma((FEATS - 1,)), dma, dma((4,)), dma((4,)),
            dma((2, PIECES)), dma((2, PIECES)),
        ],
        cost_estimate=pl.CostEstimate(flops=1 << 30, bytes_accessed=10 << 20, transcendentals=0),
        compiler_params=pltpu.CompilerParams(
            collective_id=20, has_side_effects=True, vmem_limit_bytes=60 << 20),
    )(counts, so, stitch, jnp.asarray(layout_matrix(chans), bf16), jnp.asarray(lane_sources()), cot, conv)


def leave(s_rows, bias_grad, sog, gf, pooled, weight_grad, spots):
    chunks, towers, _, wide = gf.shape
    merged = pooled.shape[-1]
    vm = pltpu.VMEM
    whole = pl.BlockSpec(memory_space=pltpu.VMEM)
    share = pl.BlockSpec(
        (towers, weight_grad.shape[1] * LAST // chunks, wide), lambda c: (0, c, 0))
    return pl.pallas_call(
        exit_kernel,
        grid=(chunks // LAST,),
        out_shape=(
            jax.ShapeDtypeStruct((spots, chunks * CHUNK, merged), bf16),
            jax.ShapeDtypeStruct((8, 128), f32),
            jax.ShapeDtypeStruct(bias_grad.shape, f32),
            jax.ShapeDtypeStruct((TOWERS, TOWERS, 8 * sog.shape[-1]), f32),
            jax.ShapeDtypeStruct(weight_grad.shape, f32),
        ),
        in_specs=[whole] * 5 + [
            pl.BlockSpec((LAST, towers, CHUNK, wide), lambda c: (c, 0, 0, 0)),
            pl.BlockSpec((LAST, GRID * GRID, CHUNK, merged), lambda c: (c, 0, 0, 0)),
            share],
        out_specs=(
            pl.BlockSpec((spots, LAST * CHUNK, merged), lambda c: (0, c, 0)),
            whole, whole, whole, share,
        ),
        scratch_shapes=[vm((2, CHUNK, 128), f32)],
        cost_estimate=pl.CostEstimate(flops=1 << 30, bytes_accessed=30 << 20, transcendentals=0),
        compiler_params=pltpu.CompilerParams(vmem_limit_bytes=60 << 20),
    )(s_rows, jnp.asarray(layout_matrix(merged // TOWERS), bf16),
      jnp.asarray(lane_sources()), bias_grad, sog, gf, pooled, weight_grad)


def total_over_blk(value):
    whole = pl.BlockSpec(memory_space=pltpu.VMEM)
    dma = pltpu.SemaphoreType.DMA
    return pl.pallas_call(
        total_kernel,
        out_shape=jax.ShapeDtypeStruct((TOWERS, TOWERS, value.shape[1] // TOWERS), f32),
        in_specs=[whole],
        out_specs=whole,
        scratch_shapes=[
            pltpu.VMEM((PLACES,) + value.shape, f32), dma((PLACES - 1,)), dma((PLACES,))],
        compiler_params=pltpu.CompilerParams(
            collective_id=21, has_side_effects=True, vmem_limit_bytes=16 << 20),
    )(value)


def body_ring(conv_maps, crop_counts, fc_weight, fc_bias, stitch_in, stitch_out, cotangent):
    num_rows = conv_maps.shape[0]
    units = fc_weight.shape[1]
    quarter = units // FEATS
    chunks = num_rows // CHUNK
    cot = cotangent.reshape(chunks, CHUNK, TOWERS, 8, quarter).transpose(3, 0, 2, 1, 4)
    feats, pooled, n, pick, so, relay, first, s_rows = entry(
        crop_counts, stitch_out, stitch_in, cot, conv_maps.transpose(1, 0, 2))
    full = PLACES * chunks // 2
    kinds = CLASSES + (full,)
    act, gf, weight_grad, bias_grad, sog = lax.switch(
        pick[0],
        [functools.partial(fc_layer, steps, at) for at, steps in enumerate(kinds)],
        n, so, fc_bias, feats, first, cot, relay, fc_weight)
    activations = act.transpose(1, 3, 2, 0, 4).reshape(num_rows, TOWERS, -1)
    conv_grad, si, bias_grad, stitch_out_grad, weight_grad = leave(
        s_rows, bias_grad, sog, gf, pooled, weight_grad, conv_maps.shape[1])
    conv_grad = conv_grad.transpose(1, 0, 2)
    stitch_in_grad = total_over_blk(si)
    return (activations, conv_grad, weight_grad, bias_grad, stitch_in_grad, stitch_out_grad)


def solution(mesh):
    ring = mesh.shape["blk"] == PLACES and mesh.shape["feat"] == FEATS
    return jax.shard_map(
        body_ring if ring else body_plain,
        mesh=mesh,
        in_specs=(
            P("blk", None, "feat"),
            P("blk"),
            P(None, "blk", "feat"),
            P(),
            P(None, None, "feat"),
            P(None, None, "feat"),
            P("blk", None, "feat"),
        ),
        out_specs=(
            P("blk", None, "feat"),
            P("blk", None, "feat"),
            P(None, "blk", "feat"),
            P(None, "blk"),
            P(None, None, "feat"),
            P(None, None, "feat"),
        ),
        check_vma=False,
    )
```

```python
import functools

import jax
import jax.numpy as jnp
import numpy as np
from jax import lax
from jax.experimental import pallas as pl
from jax.experimental.pallas import tpu as pltpu
from jax.sharding import PartitionSpec as P

MAP = 13
GRID = 6
TOWERS = 2
CHUNK = 16
CLASSES = (18, 19, 20, 21, 22, 23)
SPAN = 2
PIECES = 4
HELD = 16
PLACES = 8
FEATS = 4
RING_BLK = (0, 2, 4, 6, 7, 5, 3, 1)
MESH = pl.DeviceIdType.MESH
f32 = jnp.float32
bf16 = jnp.bfloat16
i32 = jnp.int32


def pool_table(dtype):
    position = jnp.arange(MAP * MAP)
    row_pos = position // MAP
    col_pos = position % MAP
    cell = jnp.arange(GRID * GRID)
    row_cell = cell // GRID
    col_cell = cell % GRID
    down = row_pos[:, None] - 2 * row_cell[None, :]
    across = col_pos[:, None] - 2 * col_cell[None, :]
    inside = (down >= 0) & (down < 3) & (across >= 0) & (across < 3)
    return inside.astype(dtype)


def stitch_first(pooled, stitch_in):
    return jnp.einsum("tuc,rucq->rtcq", stitch_in, pooled, precision=lax.Precision.HIGHEST)


def stitch_head(pre, stitch_out):
    act = jax.nn.gelu(pre)
    return jnp.einsum("tuk,ruk->rtk", stitch_out, act, precision=lax.Precision.HIGHEST)


def body_plain(conv_maps, crop_counts, fc_weight, fc_bias, stitch_in, stitch_out, cotangent):
    num_rows = conv_maps.shape[0]
    merged = conv_maps.shape[2]
    chans = merged // TOWERS
    cols = fc_weight.shape[1]
    feat_idx = lax.axis_index("feat")
    blk_idx = lax.axis_index("blk")
    sums = jnp.einsum("rpm,pq->rqm", conv_maps, pool_table(bf16), preferred_element_type=f32)
    pooled = jnp.transpose(sums.reshape(num_rows, GRID * GRID, chans, TOWERS), (0, 3, 2, 1)) * (
        1.0 / 9.0
    )
    mixed, pull_first = jax.vjp(stitch_first, pooled, stitch_in)
    feats = mixed.astype(bf16).reshape(num_rows, TOWERS, -1)
    own_cols = jnp.einsum(
        "rtf,tnf->rtn",
        lax.all_gather(feats, "blk", axis=0, tiled=True),
        fc_weight,
        preferred_element_type=f32,
    )
    partial_value = lax.all_to_all(own_cols, "blk", split_axis=0, concat_axis=2, tiled=True)
    pre = lax.psum_scatter(partial_value, "feat", scatter_dimension=2, tiled=True)
    quarter = pre.shape[2]
    bias_part = lax.dynamic_slice_in_dim(fc_bias, feat_idx * quarter, quarter, 1)
    pre = pre + bias_part[None]
    live = (jnp.arange(num_rows) < jnp.sum(crop_counts)).astype(f32)
    stitched, pull_head = jax.vjp(stitch_head, pre, stitch_out)
    activations = (live[:, None, None] * stitched).astype(bf16)
    grad_out = live[:, None, None] * cotangent.astype(f32)
    grad_pre, grad_so = pull_head(grad_out)
    grad_low = grad_pre.astype(bf16)
    grad_all = lax.all_gather(grad_low, "feat", axis=2, tiled=True)
    bias_terms = jnp.sum(grad_all, axis=0, dtype=f32)
    grad_cols = lax.all_to_all(grad_all, "blk", split_axis=2, concat_axis=0, tiled=True)
    weight_grad = jnp.einsum(
        "rtf,rtn->tnf",
        lax.all_gather(feats, "blk", axis=0, tiled=True),
        grad_cols,
        preferred_element_type=f32,
    )
    grad_feats = jnp.einsum(
        "rtn,tnf->rtf",
        grad_all,
        lax.all_gather(fc_weight, "blk", axis=1, tiled=True),
        preferred_element_type=f32,
    )
    grad_mixed = grad_feats.reshape(num_rows, TOWERS, chans, -1)
    grad_pooled, grad_si = pull_first(grad_mixed)
    spread = jnp.einsum(
        "rtcq,pq->rpct", grad_pooled * (1.0 / 9.0), pool_table(f32), precision=lax.Precision.HIGHEST
    )
    conv_grad = spread.reshape(num_rows, MAP * MAP, merged).astype(bf16)
    stitch_in_grad, stitch_out_grad, bias_total = lax.psum((grad_si, grad_so, bias_terms), "blk")
    bias_grad = lax.dynamic_slice_in_dim(bias_total, blk_idx * cols, cols, 1)
    return (activations, conv_grad, weight_grad, bias_grad, stitch_in_grad, stitch_out_grad)


def ring_place(blk):
    z, x = lax.div(blk, 2), lax.rem(blk, 2)
    return z + x * (7 - 2 * z)


def ring_blk(place):
    x = lax.div(place, 4)
    return 2 * (place + x * (7 - 2 * place)) + x


def fc_kernel(
    steps,
    n_ref, so_ref, bias_ref, x_ref, first_ref, cot_ref, relay_ref, w_hbm,
    act_out, gf_out, wg_hbm, bg_out, sog_out,
    w, x, land, ring_tx, ex_tx, ex_rx, gp, part, held, sums,
    cot_rx, acts, act_tx, act_rx, sog_acc, sog_tx, sog_rx, wg_acc,
    kd, nn, start, tot, slot_rc, slot_live,
    w_sem, ag_ss, ag_rs, rs_ss, rs_rs, ex_ss, ex_rs, gp_ss, gp_rs,
    cot_ss, cot_rs, act_ss, act_rs, sog_ss, sog_rs, wg_sem, free,
):
    blk, feat = lax.axis_index("blk"), lax.axis_index("feat")
    place = ring_place(blk)
    ring_to = (ring_blk(lax.rem(place + 1, 8)), ring_blk(lax.rem(place + 7, 8)))
    ring_from = (lax.rem(place + 7, 8), lax.rem(place + 1, 8))
    per = 2 * SPAN
    groups = x.shape[0] - 8 // per
    slots = groups * SPAN
    sent = PIECES * (steps - 1)
    part_dim = x.shape[-1]
    units = w.shape[1]
    quarter = units // FEATS
    row_feat = lax.div(blk, 2)
    half_at = lax.rem(blk, 2) * FEATS + feat
    mine = row_feat == feat
    side = 2 * lax.div(feat, 2)
    cot_feat = side + lax.rem(row_feat, 2)
    cot_mine = cot_feat == feat

    w_copy = pltpu.make_async_copy(w_hbm, w, w_sem)
    w_copy.start()

    bar = pltpu.get_barrier_semaphore()

    def hello(dev):
        pl.semaphore_signal(bar, inc=1, device_id=dev, device_id_type=MESH)

    for d in (0, 1):
        hello((ring_to[d], feat))
    for o in range(1, FEATS):
        hello((blk, lax.rem(feat + o, FEATS)))

    def cot_to(s):
        owner = lax.rem(feat + 2 * lax.div(s, 4), FEATS)
        return 2 * owner + lax.rem(lax.div(s, 2), 2), side + lax.rem(s, 2)

    def cot_not_me(s):
        to = cot_to(s)
        return jnp.logical_or(to[0] != blk, to[1] != feat)

    def hello_far(s, carry):
        to = (2 * feat + lax.div(s, FEATS), lax.rem(s, FEATS))

        @pl.when(jnp.logical_or(to[0] != blk, to[1] != feat))
        def _():
            hello(to)

        @pl.when(jnp.logical_or(s != blk, row_feat != feat))
        def _():
            hello((s, row_feat))

        @pl.when(cot_not_me(s))
        def _():
            hello(cot_to(s))

        @pl.when(jnp.logical_or(s != blk, cot_feat != feat))
        def _():
            hello((s, cot_feat))

        return carry

    lax.fori_loop(0, 8, hello_far, 0)

    for d in (0, 1):
        for m in range(PIECES):
            land[d, m] = first_ref[d, m]

    def own_cot(s):
        return lax.div(s, 2) * FEATS + side + lax.rem(s, 2)

    def cot_copy(s, src):
        return pltpu.make_async_remote_copy(
            src_ref=src, dst_ref=cot_rx.at[blk], send_sem=cot_ss.at[s],
            recv_sem=cot_rs.at[blk], device_id=cot_to(s), device_id_type=MESH)

    def cot_wait(r):
        return pltpu.make_async_remote_copy(
            src_ref=cot_ref.at[0], dst_ref=cot_rx.at[r], send_sem=cot_ss.at[0],
            recv_sem=cot_rs.at[r], device_id=(r, cot_feat), device_id_type=MESH)

    def far_not_me(s):
        return jnp.logical_or(2 * feat + lax.div(s, FEATS) != blk, lax.rem(s, FEATS) != feat)

    def near_not_me(r):
        return jnp.logical_or(r != blk, row_feat != feat)

    for c in range(8):
        for t in range(TOWERS):
            for h in range(2):
                x[groups + c // per, t, h, c % per // SPAN, c % SPAN] = x_ref[
                    c, t, :, h * part_dim:(h + 1) * part_dim]

    run = jnp.int32(0)
    for q in range(PLACES):
        n = n_ref[RING_BLK[q]]
        k = jnp.clip(lax.div(n + (CHUNK - 1), CHUNK), 2, 8)
        first = lax.div(run + k + 1, 2) - lax.div(run + 1, 2)
        kd[q] = first
        kd[PLACES + q] = k - first
        nn[q] = n
        run = run + k

    def ring_unit_copy(d, m):
        return pltpu.make_async_remote_copy(
            src_ref=ring_tx.at[d, lax.rem(m, 8)], dst_ref=land.at[d, m],
            send_sem=ag_ss.at[d, lax.rem(m, 8)], recv_sem=ag_rs.at[d, m],
            device_id=(ring_to[d], feat), device_id_type=MESH)

    own_k = (kd[place], kd[PLACES + place])
    prev_k = tuple(kd[d * PLACES + ring_from[d]] for d in (0, 1))

    def chunk_of(d, c, first):
        return jnp.where(c == 0, d, (c + 1 if d == 0 else first + c))

    def own_piece(d, pos, t, h):
        c = chunk_of(d, pos, own_k[0])
        return x[groups + lax.div(c, per), t, h, lax.div(lax.rem(c, per), SPAN), lax.rem(c, SPAN)]

    def cot_send(s, carry):
        @pl.when(cot_not_me(s))
        def _():
            cot_copy(s, cot_ref.at[own_cot(s)]).start()

        @pl.when(jnp.logical_not(cot_not_me(s)))
        def _():
            cot_rx[blk] = cot_ref[own_cot(s)]

        @pl.when(cot_not_me(s + 4))
        def _():
            cot_copy(s + 4, relay_ref.at[s]).start()

        @pl.when(jnp.logical_not(cot_not_me(s + 4)))
        def _():
            cot_rx[blk] = relay_ref[s]

        return carry


    for d in (0, 1):
        run = jnp.int32(0)
        for h in range(1, PLACES + 1):
            at = lax.rem(place + (PLACES - h if d == 0 else h), PLACES)
            start[d * PLACES + at] = run
            run = run + kd[d * PLACES + at]
        tot[d] = run

        def fill(i, carry, d=d):
            h, c = carry
            hc = jnp.minimum(h, PLACES)
            at = lax.rem(place + (2 * PLACES - hc if d == 0 else hc), PLACES)
            chunk = jnp.minimum(chunk_of(d, c, kd[at]), 7)
            live = jnp.clip(nn[at] - CHUNK * chunk, 0, CHUNK)
            slot_rc[d * slots + i] = ring_blk(at) * 8 + chunk
            slot_live[d * slots + i] = jnp.where(h <= PLACES, live, 0)
            over = c + 1 >= kd[d * PLACES + at]
            return jnp.where(over, h + 1, h), jnp.where(over, 0, c + 1)

        lax.fori_loop(0, slots, fill, (jnp.int32(1), jnp.int32(0)))

    own_at = (tot[0] - own_k[0], tot[1] - own_k[1])
    held[...] = jnp.zeros_like(held)
    sog_acc[...] = jnp.zeros_like(sog_acc)
    pl.semaphore_wait(
        bar, jnp.where(mine, 2 + 3 + 14, 2 + 3 + 16) + jnp.where(cot_mine, 14, 16))
    lax.fori_loop(0, 4, cot_send, 0)

    def ex_copy(slot, g, o):
        to = lax.rem(feat + o, FEATS)
        return pltpu.make_async_remote_copy(
            src_ref=ex_tx.at[slot, to], dst_ref=ex_rx.at[g, feat], send_sem=ex_ss.at[slot, o - 1],
            recv_sem=ex_rs.at[g, feat], device_id=(blk, to), device_id_type=MESH)

    def ex_wait(g, o):
        src = lax.rem(feat + o, FEATS)
        return pltpu.make_async_remote_copy(
            src_ref=ex_tx.at[0, src], dst_ref=ex_rx.at[g, src], send_sem=ex_ss.at[0, o - 1],
            recv_sem=ex_rs.at[g, src], device_id=(blk, src), device_id_type=MESH)

    def gp_copy(g, o):
        to = lax.rem(feat + o, FEATS)
        return pltpu.make_async_remote_copy(
            src_ref=gp.at[g, feat], dst_ref=gp.at[g, feat], send_sem=gp_ss.at[g, o - 1],
            recv_sem=gp_rs.at[g, feat], device_id=(blk, to), device_id_type=MESH)

    def gp_wait(g, o):
        src = lax.rem(feat + o, FEATS)
        return pltpu.make_async_remote_copy(
            src_ref=gp.at[g, src], dst_ref=gp.at[g, src], send_sem=gp_ss.at[g, o - 1],
            recv_sem=gp_rs.at[g, src], device_id=(blk, src), device_id_type=MESH)

    def forward(g, t):
        slot = lax.rem(g, 2)

        @pl.when(jnp.logical_and(g >= 2, t == 0))
        def _():
            for o in range(1, FEATS):
                ex_copy(slot, g, o).wait_send()

        for n in range(2):
            out = sum(
                lax.dot_general(
                    x[g, t, h].reshape(per * CHUNK, part_dim),
                    w[t, 2 * n * quarter:2 * (n + 1) * quarter, h * part_dim:(h + 1) * part_dim],
                    (((1,), (1,)), ((), ())), preferred_element_type=f32)
                for h in range(2))
            for e in range(2):
                ex_tx[slot, 2 * n + e, t] = out[:, e * quarter:(e + 1) * quarter].reshape(
                    per, CHUNK, quarter)

        @pl.when(t == 1)
        def _():
            for o in range(1, FEATS):
                ex_copy(slot, g, o).start()
            ex_rx[g, feat] = ex_tx[slot, feat]

    bias_here = bias_ref[:, pl.ds(pl.multiple_of(blk * units + feat * quarter, quarter), quarter)]

    def head(g):
        for o in range(1, FEATS):
            ex_wait(g, o).wait_recv()

        def one(s, carry):
            d, ci = lax.div(s, SPAN), lax.rem(s, SPAN)
            i = g * SPAN + ci
            rc = slot_rc[d * slots + i]
            live = slot_live[d * slots + i]
            mask = jnp.where(
                lax.broadcasted_iota(i32, (CHUNK, quarter), 0) < live, f32(1), f32(0))
            act, slope, cot = [], [], []
            for t in range(TOWERS):
                pre = ex_rx[g, 0, t, s]
                for q in range(1, FEATS):
                    pre = pre + ex_rx[g, q, t, s]
                pre = pre + bias_here[t:t + 1]
                square = pre * pre
                th = jnp.tanh(f32(0.7978845608028654) * (pre + f32(0.044715) * (square * pre)))
                cdf = f32(0.5) * (f32(1) + th)
                act.append(pre * cdf)
                slope.append(cdf + f32(0.5) * pre * (f32(1) - th * th) * (
                    f32(0.7978845608028654) * (f32(1) + f32(3 * 0.044715) * square)))
                cot.append(cot_rx[lax.div(rc, 8), lax.rem(rc, 8), t].astype(f32) * mask)
            for t in range(TOWERS):
                out = so_ref[2 * t:2 * t + 1] * act[0] + so_ref[2 * t + 1:2 * t + 2] * act[1]
                acts[i, d, t] = (out * mask).astype(bf16)
                for u in range(TOWERS):
                    sog_acc[2 * t + u] = sog_acc[2 * t + u] + cot[t] * act[u]
            for u in range(TOWERS):
                back = so_ref[u:u + 1] * cot[0] + so_ref[2 + u:3 + u] * cot[1]
                gp[g, feat, u, s] = (slope[u] * back).astype(bf16)
            return carry

        lax.fori_loop(0, per, one, 0)
        for o in range(1, FEATS):
            gp_copy(g, o).start()

    tile = part_dim // 3

    def backward(g, t):
        rows = jnp.concatenate(
            [gp[g, q, t].reshape(per * CHUNK, quarter) for q in range(FEATS)], axis=1)
        for h in range(2):
            part[t, h] = jnp.dot(
                rows, w[t, :, h * part_dim:(h + 1) * part_dim],
                preferred_element_type=f32).reshape(per, CHUNK, part_dim)

    def tile_at(q):
        t, n = lax.div(q, 6), lax.rem(q, 6)
        return t, lax.div(n, 3), pl.multiple_of(n * tile, 128), pl.multiple_of(lax.rem(n, 3) * tile, 128)

    def wg_copy(q):
        t, _, whole_at, _ = tile_at(q)
        cols = pl.ds(whole_at, tile)
        return pltpu.make_async_copy(wg_acc.at[t, :, cols], wg_hbm.at[t, :, cols], wg_sem.at[q])

    def weight_tile(q, first, count):
        t, h, whole_at, part_at = tile_at(q)
        rows = x[first:first + count, t, h, :, :, :, pl.ds(part_at, tile)].reshape(
            count * per * CHUNK, tile)
        for e in range(FEATS):
            grads = gp[first:first + count, e, t].reshape(count * per * CHUNK, quarter)
            value = lax.dot_general(
                grads, rows, (((0,), (0,)), ((), ())), preferred_element_type=f32)
            at = (t, pl.ds(e * quarter, quarter), pl.ds(whole_at, tile))
            wg_acc[at] = value + wg_acc[at] if first else value

    def gather_unit(g, q):
        u = PIECES * SPAN * g + q
        ci, t, h = lax.div(q, PIECES), lax.rem(lax.div(q, 2), 2), lax.rem(q, 2)
        i = SPAN * g + ci
        for d in (0, 1):
            own = own_piece(d, jnp.clip(i - own_at[d], 0, own_k[d] - 1), t, h)

            @pl.when(u < sent)
            def _(d=d, own=own):
                @pl.when(u >= PIECES)
                def _():
                    ring_unit_copy(d, u).wait_recv()

                x[g, t, h, d, ci] = jnp.where(i >= own_at[d], own, land[d, u])

            @pl.when(u >= sent)
            def _(d=d, own=own):
                x[g, t, h, d, ci] = own

            m = u + PIECES

            @pl.when(m < sent)
            def _(d=d):
                @pl.when(m >= 8 + PIECES)
                def _():
                    ring_unit_copy(d, m).wait_send()

                here = i + 1 < own_k[d]
                c = chunk_of(d, jnp.minimum(i + 1, own_k[d] - 1), own_k[0])
                src = jnp.maximum(i + 1 - own_k[d], 0)
                ring_tx[d, lax.rem(m, 8)] = x[
                    jnp.where(here, groups + lax.div(c, per), lax.div(src, SPAN)), t, h,
                    jnp.where(here, lax.div(lax.rem(c, per), SPAN), d),
                    jnp.where(here, lax.rem(c, SPAN), lax.rem(src, SPAN))]
                ring_unit_copy(d, m).start()

    def sum_copy(d, v):
        return pltpu.make_async_remote_copy(
            src_ref=sums.at[d, v], dst_ref=land.at[d, v], send_sem=rs_ss.at[d, lax.rem(v, HELD)],
            recv_sem=rs_rs.at[d, v], device_id=(ring_to[d], feat), device_id_type=MESH)

    def sum_unit(g, q):
        v = PIECES * SPAN * g + q
        ci, t, h = lax.div(q, PIECES), lax.rem(lax.div(q, 2), 2), lax.rem(q, 2)
        before = v - PIECES
        for d in (0, 1):
            @pl.when(jnp.logical_and(before >= 0, before < sent))
            def _(d=d):
                sum_copy(d, before).wait_recv()
                held[d, lax.rem(before, HELD)] = land[d, before]

            came = held[d, lax.rem(v - PIECES * prev_k[d] + HELD, HELD)].astype(f32)
            value = part[t, h, d * SPAN + ci] + came * jnp.where(
                v >= PIECES * prev_k[d], f32(1), f32(0))
            sums[d, v] = value.astype(bf16)

            @pl.when(v < sent)
            def _(d=d):
                @pl.when(v >= HELD)
                def _():
                    sum_copy(d, v).wait_send()

                sum_copy(d, v).start()

    def act_copy(r):
        return pltpu.make_async_remote_copy(
            src_ref=act_tx.at[r], dst_ref=act_rx.at[half_at], send_sem=act_ss.at[r],
            recv_sem=act_rs.at[half_at], device_id=(r, row_feat), device_id_type=MESH)

    def act_wait(s):
        return pltpu.make_async_remote_copy(
            src_ref=act_tx.at[0], dst_ref=act_rx.at[s], send_sem=act_ss.at[0],
            recv_sem=act_rs.at[s], device_id=(blk, feat), device_id_type=MESH)

    def sog_copy(r):
        return pltpu.make_async_remote_copy(
            src_ref=sog_tx, dst_ref=sog_rx.at[half_at], send_sem=sog_ss.at[r],
            recv_sem=sog_rs.at[half_at], device_id=(r, row_feat), device_id_type=MESH)

    def sog_wait(s):
        return pltpu.make_async_remote_copy(
            src_ref=sog_tx, dst_ref=sog_rx.at[s], send_sem=sog_ss.at[0],
            recv_sem=sog_rs.at[s], device_id=(blk, feat), device_id_type=MESH)

    def send_acts(r):
        at = ring_place(r)
        first, second = kd[at], kd[PLACES + at]
        for c in range(8):
            late = c > first
            d = jnp.where(late, 1, 0) if c > 1 else c
            pos = jnp.where(late, c - first, c - 1) if c > 1 else 0
            i = jnp.minimum(start[d * PLACES + at] + pos, slots - 1)
            keep = jnp.where(c < first + second, f32(1), f32(0))
            for t in range(TOWERS):
                act_tx[r, c, t] = (acts[i, d, t].astype(f32) * keep).astype(bf16)

        @pl.when(near_not_me(r))
        def _():
            act_copy(r).start()
            sog_copy(r).start()

        @pl.when(jnp.logical_not(near_not_me(r)))
        def _():
            act_rx[half_at] = act_tx[r]
            sog_rx[half_at] = sog_tx[...]

    def add_bias():
        for e in range(FEATS):
            for t in range(TOWERS):
                def add(g, total, e=e, t=t):
                    return total + jnp.sum(gp[g, e, t].astype(f32), axis=0)

                total = lax.fori_loop(0, groups, add, jnp.zeros((CHUNK, quarter), f32))
                bg_out[t:t + 1, e * quarter:(e + 1) * quarter] = jnp.sum(
                    total, axis=0, keepdims=True)

    early = groups - 2

    def iteration(it, carry):
        @pl.when(it >= 3)
        def _():
            for o in range(1, FEATS):
                gp_wait(it - 3, o).wait_recv()
            backward(it - 3, 0)

        @pl.when(it == 1)
        def _():
            w_copy.wait()

        @pl.when(it == 2)
        def _():
            def arrived(r, carry):
                @pl.when(jnp.logical_or(r != blk, cot_feat != feat))
                def _():
                    cot_wait(r).wait_recv()

                return carry

            lax.fori_loop(0, PLACES, arrived, 0)

        @pl.when(jnp.logical_and(it >= 2, it < groups + 2))
        def _():
            head(it - 2)

        @pl.when(it == groups + 1)
        def _():
            sog_tx[...] = jnp.concatenate(
                [jnp.sum(sog_acc[e], axis=0, keepdims=True) for e in range(4)] * 2, axis=0)

        @pl.when(it >= 3)
        def _():
            for d in (0, 1):
                pl.semaphore_wait(free.at[d], 1)

        def unit(q, carry):
            @pl.when(it < groups)
            def _():
                gather_unit(it, q)

            @pl.when(it >= 3)
            def _():
                sum_unit(it - 3, q)

            @pl.when(jnp.logical_and(
                lax.rem(q, 2) == 0, jnp.logical_and(q < 4, jnp.logical_and(it >= 1, it < groups + 1))))
            def _():
                forward(it - 1, lax.div(q, 2))

            @pl.when(jnp.logical_and(it >= 3, q == 1))
            def _():
                backward(it - 3, 1)

            @pl.when(it == groups + 1)
            def _():
                send_acts(q)

            @pl.when(jnp.logical_and(it == groups + 2, q == 3))
            def _():
                add_bias()

            @pl.when(jnp.logical_and(jnp.logical_or(it == groups, it == groups + 1), q < 6))
            def _():
                weight_tile(q + 6 * (it - groups), 0, early)

            @pl.when(jnp.logical_and(it == groups + 2, q < 6))
            def _():
                def last(e, carry):
                    weight_tile(2 * q + e, early, 2)
                    wg_copy(2 * q + e).start()
                    return carry

                lax.fori_loop(0, 2, last, 0)

            return carry

        lax.fori_loop(0, PIECES * SPAN, unit, 0)

        @pl.when(it < groups)
        def _():
            for d in (0, 1):
                pl.semaphore_signal(
                    free.at[d], inc=1, device_id=(ring_blk(ring_from[d]), feat), device_id_type=MESH)

        return carry

    lax.fori_loop(0, groups + 3, iteration, 0)

    for c in range(8):
        late = c > own_k[0]
        d = jnp.where(late, 1, 0) if c > 1 else c
        i = jnp.where(late, own_at[1] + c - own_k[0], own_at[0] + c - 1) if c > 1 else own_at[c]
        i = jnp.clip(i, 0, slots - 1)
        keep = jnp.where(c < own_k[0] + own_k[1], f32(1), f32(0))
        for t in range(TOWERS):
            for h in range(2):
                gf_out[c, t, :, h * part_dim:(h + 1) * part_dim] = (
                    sums[d, PIECES * i + 2 * t + h].astype(f32) * keep).astype(bf16)

    def finish(s, carry):
        @pl.when(far_not_me(s))
        def _():
            act_wait(s).wait_recv()
            sog_wait(s).wait_recv()

        @pl.when(cot_not_me(s))
        def _():
            cot_copy(s, cot_ref.at[0]).wait_send()

        @pl.when(near_not_me(s))
        def _():
            act_copy(s).wait_send()
            sog_copy(s).wait_send()

        return carry

    lax.fori_loop(0, 8, finish, 0)
    act_out[...] = act_rx[...]
    sog_out[...] = sog_rx[...]

    def finish_sums(v, carry):
        for d in (0, 1):
            sum_copy(d, v).wait_send()
        return carry

    lax.fori_loop(sent - HELD, sent, finish_sums, 0)
    for m in range(sent - 8, sent):
        for d in (0, 1):
            ring_unit_copy(d, jnp.int32(m)).wait_send()
    for o in range(1, FEATS):
        for g in (groups - 2, groups - 1):
            ex_copy(g % 2, g, o).wait_send()

        def finish_gp(g, carry, o=o):
            gp_copy(g, o).wait_send()
            return carry

        lax.fori_loop(0, groups, finish_gp, 0)
    for q in range(12):
        wg_copy(jnp.int32(q)).wait()


def fc_layer(steps, number, n, so, bias, x, first, cot, relay, weight):
    units, feats_dim = weight.shape[1:]
    quarter = units // FEATS
    groups = -(-steps // SPAN)
    slots = groups * SPAN
    vm = pltpu.VMEM
    dma = pltpu.SemaphoreType.DMA
    sm = pltpu.SMEM
    unit = (CHUNK, feats_dim // 2)
    vmem_spec = pl.BlockSpec(memory_space=pltpu.VMEM)
    any_spec = pl.BlockSpec(memory_space=pl.ANY)
    rows = 2 * slots * CHUNK
    return pl.pallas_call(
        functools.partial(fc_kernel, steps),
        out_shape=(
            jax.ShapeDtypeStruct((8, 8, TOWERS, CHUNK, quarter), bf16),
            jax.ShapeDtypeStruct((8, TOWERS, CHUNK, feats_dim), bf16),
            jax.ShapeDtypeStruct(weight.shape, f32),
            jax.ShapeDtypeStruct((TOWERS, units), f32),
            jax.ShapeDtypeStruct((8, 8, quarter), f32),
        ),
        in_specs=[pl.BlockSpec(memory_space=pltpu.SMEM)] + [vmem_spec] * 6 + [any_spec],
        out_specs=(vmem_spec, vmem_spec, any_spec, vmem_spec, vmem_spec),
        scratch_shapes=[
            vm(weight.shape, bf16),
            vm((groups + 8 // (2 * SPAN), TOWERS, 2, 2, SPAN) + unit, bf16),
            vm((2, PIECES * (steps - 1)) + unit, bf16),
            vm((2, 8) + unit, bf16),
            vm((2, FEATS, TOWERS, 2 * SPAN, CHUNK, quarter), f32),
            vm((groups, FEATS, TOWERS, 2 * SPAN, CHUNK, quarter), f32),
            vm((groups, FEATS, TOWERS, 2 * SPAN, CHUNK, quarter), bf16),
            vm((TOWERS, 2, 2 * SPAN) + unit, f32),
            vm((2, HELD) + unit, bf16),
            vm((2, PIECES * slots) + unit, bf16),
            vm((8, 8, TOWERS, CHUNK, quarter), bf16),
            vm((slots, 2, TOWERS, CHUNK, quarter), bf16),
            vm((8, 8, TOWERS, CHUNK, quarter), bf16),
            vm((8, 8, TOWERS, CHUNK, quarter), bf16),
            vm((4, CHUNK, quarter), f32),
            vm((8, quarter), f32),
            vm((8, 8, quarter), f32),
            vm(weight.shape, f32),
            sm((2 * PLACES,), i32),
            sm((PLACES,), i32),
            sm((2 * PLACES,), i32),
            sm((2,), i32),
            sm((2 * slots,), i32),
            sm((2 * slots,), i32),
            dma,
            dma((2, 8)),
            dma((2, PIECES * (steps - 1))),
            dma((2, HELD)),
            dma((2, PIECES * (steps - 1))),
            dma((2, 3)),
            dma((groups, FEATS)),
            dma((groups, 3)),
            dma((groups, FEATS)),
            dma((8,)),
            dma((8,)),
            dma((8,)),
            dma((8,)),
            dma((8,)),
            dma((8,)),
            dma((12,)),
            pltpu.SemaphoreType.REGULAR((2,)),
        ],
        cost_estimate=pl.CostEstimate(
            flops=6 * rows * TOWERS * units * feats_dim, bytes_accessed=30 << 20,
            transcendentals=rows * TOWERS * quarter),
        compiler_params=pltpu.CompilerParams(
            collective_id=number, has_side_effects=True, vmem_limit_bytes=60 << 20),
    )(n, so, bias, x, first, cot, relay, weight)


def layout_matrix(chans):
    table = np.zeros((4 * 2 * chans, 4 * 2 * chans), np.float32)
    for q0 in range(4):
        for c in range(chans):
            for t in range(TOWERS):
                lane = 4 * ((9 * c) % 32) + q0
                table[q0 * 2 * chans + 2 * c + t, (2 * t + c // 32) * 128 + lane] = 1
    return table


def lane_sources():
    slot = np.arange(128) // 4
    rows = [(slot + 32 * j) % 9 for j in range(9)] + [(2 * (q1 - slot)) % 9 for q1 in range(9)]
    return np.broadcast_to(np.stack(rows)[:, None, :], (18, CHUNK, 128)).astype(np.int32)


def lane_pairs(chans):
    shape = (chans, TOWERS * chans)
    lane, chan = lax.broadcasted_iota(i32, shape, 1), lax.broadcasted_iota(i32, shape, 0)
    return tuple((lane == 2 * chan + t).astype(f32) for t in range(TOWERS))


def exact_dot(a, b, dims):
    return lax.dot_general(
        a, b, (dims, ((), ())), precision=lax.Precision.HIGHEST, preferred_element_type=f32)


def pair_swap():
    even = (lax.broadcasted_iota(i32, (CHUNK, 128), 1) & 1) == 0

    def swap(value):
        return jnp.where(even, pltpu.roll(value, 127, 1), pltpu.roll(value, 1, 1))

    return swap


BATCH = 2
LAST = 4
STEPS = 2
WAYS = 4


def entry_kernel(
    cc_ref, so_ref, si_ref, perm_ref, source_ref, cot_ref, conv_ref,
    feats_out, pooled_out, n_out, pick_out, so_out, relay_out, first_out, s_out,
    n_tx, n_rx, so_tx, so_rx, relay_rx, first_tx, first_rx, s_ref,
    n_ss, n_rs, so_ss, so_rs, relay_ss, relay_rs, first_ss, first_rs,
):
    blk, feat = lax.axis_index("blk"), lax.axis_index("feat")
    step = pl.program_id(0)
    holds = lax.div(blk, 2) == feat

    def n_copy(o):
        to = lax.rem(blk + o, PLACES)
        return pltpu.make_async_remote_copy(
            src_ref=n_tx, dst_ref=n_rx.at[blk], send_sem=n_ss.at[o - 1], recv_sem=n_rs.at[blk],
            device_id=(to, feat), device_id_type=MESH)

    def n_wait(o):
        src = lax.rem(blk + o, PLACES)
        return pltpu.make_async_remote_copy(
            src_ref=n_tx, dst_ref=n_rx.at[src], send_sem=n_ss.at[o - 1], recv_sem=n_rs.at[src],
            device_id=(src, feat), device_id_type=MESH)

    def so_copy(o):
        to = lax.rem(feat + o, FEATS)
        return pltpu.make_async_remote_copy(
            src_ref=so_tx.at[to], dst_ref=so_rx, send_sem=so_ss.at[o - 1], recv_sem=so_rs,
            device_id=(blk, to), device_id_type=MESH)

    across_y = lax.rem(feat + 2, FEATS)
    place = ring_place(blk)
    half = feats_out.shape[-1] // 2

    def first_copy(d, m):
        return pltpu.make_async_remote_copy(
            src_ref=first_tx.at[d, m], dst_ref=first_rx.at[d, m], send_sem=first_ss.at[d, m],
            recv_sem=first_rs.at[d, m],
            device_id=(ring_blk(lax.rem(place + (7 if d else 1), 8)), feat), device_id_type=MESH)

    def relay_copy(s):
        return pltpu.make_async_remote_copy(
            src_ref=cot_ref.at[s // 2 * FEATS + 2 * lax.div(across_y, 2) + s % 2],
            dst_ref=relay_rx.at[s], send_sem=relay_ss.at[s], recv_sem=relay_rs.at[s],
            device_id=(blk, across_y), device_id_type=MESH)

    @pl.when(step == 0)
    def _():
        bar = pltpu.get_barrier_semaphore()
        for o in range(1, PLACES):
            pl.semaphore_signal(
                bar, inc=1, device_id=(lax.rem(blk + o, PLACES), feat), device_id_type=MESH)
        for o in range(1, FEATS):
            pl.semaphore_signal(
                bar, inc=1, device_id=(blk, lax.rem(feat + o, FEATS)), device_id_type=MESH)
        total = cc_ref[0]
        for e in range(1, cc_ref.shape[0]):
            total = total + cc_ref[e]
        n_tx[...] = jnp.full(n_tx.shape, total, i32)
        n_rx[blk] = n_tx[...]
        for q in range(FEATS):
            at = pl.ds(pl.multiple_of(lax.rem(blk, 2) * 512 + q * 128, 128), 128)
            for t in range(TOWERS):
                so_tx[q, 2 * t:2 * t + 2] = so_ref[t, :, at]
                so_tx[q, 4 + 2 * t:6 + 2 * t] = so_ref[t, :, at]
        even, odd = lane_pairs(si_ref.shape[-1])
        rows = [[exact_dot(si_ref[t], v, ((1,), (0,))) for v in (even, odd)] for t in range(TOWERS)]
        s_ref[0:1] = rows[0][0][0:1] + rows[1][1][1:2]
        s_ref[1:2] = rows[0][0][1:2] + rows[1][1][0:1]
        s_ref[2:3] = rows[1][0][0:1] + rows[0][1][1:2]
        s_ref[3:8] = jnp.zeros((5, s_ref.shape[1]), f32)
        pl.semaphore_wait(bar, PLACES - 1 + FEATS - 1)
        for o in range(1, PLACES):
            n_copy(o).start()
        for s in range(4):
            relay_copy(s).start()

        @pl.when(holds)
        def _():
            so_rx[...] = so_tx[feat]
            for o in range(1, FEATS):
                so_copy(o).start()

    def chunk(e, carry):
        swap = pair_swap()
        at_row = pl.ds(pl.multiple_of(e * CHUNK, CHUNK), CHUNK)
        across = {}
        for row in range(MAP):
            line = [conv_ref[MAP * row + col, at_row].astype(f32) for col in range(MAP)]
            for v in range(GRID):
                across[row, v] = line[2 * v] + line[2 * v + 1] + line[2 * v + 2]
        own, other = s_ref[0:1], s_ref[1:2]
        parts = []
        for q1 in range(9):
            here = []
            for q0 in range(4):
                q = 4 * q1 + q0
                u, v = q // GRID, q % GRID
                pooled = (across[2 * u, v] + across[2 * u + 1, v] + across[2 * u + 2, v]) * f32(1 / 9)
                pooled_out[e, q] = pooled
                here.append((own * pooled + other * swap(pooled)).astype(bf16))
            parts.append(jnp.concatenate(here, axis=1))
        spread = jnp.dot(
            jnp.concatenate(parts, axis=0), perm_ref[...], preferred_element_type=f32)
        turned = [
            pltpu.roll(spread[q1 * CHUNK:(q1 + 1) * CHUNK, at:at + 128], 4 * q1, 1)
            if q1 else spread[0:CHUNK, at:at + 128] for q1 in range(9) for at in range(0, 512, 128)]
        for j in range(9):
            source = source_ref[j]
            tiles = turned[0:4]
            for q1 in range(1, 9):
                here = source == q1
                tiles = [jnp.where(here, turned[4 * q1 + k], tiles[k]) for k in range(4)]
            for k in range(4):
                n = 9 * (k % 2) + j
                feats_out[e, k // 2, :, n * 128:(n + 1) * 128] = tiles[k].astype(bf16)
        return carry

    lax.fori_loop(0, BATCH, chunk, 0)

    @pl.when(step == 0)
    def _():
        for m in range(PIECES):
            for d in range(2):
                first_tx[d, m] = feats_out[d, m // 2, :, m % 2 * half:(m % 2 + 1) * half]
                first_copy(d, m).start()

    @pl.when(step == pl.num_programs(0) - 1)
    def _():
        for m in range(PIECES):
            for d in range(2):
                first_copy(d, m).wait()
        first_out[...] = first_rx[...]
        s_out[...] = s_ref[...]
        for o in range(1, PLACES):
            n_wait(o).wait_recv()
            n_copy(o).wait_send()

        @pl.when(holds)
        def _():
            for o in range(1, FEATS):
                so_copy(o).wait_send()

        @pl.when(jnp.logical_not(holds))
        def _():
            so_copy(1).wait_recv()

        for s in range(4):
            relay_copy(s).wait()
        chunks = jnp.int32(0)
        for q in range(PLACES):
            n = jnp.max(n_rx[q])
            n_out[q] = n
            chunks = chunks + lax.div(n + (CHUNK - 1), CHUNK)
        need = lax.div(chunks + 1, 2)
        pick_out[0] = sum(((need > c).astype(i32) for c in CLASSES), jnp.int32(0))
        so_out[...] = so_rx[...]
        relay_out[...] = relay_rx[...]


def exit_kernel(
    s_ref, perm_ref, source_ref, bg_ref, sog_ref, gf_ref, pooled_ref, wg_ref,
    conv_out, si_out, bg_out, sog_out, wg_out, acc, wg, wg_in, wg_back,
):
    step = pl.program_id(0)

    size = wg.shape[1] // WAYS

    def wg_read(e):
        at = pl.ds(e * size, size)
        return pltpu.make_async_copy(wg_ref.at[:, at], wg.at[:, at], wg_in.at[e])

    def wg_write(e):
        at = pl.ds(e * size, size)
        return pltpu.make_async_copy(wg.at[:, at], wg_out.at[:, at], wg_back.at[e])

    @pl.when(step == 0)
    def _():
        acc[...] = jnp.zeros_like(acc)
        for e in range(WAYS):
            wg_read(e).start()
    def chunk(e, carry):
        swap = pair_swap()
        at_row = pl.ds(pl.multiple_of(e * CHUNK, CHUNK), CHUNK)
        tiles = [
            gf_ref[e, k // 2, :, (9 * (k % 2) + j) * 128:(9 * (k % 2) + j + 1) * 128].astype(f32)
            for j in range(9) for k in range(4)]
        rows = []
        for q1 in range(9):
            source = source_ref[9 + q1]
            here = tiles[0:4]
            for j in range(1, 9):
                mask = source == j
                here = [jnp.where(mask, tiles[4 * j + k], here[k]) for k in range(4)]
            rows.append(jnp.concatenate(
                [pltpu.roll(v, 128 - 4 * q1, 1) if q1 else v for v in here], axis=1).astype(bf16))
        grads = lax.dot_general(
            jnp.concatenate(rows, axis=0), perm_ref[...], (((1,), (1,)), ((), ())),
            preferred_element_type=f32)
        own, other = s_ref[0:1] * f32(1 / 9), s_ref[2:3] * f32(1 / 9)
        same = acc[0]
        cross = acc[1]
        back = {}
        for q in range(GRID * GRID):
            q1, q0 = q // 4, q % 4
            grad = grads[q1 * CHUNK:(q1 + 1) * CHUNK, q0 * 128:(q0 + 1) * 128]
            pooled = pooled_ref[e, q]
            swapped = swap(grad)
            same = same + grad * pooled
            cross = cross + swapped * pooled
            back[q // GRID, q % GRID] = own * grad + other * swapped
        acc[0] = same
        acc[1] = cross
        lines = []
        for u in range(GRID):
            line = []
            for col in range(MAP):
                v = col // 2
                if col % 2:
                    line.append(back[u, v])
                elif col == 0:
                    line.append(back[u, 0])
                elif col == MAP - 1:
                    line.append(back[u, GRID - 1])
                else:
                    line.append(back[u, v - 1] + back[u, v])
            lines.append(line)
        for row in range(MAP):
            u = row // 2
            for col in range(MAP):
                if row % 2 or row == 0:
                    value = lines[u][col]
                elif row == MAP - 1:
                    value = lines[GRID - 1][col]
                else:
                    value = lines[u - 1][col] + lines[u][col]
                conv_out[MAP * row + col, at_row] = value.astype(bf16)
        return carry

    lax.fori_loop(0, LAST, chunk, 0)

    for n in range(STEPS):
        @pl.when(step == n)
        def _(n=n):
            for e in range(WAYS * n // STEPS, WAYS * (n + 1) // STEPS):
                wg_read(e).wait()
                wg_write(e).start()

    @pl.when(step == pl.num_programs(0) - 1)
    def _():
        sums = jnp.concatenate(
            [jnp.sum(acc[e], axis=0, keepdims=True) for e in range(2)] * 4, axis=0)
        chans = sums.shape[1] // TOWERS
        even, odd = (exact_dot(sums, v, ((1,), (1,))) for v in lane_pairs(chans))
        si_out[...] = jnp.zeros_like(si_out)
        si_out[0:1, 0:chans] = even[0:1]
        si_out[1:2, 0:chans] = odd[1:2]
        si_out[2:3, 0:chans] = even[1:2]
        si_out[3:4, 0:chans] = odd[0:1]
        bg_out[...] = bg_ref[...]
        for e in range(8):
            for t in range(TOWERS):
                sog_out[t, :, e * 128:(e + 1) * 128] = sog_ref[e, TOWERS * t:TOWERS * (t + 1)]
        for e in range(WAYS):
            wg_write(e).wait()


def total_kernel(x_ref, out, rx, ss, rs):
    blk, feat = lax.axis_index("blk"), lax.axis_index("feat")

    def copy(o):
        return pltpu.make_async_remote_copy(
            src_ref=x_ref, dst_ref=rx.at[blk], send_sem=ss.at[o - 1], recv_sem=rs.at[blk],
            device_id=(lax.rem(blk + o, PLACES), feat), device_id_type=MESH)

    def wait(o):
        src = lax.rem(blk + o, PLACES)
        return pltpu.make_async_remote_copy(
            src_ref=x_ref, dst_ref=rx.at[src], send_sem=ss.at[o - 1], recv_sem=rs.at[src],
            device_id=(src, feat), device_id_type=MESH)

    bar = pltpu.get_barrier_semaphore()
    for o in range(1, PLACES):
        pl.semaphore_signal(
            bar, inc=1, device_id=(lax.rem(blk + o, PLACES), feat), device_id_type=MESH)
    pl.semaphore_wait(bar, PLACES - 1)
    for o in range(1, PLACES):
        copy(o).start()
    rx[blk] = x_ref[...]
    for o in range(1, PLACES):
        wait(o).wait_recv()
    total = rx[0]
    for q in range(1, PLACES):
        total = total + rx[q]
    for t in range(TOWERS):
        out[t] = total[TOWERS * t:TOWERS * (t + 1), 0:out.shape[-1]]
    for o in range(1, PLACES):
        copy(o).wait_send()


def entry(counts, so, stitch, cot, conv):
    spots, rows, merged = conv.shape
    chunks = rows // CHUNK
    chans = merged // TOWERS
    wide = chans * GRID * GRID
    vm, dma = pltpu.VMEM, pltpu.SemaphoreType.DMA
    whole = pl.BlockSpec(memory_space=pltpu.VMEM)
    scalars = pl.BlockSpec(memory_space=pltpu.SMEM)
    return pl.pallas_call(
        entry_kernel,
        grid=(chunks // BATCH,),
        out_shape=(
            jax.ShapeDtypeStruct((chunks, TOWERS, CHUNK, wide), bf16),
            jax.ShapeDtypeStruct((chunks, GRID * GRID, CHUNK, merged), f32),
            jax.ShapeDtypeStruct((PLACES,), i32),
            jax.ShapeDtypeStruct((1,), i32),
            jax.ShapeDtypeStruct((8, 128), f32),
            jax.ShapeDtypeStruct((4,) + cot.shape[1:], bf16),
            jax.ShapeDtypeStruct((2, PIECES, CHUNK, wide // 2), bf16),
            jax.ShapeDtypeStruct((8, merged), f32),
        ),
        in_specs=[scalars] + [whole] * 5 + [
            pl.BlockSpec((spots, BATCH * CHUNK, merged), lambda c: (0, c, 0))],
        out_specs=(
            pl.BlockSpec((BATCH, TOWERS, CHUNK, wide), lambda c: (c, 0, 0, 0)),
            pl.BlockSpec((BATCH, GRID * GRID, CHUNK, merged), lambda c: (c, 0, 0, 0)),
            scalars, scalars, whole, whole, whole, whole,
        ),
        scratch_shapes=[
            vm((8, 128), i32), vm((PLACES, 8, 128), i32), vm((FEATS, 8, 128), f32), vm((8, 128), f32),
            vm((4,) + cot.shape[1:], bf16), vm((2, PIECES, CHUNK, wide // 2), bf16),
            vm((2, PIECES, CHUNK, wide // 2), bf16), vm((8, merged), f32),
            dma((PLACES - 1,)), dma((PLACES,)), dma((FEATS - 1,)), dma, dma((4,)), dma((4,)),
            dma((2, PIECES)), dma((2, PIECES)),
        ],
        cost_estimate=pl.CostEstimate(flops=1 << 30, bytes_accessed=10 << 20, transcendentals=0),
        compiler_params=pltpu.CompilerParams(
            collective_id=20, has_side_effects=True, vmem_limit_bytes=60 << 20),
    )(counts, so, stitch, jnp.asarray(layout_matrix(chans), bf16), jnp.asarray(lane_sources()), cot, conv)


def leave(s_rows, bias_grad, sog, gf, pooled, weight_grad, spots):
    chunks, towers, _, wide = gf.shape
    merged = pooled.shape[-1]
    vm = pltpu.VMEM
    whole = pl.BlockSpec(memory_space=pltpu.VMEM)
    share = pl.BlockSpec(memory_space=pl.ANY)
    return pl.pallas_call(
        exit_kernel,
        grid=(chunks // LAST,),
        out_shape=(
            jax.ShapeDtypeStruct((spots, chunks * CHUNK, merged), bf16),
            jax.ShapeDtypeStruct((8, 128), f32),
            jax.ShapeDtypeStruct(bias_grad.shape, f32),
            jax.ShapeDtypeStruct((TOWERS, TOWERS, 8 * sog.shape[-1]), f32),
            jax.ShapeDtypeStruct(weight_grad.shape, f32),
        ),
        in_specs=[whole] * 5 + [
            pl.BlockSpec((LAST, towers, CHUNK, wide), lambda c: (c, 0, 0, 0)),
            pl.BlockSpec((LAST, GRID * GRID, CHUNK, merged), lambda c: (c, 0, 0, 0)),
            share],
        out_specs=(
            pl.BlockSpec((spots, LAST * CHUNK, merged), lambda c: (0, c, 0)),
            whole, whole, whole, share,
        ),
        scratch_shapes=[
            vm((2, CHUNK, 128), f32), vm(weight_grad.shape, f32),
            pltpu.SemaphoreType.DMA((WAYS,)), pltpu.SemaphoreType.DMA((WAYS,))],
        cost_estimate=pl.CostEstimate(flops=1 << 30, bytes_accessed=30 << 20, transcendentals=0),
        compiler_params=pltpu.CompilerParams(vmem_limit_bytes=60 << 20),
    )(s_rows, jnp.asarray(layout_matrix(merged // TOWERS), bf16),
      jnp.asarray(lane_sources()), bias_grad, sog, gf, pooled, weight_grad)


def total_over_blk(value):
    whole = pl.BlockSpec(memory_space=pltpu.VMEM)
    dma = pltpu.SemaphoreType.DMA
    return pl.pallas_call(
        total_kernel,
        out_shape=jax.ShapeDtypeStruct((TOWERS, TOWERS, value.shape[1] // TOWERS), f32),
        in_specs=[whole],
        out_specs=whole,
        scratch_shapes=[
            pltpu.VMEM((PLACES,) + value.shape, f32), dma((PLACES - 1,)), dma((PLACES,))],
        compiler_params=pltpu.CompilerParams(
            collective_id=21, has_side_effects=True, vmem_limit_bytes=16 << 20),
    )(value)


def body_ring(conv_maps, crop_counts, fc_weight, fc_bias, stitch_in, stitch_out, cotangent):
    num_rows = conv_maps.shape[0]
    units = fc_weight.shape[1]
    quarter = units // FEATS
    chunks = num_rows // CHUNK
    cot = cotangent.reshape(chunks, CHUNK, TOWERS, 8, quarter).transpose(3, 0, 2, 1, 4)
    feats, pooled, n, pick, so, relay, first, s_rows = entry(
        crop_counts, stitch_out, stitch_in, cot, conv_maps.transpose(1, 0, 2))
    full = PLACES * chunks // 2
    kinds = CLASSES + (full,)
    act, gf, weight_grad, bias_grad, sog = lax.switch(
        pick[0],
        [functools.partial(fc_layer, steps, at) for at, steps in enumerate(kinds)],
        n, so, fc_bias, feats, first, cot, relay, fc_weight)
    activations = act.transpose(1, 3, 2, 0, 4).reshape(num_rows, TOWERS, -1)
    conv_grad, si, bias_grad, stitch_out_grad, weight_grad = leave(
        s_rows, bias_grad, sog, gf, pooled, weight_grad, conv_maps.shape[1])
    conv_grad = conv_grad.transpose(1, 0, 2)
    stitch_in_grad = total_over_blk(si)
    return (activations, conv_grad, weight_grad, bias_grad, stitch_in_grad, stitch_out_grad)


def solution(mesh):
    ring = mesh.shape["blk"] == PLACES and mesh.shape["feat"] == FEATS
    return jax.shard_map(
        body_ring if ring else body_plain,
        mesh=mesh,
        in_specs=(
            P("blk", None, "feat"),
            P("blk"),
            P(None, "blk", "feat"),
            P(),
            P(None, None, "feat"),
            P(None, None, "feat"),
            P("blk", None, "feat"),
        ),
        out_specs=(
            P("blk", None, "feat"),
            P("blk", None, "feat"),
            P(None, "blk", "feat"),
            P(None, "blk"),
            P(None, None, "feat"),
            P(None, None, "feat"),
        ),
        check_vma=False,
    )
```

```python
import functools

import jax
import jax.numpy as jnp
import numpy as np
from jax import lax
from jax.experimental import pallas as pl
from jax.experimental.pallas import tpu as pltpu
from jax.sharding import PartitionSpec as P

MAP = 13
GRID = 6
TOWERS = 2
CHUNK = 16
CLASSES = (18, 19, 20, 21, 22, 23)
SPAN = 2
PIECES = 4
HELD = 16
PLACES = 8
FEATS = 4
RING_BLK = (0, 2, 4, 6, 7, 5, 3, 1)
MESH = pl.DeviceIdType.MESH
f32 = jnp.float32
bf16 = jnp.bfloat16
i32 = jnp.int32


def pool_table(dtype):
    position = jnp.arange(MAP * MAP)
    row_pos = position // MAP
    col_pos = position % MAP
    cell = jnp.arange(GRID * GRID)
    row_cell = cell // GRID
    col_cell = cell % GRID
    down = row_pos[:, None] - 2 * row_cell[None, :]
    across = col_pos[:, None] - 2 * col_cell[None, :]
    inside = (down >= 0) & (down < 3) & (across >= 0) & (across < 3)
    return inside.astype(dtype)


def stitch_first(pooled, stitch_in):
    return jnp.einsum("tuc,rucq->rtcq", stitch_in, pooled, precision=lax.Precision.HIGHEST)


def stitch_head(pre, stitch_out):
    act = jax.nn.gelu(pre)
    return jnp.einsum("tuk,ruk->rtk", stitch_out, act, precision=lax.Precision.HIGHEST)


def body_plain(conv_maps, crop_counts, fc_weight, fc_bias, stitch_in, stitch_out, cotangent):
    num_rows = conv_maps.shape[0]
    merged = conv_maps.shape[2]
    chans = merged // TOWERS
    cols = fc_weight.shape[1]
    feat_idx = lax.axis_index("feat")
    blk_idx = lax.axis_index("blk")
    sums = jnp.einsum("rpm,pq->rqm", conv_maps, pool_table(bf16), preferred_element_type=f32)
    pooled = jnp.transpose(sums.reshape(num_rows, GRID * GRID, chans, TOWERS), (0, 3, 2, 1)) * (
        1.0 / 9.0
    )
    mixed, pull_first = jax.vjp(stitch_first, pooled, stitch_in)
    feats = mixed.astype(bf16).reshape(num_rows, TOWERS, -1)
    own_cols = jnp.einsum(
        "rtf,tnf->rtn",
        lax.all_gather(feats, "blk", axis=0, tiled=True),
        fc_weight,
        preferred_element_type=f32,
    )
    partial_value = lax.all_to_all(own_cols, "blk", split_axis=0, concat_axis=2, tiled=True)
    pre = lax.psum_scatter(partial_value, "feat", scatter_dimension=2, tiled=True)
    quarter = pre.shape[2]
    bias_part = lax.dynamic_slice_in_dim(fc_bias, feat_idx * quarter, quarter, 1)
    pre = pre + bias_part[None]
    live = (jnp.arange(num_rows) < jnp.sum(crop_counts)).astype(f32)
    stitched, pull_head = jax.vjp(stitch_head, pre, stitch_out)
    activations = (live[:, None, None] * stitched).astype(bf16)
    grad_out = live[:, None, None] * cotangent.astype(f32)
    grad_pre, grad_so = pull_head(grad_out)
    grad_low = grad_pre.astype(bf16)
    grad_all = lax.all_gather(grad_low, "feat", axis=2, tiled=True)
    bias_terms = jnp.sum(grad_all, axis=0, dtype=f32)
    grad_cols = lax.all_to_all(grad_all, "blk", split_axis=2, concat_axis=0, tiled=True)
    weight_grad = jnp.einsum(
        "rtf,rtn->tnf",
        lax.all_gather(feats, "blk", axis=0, tiled=True),
        grad_cols,
        preferred_element_type=f32,
    )
    grad_feats = jnp.einsum(
        "rtn,tnf->rtf",
        grad_all,
        lax.all_gather(fc_weight, "blk", axis=1, tiled=True),
        preferred_element_type=f32,
    )
    grad_mixed = grad_feats.reshape(num_rows, TOWERS, chans, -1)
    grad_pooled, grad_si = pull_first(grad_mixed)
    spread = jnp.einsum(
        "rtcq,pq->rpct", grad_pooled * (1.0 / 9.0), pool_table(f32), precision=lax.Precision.HIGHEST
    )
    conv_grad = spread.reshape(num_rows, MAP * MAP, merged).astype(bf16)
    stitch_in_grad, stitch_out_grad, bias_total = lax.psum((grad_si, grad_so, bias_terms), "blk")
    bias_grad = lax.dynamic_slice_in_dim(bias_total, blk_idx * cols, cols, 1)
    return (activations, conv_grad, weight_grad, bias_grad, stitch_in_grad, stitch_out_grad)


def ring_place(blk):
    z, x = lax.div(blk, 2), lax.rem(blk, 2)
    return z + x * (7 - 2 * z)


def ring_blk(place):
    x = lax.div(place, 4)
    return 2 * (place + x * (7 - 2 * place)) + x


def fc_kernel(
    steps,
    n_ref, so_ref, bias_ref, x_ref, first_ref, cot_ref, relay_ref, w_hbm,
    act_out, gf_out, wg_hbm, bg_out, sog_out,
    w, x, land, ring_tx, ex_tx, ex_rx, gp, part, held, sums,
    cot_rx, acts, act_tx, act_rx, sog_acc, sog_tx, sog_rx, wg_acc,
    kd, nn, start, tot, slot_rc, slot_live,
    w_sem, ag_ss, ag_rs, rs_ss, rs_rs, ex_ss, ex_rs, gp_ss, gp_rs,
    cot_ss, cot_rs, act_ss, act_rs, sog_ss, sog_rs, wg_sem, free,
):
    blk, feat = lax.axis_index("blk"), lax.axis_index("feat")
    place = ring_place(blk)
    ring_to = (ring_blk(lax.rem(place + 1, 8)), ring_blk(lax.rem(place + 7, 8)))
    ring_from = (lax.rem(place + 7, 8), lax.rem(place + 1, 8))
    per = 2 * SPAN
    groups = x.shape[0] - 8 // per
    slots = groups * SPAN
    sent = PIECES * (steps - 1)
    part_dim = x.shape[-1]
    units = w.shape[1]
    quarter = units // FEATS
    row_feat = lax.div(blk, 2)
    half_at = lax.rem(blk, 2) * FEATS + feat
    mine = row_feat == feat
    side = 2 * lax.div(feat, 2)
    cot_feat = side + lax.rem(row_feat, 2)
    cot_mine = cot_feat == feat

    w_copy = pltpu.make_async_copy(w_hbm, w, w_sem)
    w_copy.start()

    bar = pltpu.get_barrier_semaphore()

    def hello(dev):
        pl.semaphore_signal(bar, inc=1, device_id=dev, device_id_type=MESH)

    for d in (0, 1):
        hello((ring_to[d], feat))
    for o in range(1, FEATS):
        hello((blk, lax.rem(feat + o, FEATS)))

    def cot_to(s):
        owner = lax.rem(feat + 2 * lax.div(s, 4), FEATS)
        return 2 * owner + lax.rem(lax.div(s, 2), 2), side + lax.rem(s, 2)

    def cot_not_me(s):
        to = cot_to(s)
        return jnp.logical_or(to[0] != blk, to[1] != feat)

    def hello_far(s, carry):
        to = (2 * feat + lax.div(s, FEATS), lax.rem(s, FEATS))

        @pl.when(jnp.logical_or(to[0] != blk, to[1] != feat))
        def _():
            hello(to)

        @pl.when(jnp.logical_or(s != blk, row_feat != feat))
        def _():
            hello((s, row_feat))

        @pl.when(cot_not_me(s))
        def _():
            hello(cot_to(s))

        @pl.when(jnp.logical_or(s != blk, cot_feat != feat))
        def _():
            hello((s, cot_feat))

        return carry

    lax.fori_loop(0, 8, hello_far, 0)

    for d in (0, 1):
        for m in range(PIECES):
            land[d, m] = first_ref[d, m]

    def own_cot(s):
        return lax.div(s, 2) * FEATS + side + lax.rem(s, 2)

    def cot_copy(s, src):
        return pltpu.make_async_remote_copy(
            src_ref=src, dst_ref=cot_rx.at[blk], send_sem=cot_ss.at[s],
            recv_sem=cot_rs.at[blk], device_id=cot_to(s), device_id_type=MESH)

    def cot_wait(r):
        return pltpu.make_async_remote_copy(
            src_ref=cot_ref.at[0], dst_ref=cot_rx.at[r], send_sem=cot_ss.at[0],
            recv_sem=cot_rs.at[r], device_id=(r, cot_feat), device_id_type=MESH)

    def far_not_me(s):
        return jnp.logical_or(2 * feat + lax.div(s, FEATS) != blk, lax.rem(s, FEATS) != feat)

    def near_not_me(r):
        return jnp.logical_or(r != blk, row_feat != feat)

    for c in range(8):
        for t in range(TOWERS):
            for h in range(2):
                x[groups + c // per, t, h, c % per // SPAN, c % SPAN] = x_ref[
                    c, t, :, h * part_dim:(h + 1) * part_dim]

    run = jnp.int32(0)
    for q in range(PLACES):
        n = n_ref[RING_BLK[q]]
        k = jnp.clip(lax.div(n + (CHUNK - 1), CHUNK), 2, 8)
        first = lax.div(run + k + 1, 2) - lax.div(run + 1, 2)
        kd[q] = first
        kd[PLACES + q] = k - first
        nn[q] = n
        run = run + k

    def ring_unit_copy(d, m):
        return pltpu.make_async_remote_copy(
            src_ref=ring_tx.at[d, lax.rem(m, 8)], dst_ref=land.at[d, m],
            send_sem=ag_ss.at[d, lax.rem(m, 8)], recv_sem=ag_rs.at[d, m],
            device_id=(ring_to[d], feat), device_id_type=MESH)

    own_k = (kd[place], kd[PLACES + place])
    prev_k = tuple(kd[d * PLACES + ring_from[d]] for d in (0, 1))

    def chunk_of(d, c, first):
        return jnp.where(c == 0, d, (c + 1 if d == 0 else first + c))

    def own_piece(d, pos, t, h):
        c = chunk_of(d, pos, own_k[0])
        return x[groups + lax.div(c, per), t, h, lax.div(lax.rem(c, per), SPAN), lax.rem(c, SPAN)]

    def cot_send(s, carry):
        @pl.when(cot_not_me(s))
        def _():
            cot_copy(s, cot_ref.at[own_cot(s)]).start()

        @pl.when(jnp.logical_not(cot_not_me(s)))
        def _():
            cot_rx[blk] = cot_ref[own_cot(s)]

        @pl.when(cot_not_me(s + 4))
        def _():
            cot_copy(s + 4, relay_ref.at[s]).start()

        @pl.when(jnp.logical_not(cot_not_me(s + 4)))
        def _():
            cot_rx[blk] = relay_ref[s]

        return carry


    for d in (0, 1):
        run = jnp.int32(0)
        for h in range(1, PLACES + 1):
            at = lax.rem(place + (PLACES - h if d == 0 else h), PLACES)
            start[d * PLACES + at] = run
            run = run + kd[d * PLACES + at]
        tot[d] = run

        def fill(i, carry, d=d):
            h, c = carry
            hc = jnp.minimum(h, PLACES)
            at = lax.rem(place + (2 * PLACES - hc if d == 0 else hc), PLACES)
            chunk = jnp.minimum(chunk_of(d, c, kd[at]), 7)
            live = jnp.clip(nn[at] - CHUNK * chunk, 0, CHUNK)
            slot_rc[d * slots + i] = ring_blk(at) * 8 + chunk
            slot_live[d * slots + i] = jnp.where(h <= PLACES, live, 0)
            over = c + 1 >= kd[d * PLACES + at]
            return jnp.where(over, h + 1, h), jnp.where(over, 0, c + 1)

        lax.fori_loop(0, slots, fill, (jnp.int32(1), jnp.int32(0)))

    own_at = (tot[0] - own_k[0], tot[1] - own_k[1])
    held[...] = jnp.zeros_like(held)
    sog_acc[...] = jnp.zeros_like(sog_acc)
    pl.semaphore_wait(
        bar, jnp.where(mine, 2 + 3 + 14, 2 + 3 + 16) + jnp.where(cot_mine, 14, 16))
    lax.fori_loop(0, 4, cot_send, 0)

    def ex_copy(slot, g, o):
        to = lax.rem(feat + o, FEATS)
        return pltpu.make_async_remote_copy(
            src_ref=ex_tx.at[slot, to], dst_ref=ex_rx.at[g, feat], send_sem=ex_ss.at[slot, o - 1],
            recv_sem=ex_rs.at[g, feat], device_id=(blk, to), device_id_type=MESH)

    def ex_wait(g, o):
        src = lax.rem(feat + o, FEATS)
        return pltpu.make_async_remote_copy(
            src_ref=ex_tx.at[0, src], dst_ref=ex_rx.at[g, src], send_sem=ex_ss.at[0, o - 1],
            recv_sem=ex_rs.at[g, src], device_id=(blk, src), device_id_type=MESH)

    def gp_copy(g, o):
        to = lax.rem(feat + o, FEATS)
        return pltpu.make_async_remote_copy(
            src_ref=gp.at[g, feat], dst_ref=gp.at[g, feat], send_sem=gp_ss.at[g, o - 1],
            recv_sem=gp_rs.at[g, feat], device_id=(blk, to), device_id_type=MESH)

    def gp_wait(g, o):
        src = lax.rem(feat + o, FEATS)
        return pltpu.make_async_remote_copy(
            src_ref=gp.at[g, src], dst_ref=gp.at[g, src], send_sem=gp_ss.at[g, o - 1],
            recv_sem=gp_rs.at[g, src], device_id=(blk, src), device_id_type=MESH)

    def forward(g, t):
        slot = lax.rem(g, 2)

        @pl.when(jnp.logical_and(g >= 2, t == 0))
        def _():
            for o in range(1, FEATS):
                ex_copy(slot, g, o).wait_send()

        for n in range(2):
            out = sum(
                lax.dot_general(
                    x[g, t, h].reshape(per * CHUNK, part_dim),
                    w[t, 2 * n * quarter:2 * (n + 1) * quarter, h * part_dim:(h + 1) * part_dim],
                    (((1,), (1,)), ((), ())), preferred_element_type=f32)
                for h in range(2))
            for e in range(2):
                ex_tx[slot, 2 * n + e, t] = out[:, e * quarter:(e + 1) * quarter].reshape(
                    per, CHUNK, quarter)

        @pl.when(t == 1)
        def _():
            for o in range(1, FEATS):
                ex_copy(slot, g, o).start()
            ex_rx[g, feat] = ex_tx[slot, feat]

    bias_here = bias_ref[:, pl.ds(pl.multiple_of(blk * units + feat * quarter, quarter), quarter)]

    def head(g):
        for o in range(1, FEATS):
            ex_wait(g, o).wait_recv()

        def one(s, carry):
            d, ci = lax.div(s, SPAN), lax.rem(s, SPAN)
            i = g * SPAN + ci
            rc = slot_rc[d * slots + i]
            live = slot_live[d * slots + i]
            mask = jnp.where(
                lax.broadcasted_iota(i32, (CHUNK, quarter), 0) < live, f32(1), f32(0))
            act, slope, cot = [], [], []
            for t in range(TOWERS):
                pre = ex_rx[g, 0, t, s]
                for q in range(1, FEATS):
                    pre = pre + ex_rx[g, q, t, s]
                pre = pre + bias_here[t:t + 1]
                square = pre * pre
                th = jnp.tanh(f32(0.7978845608028654) * (pre + f32(0.044715) * (square * pre)))
                cdf = f32(0.5) * (f32(1) + th)
                act.append(pre * cdf)
                slope.append(cdf + f32(0.5) * pre * (f32(1) - th * th) * (
                    f32(0.7978845608028654) * (f32(1) + f32(3 * 0.044715) * square)))
                cot.append(cot_rx[lax.div(rc, 8), lax.rem(rc, 8), t].astype(f32) * mask)
            for t in range(TOWERS):
                out = so_ref[2 * t:2 * t + 1] * act[0] + so_ref[2 * t + 1:2 * t + 2] * act[1]
                acts[i, d, t] = (out * mask).astype(bf16)
                for u in range(TOWERS):
                    sog_acc[2 * t + u] = sog_acc[2 * t + u] + cot[t] * act[u]
            for u in range(TOWERS):
                back = so_ref[u:u + 1] * cot[0] + so_ref[2 + u:3 + u] * cot[1]
                gp[g, feat, u, s] = (slope[u] * back).astype(bf16)
            return carry

        lax.fori_loop(0, per, one, 0)
        for o in range(1, FEATS):
            gp_copy(g, o).start()

    tile = part_dim // 3

    def backward(g, t):
        rows = jnp.concatenate(
            [gp[g, q, t].reshape(per * CHUNK, quarter) for q in range(FEATS)], axis=1)
        for h in range(2):
            part[t, h] = jnp.dot(
                rows, w[t, :, h * part_dim:(h + 1) * part_dim],
                preferred_element_type=f32).reshape(per, CHUNK, part_dim)

    def tile_at(q):
        t, n = lax.div(q, 6), lax.rem(q, 6)
        return t, lax.div(n, 3), pl.multiple_of(n * tile, 128), pl.multiple_of(lax.rem(n, 3) * tile, 128)

    def wg_copy(q):
        t, _, whole_at, _ = tile_at(q)
        cols = pl.ds(whole_at, tile)
        return pltpu.make_async_copy(wg_acc.at[t, :, cols], wg_hbm.at[t, :, cols], wg_sem.at[q])

    def weight_tile(q, first, count):
        t, h, whole_at, part_at = tile_at(q)
        rows = x[first:first + count, t, h, :, :, :, pl.ds(part_at, tile)].reshape(
            count * per * CHUNK, tile)
        for e in range(FEATS):
            grads = gp[first:first + count, e, t].reshape(count * per * CHUNK, quarter)
            value = lax.dot_general(
                grads, rows, (((0,), (0,)), ((), ())), preferred_element_type=f32)
            at = (t, pl.ds(e * quarter, quarter), pl.ds(whole_at, tile))
            wg_acc[at] = value + wg_acc[at] if first else value

    def gather_unit(g, q):
        u = PIECES * SPAN * g + q
        ci, t, h = lax.div(q, PIECES), lax.rem(lax.div(q, 2), 2), lax.rem(q, 2)
        i = SPAN * g + ci
        for d in (0, 1):
            own = own_piece(d, jnp.clip(i - own_at[d], 0, own_k[d] - 1), t, h)

            @pl.when(u < sent)
            def _(d=d, own=own):
                @pl.when(u >= PIECES)
                def _():
                    ring_unit_copy(d, u).wait_recv()

                x[g, t, h, d, ci] = jnp.where(i >= own_at[d], own, land[d, u])

            @pl.when(u >= sent)
            def _(d=d, own=own):
                x[g, t, h, d, ci] = own

            m = u + PIECES

            @pl.when(m < sent)
            def _(d=d):
                @pl.when(m >= 8 + PIECES)
                def _():
                    ring_unit_copy(d, m).wait_send()

                here = i + 1 < own_k[d]
                c = chunk_of(d, jnp.minimum(i + 1, own_k[d] - 1), own_k[0])
                src = jnp.maximum(i + 1 - own_k[d], 0)
                ring_tx[d, lax.rem(m, 8)] = x[
                    jnp.where(here, groups + lax.div(c, per), lax.div(src, SPAN)), t, h,
                    jnp.where(here, lax.div(lax.rem(c, per), SPAN), d),
                    jnp.where(here, lax.rem(c, SPAN), lax.rem(src, SPAN))]
                ring_unit_copy(d, m).start()

    def sum_copy(d, v):
        return pltpu.make_async_remote_copy(
            src_ref=sums.at[d, v], dst_ref=land.at[d, v], send_sem=rs_ss.at[d, lax.rem(v, HELD)],
            recv_sem=rs_rs.at[d, v], device_id=(ring_to[d], feat), device_id_type=MESH)

    def sum_unit(g, q):
        v = PIECES * SPAN * g + q
        ci, t, h = lax.div(q, PIECES), lax.rem(lax.div(q, 2), 2), lax.rem(q, 2)
        before = v - PIECES
        for d in (0, 1):
            @pl.when(jnp.logical_and(before >= 0, before < sent))
            def _(d=d):
                sum_copy(d, before).wait_recv()
                held[d, lax.rem(before, HELD)] = land[d, before]

            came = held[d, lax.rem(v - PIECES * prev_k[d] + HELD, HELD)].astype(f32)
            value = part[t, h, d * SPAN + ci] + came * jnp.where(
                v >= PIECES * prev_k[d], f32(1), f32(0))
            sums[d, v] = value.astype(bf16)

            @pl.when(v < sent)
            def _(d=d):
                @pl.when(v >= HELD)
                def _():
                    sum_copy(d, v).wait_send()

                sum_copy(d, v).start()

    def act_copy(r):
        return pltpu.make_async_remote_copy(
            src_ref=act_tx.at[r], dst_ref=act_rx.at[half_at], send_sem=act_ss.at[r],
            recv_sem=act_rs.at[half_at], device_id=(r, row_feat), device_id_type=MESH)

    def act_wait(s):
        return pltpu.make_async_remote_copy(
            src_ref=act_tx.at[0], dst_ref=act_rx.at[s], send_sem=act_ss.at[0],
            recv_sem=act_rs.at[s], device_id=(blk, feat), device_id_type=MESH)

    def sog_copy(r):
        return pltpu.make_async_remote_copy(
            src_ref=sog_tx, dst_ref=sog_rx.at[half_at], send_sem=sog_ss.at[r],
            recv_sem=sog_rs.at[half_at], device_id=(r, row_feat), device_id_type=MESH)

    def sog_wait(s):
        return pltpu.make_async_remote_copy(
            src_ref=sog_tx, dst_ref=sog_rx.at[s], send_sem=sog_ss.at[0],
            recv_sem=sog_rs.at[s], device_id=(blk, feat), device_id_type=MESH)

    def send_acts(r):
        at = ring_place(r)
        first, second = kd[at], kd[PLACES + at]
        for c in range(8):
            late = c > first
            d = jnp.where(late, 1, 0) if c > 1 else c
            pos = jnp.where(late, c - first, c - 1) if c > 1 else 0
            i = jnp.minimum(start[d * PLACES + at] + pos, slots - 1)
            keep = jnp.where(c < first + second, f32(1), f32(0))
            for t in range(TOWERS):
                act_tx[r, c, t] = (acts[i, d, t].astype(f32) * keep).astype(bf16)

        @pl.when(near_not_me(r))
        def _():
            act_copy(r).start()
            sog_copy(r).start()

        @pl.when(jnp.logical_not(near_not_me(r)))
        def _():
            act_rx[half_at] = act_tx[r]
            sog_rx[half_at] = sog_tx[...]

    def add_bias():
        for e in range(FEATS):
            for t in range(TOWERS):
                def add(g, total, e=e, t=t):
                    return total + jnp.sum(gp[g, e, t].astype(f32), axis=0)

                total = lax.fori_loop(0, groups, add, jnp.zeros((CHUNK, quarter), f32))
                bg_out[t:t + 1, e * quarter:(e + 1) * quarter] = jnp.sum(
                    total, axis=0, keepdims=True)

    early = groups - 2

    def iteration(it, carry):
        @pl.when(it >= 3)
        def _():
            for o in range(1, FEATS):
                gp_wait(it - 3, o).wait_recv()
            backward(it - 3, 0)

        @pl.when(it == 1)
        def _():
            w_copy.wait()

        @pl.when(it == 2)
        def _():
            def arrived(r, carry):
                @pl.when(jnp.logical_or(r != blk, cot_feat != feat))
                def _():
                    cot_wait(r).wait_recv()

                return carry

            lax.fori_loop(0, PLACES, arrived, 0)

        @pl.when(jnp.logical_and(it >= 2, it < groups + 2))
        def _():
            head(it - 2)

        @pl.when(it == groups + 1)
        def _():
            sog_tx[...] = jnp.concatenate(
                [jnp.sum(sog_acc[e], axis=0, keepdims=True) for e in range(4)] * 2, axis=0)

        @pl.when(it >= 3)
        def _():
            for d in (0, 1):
                pl.semaphore_wait(free.at[d], 1)

        def unit(q, carry):
            @pl.when(it < groups)
            def _():
                gather_unit(it, q)

            @pl.when(it >= 3)
            def _():
                sum_unit(it - 3, q)

            @pl.when(jnp.logical_and(
                lax.rem(q, 2) == 0, jnp.logical_and(q < 4, jnp.logical_and(it >= 1, it < groups + 1))))
            def _():
                forward(it - 1, lax.div(q, 2))

            @pl.when(jnp.logical_and(it >= 3, q == 1))
            def _():
                backward(it - 3, 1)

            @pl.when(it == groups + 1)
            def _():
                send_acts(q)

            @pl.when(jnp.logical_and(it == groups + 2, q == 3))
            def _():
                add_bias()

            @pl.when(jnp.logical_and(jnp.logical_or(it == groups, it == groups + 1), q < 6))
            def _():
                weight_tile(q + 6 * (it - groups), 0, early)

            @pl.when(jnp.logical_and(it == groups + 2, q < 6))
            def _():
                def last(e, carry):
                    weight_tile(2 * q + e, early, 2)
                    wg_copy(2 * q + e).start()
                    return carry

                lax.fori_loop(0, 2, last, 0)

            return carry

        lax.fori_loop(0, PIECES * SPAN, unit, 0)

        @pl.when(it < groups)
        def _():
            for d in (0, 1):
                pl.semaphore_signal(
                    free.at[d], inc=1, device_id=(ring_blk(ring_from[d]), feat), device_id_type=MESH)

        return carry

    lax.fori_loop(0, groups + 3, iteration, 0)

    for c in range(8):
        late = c > own_k[0]
        d = jnp.where(late, 1, 0) if c > 1 else c
        i = jnp.where(late, own_at[1] + c - own_k[0], own_at[0] + c - 1) if c > 1 else own_at[c]
        i = jnp.clip(i, 0, slots - 1)
        keep = jnp.where(c < own_k[0] + own_k[1], f32(1), f32(0))
        for t in range(TOWERS):
            for h in range(2):
                gf_out[c, t, :, h * part_dim:(h + 1) * part_dim] = (
                    sums[d, PIECES * i + 2 * t + h].astype(f32) * keep).astype(bf16)

    def finish(s, carry):
        @pl.when(far_not_me(s))
        def _():
            act_wait(s).wait_recv()
            sog_wait(s).wait_recv()

        @pl.when(cot_not_me(s))
        def _():
            cot_copy(s, cot_ref.at[0]).wait_send()

        @pl.when(near_not_me(s))
        def _():
            act_copy(s).wait_send()
            sog_copy(s).wait_send()

        return carry

    lax.fori_loop(0, 8, finish, 0)
    act_out[...] = act_rx[...]
    sog_out[...] = sog_rx[...]

    def finish_sums(v, carry):
        for d in (0, 1):
            sum_copy(d, v).wait_send()
        return carry

    lax.fori_loop(sent - HELD, sent, finish_sums, 0)
    for m in range(sent - 8, sent):
        for d in (0, 1):
            ring_unit_copy(d, jnp.int32(m)).wait_send()
    for o in range(1, FEATS):
        for g in (groups - 2, groups - 1):
            ex_copy(g % 2, g, o).wait_send()

        def finish_gp(g, carry, o=o):
            gp_copy(g, o).wait_send()
            return carry

        lax.fori_loop(0, groups, finish_gp, 0)
    for q in range(12):
        wg_copy(jnp.int32(q)).wait()


def fc_layer(steps, number, n, so, bias, x, first, cot, relay, weight):
    units, feats_dim = weight.shape[1:]
    quarter = units // FEATS
    groups = -(-steps // SPAN)
    slots = groups * SPAN
    vm = pltpu.VMEM
    dma = pltpu.SemaphoreType.DMA
    sm = pltpu.SMEM
    unit = (CHUNK, feats_dim // 2)
    vmem_spec = pl.BlockSpec(memory_space=pltpu.VMEM)
    any_spec = pl.BlockSpec(memory_space=pl.ANY)
    rows = 2 * slots * CHUNK
    return pl.pallas_call(
        functools.partial(fc_kernel, steps),
        out_shape=(
            jax.ShapeDtypeStruct((8, 8, TOWERS, CHUNK, quarter), bf16),
            jax.ShapeDtypeStruct((8, TOWERS, CHUNK, feats_dim), bf16),
            jax.ShapeDtypeStruct(weight.shape, f32),
            jax.ShapeDtypeStruct((TOWERS, units), f32),
            jax.ShapeDtypeStruct((8, 8, quarter), f32),
        ),
        in_specs=[pl.BlockSpec(memory_space=pltpu.SMEM)] + [vmem_spec] * 6 + [any_spec],
        out_specs=(vmem_spec, vmem_spec, any_spec, vmem_spec, vmem_spec),
        scratch_shapes=[
            vm(weight.shape, bf16),
            vm((groups + 8 // (2 * SPAN), TOWERS, 2, 2, SPAN) + unit, bf16),
            vm((2, PIECES * (steps - 1)) + unit, bf16),
            vm((2, 8) + unit, bf16),
            vm((2, FEATS, TOWERS, 2 * SPAN, CHUNK, quarter), f32),
            vm((groups, FEATS, TOWERS, 2 * SPAN, CHUNK, quarter), f32),
            vm((groups, FEATS, TOWERS, 2 * SPAN, CHUNK, quarter), bf16),
            vm((TOWERS, 2, 2 * SPAN) + unit, f32),
            vm((2, HELD) + unit, bf16),
            vm((2, PIECES * slots) + unit, bf16),
            vm((8, 8, TOWERS, CHUNK, quarter), bf16),
            vm((slots, 2, TOWERS, CHUNK, quarter), bf16),
            vm((8, 8, TOWERS, CHUNK, quarter), bf16),
            vm((8, 8, TOWERS, CHUNK, quarter), bf16),
            vm((4, CHUNK, quarter), f32),
            vm((8, quarter), f32),
            vm((8, 8, quarter), f32),
            vm(weight.shape, f32),
            sm((2 * PLACES,), i32),
            sm((PLACES,), i32),
            sm((2 * PLACES,), i32),
            sm((2,), i32),
            sm((2 * slots,), i32),
            sm((2 * slots,), i32),
            dma,
            dma((2, 8)),
            dma((2, PIECES * (steps - 1))),
            dma((2, HELD)),
            dma((2, PIECES * (steps - 1))),
            dma((2, 3)),
            dma((groups, FEATS)),
            dma((groups, 3)),
            dma((groups, FEATS)),
            dma((8,)),
            dma((8,)),
            dma((8,)),
            dma((8,)),
            dma((8,)),
            dma((8,)),
            dma((12,)),
            pltpu.SemaphoreType.REGULAR((2,)),
        ],
        cost_estimate=pl.CostEstimate(
            flops=6 * rows * TOWERS * units * feats_dim, bytes_accessed=30 << 20,
            transcendentals=rows * TOWERS * quarter),
        compiler_params=pltpu.CompilerParams(
            collective_id=number, has_side_effects=True, vmem_limit_bytes=60 << 20),
    )(n, so, bias, x, first, cot, relay, weight)


def layout_matrix(chans):
    table = np.zeros((4 * 2 * chans, 4 * 2 * chans), np.float32)
    for q0 in range(4):
        for c in range(chans):
            for t in range(TOWERS):
                lane = 4 * ((9 * c) % 32) + q0
                table[q0 * 2 * chans + 2 * c + t, (2 * t + c // 32) * 128 + lane] = 1
    return table


def lane_sources():
    slot = np.arange(128) // 4
    rows = [(slot + 32 * j) % 9 for j in range(9)] + [(2 * (q1 - slot)) % 9 for q1 in range(9)]
    return np.broadcast_to(np.stack(rows)[:, None, :], (18, CHUNK, 128)).astype(np.int32)


def lane_pairs(chans):
    shape = (chans, TOWERS * chans)
    lane, chan = lax.broadcasted_iota(i32, shape, 1), lax.broadcasted_iota(i32, shape, 0)
    return tuple((lane == 2 * chan + t).astype(f32) for t in range(TOWERS))


def exact_dot(a, b, dims):
    return lax.dot_general(
        a, b, (dims, ((), ())), precision=lax.Precision.HIGHEST, preferred_element_type=f32)


def pair_swap():
    even = (lax.broadcasted_iota(i32, (CHUNK, 128), 1) & 1) == 0

    def swap(value):
        return jnp.where(even, pltpu.roll(value, 127, 1), pltpu.roll(value, 1, 1))

    return swap


BATCH = 2
LAST = 4
STEPS = 2
WAYS = 4


def entry_kernel(
    cc_ref, so_ref, si_ref, perm_ref, source_ref, cot_ref, conv_ref,
    feats_out, pooled_out, n_out, pick_out, so_out, relay_out, first_out, s_out,
    n_tx, n_rx, so_tx, so_rx, relay_rx, first_tx, first_rx, s_ref,
    n_ss, n_rs, so_ss, so_rs, relay_ss, relay_rs, first_ss, first_rs,
):
    blk, feat = lax.axis_index("blk"), lax.axis_index("feat")
    step = pl.program_id(0)
    holds = lax.div(blk, 2) == feat

    def n_copy(o):
        to = lax.rem(blk + o, PLACES)
        return pltpu.make_async_remote_copy(
            src_ref=n_tx, dst_ref=n_rx.at[blk], send_sem=n_ss.at[o - 1], recv_sem=n_rs.at[blk],
            device_id=(to, feat), device_id_type=MESH)

    def n_wait(o):
        src = lax.rem(blk + o, PLACES)
        return pltpu.make_async_remote_copy(
            src_ref=n_tx, dst_ref=n_rx.at[src], send_sem=n_ss.at[o - 1], recv_sem=n_rs.at[src],
            device_id=(src, feat), device_id_type=MESH)

    def so_copy(o):
        to = lax.rem(feat + o, FEATS)
        return pltpu.make_async_remote_copy(
            src_ref=so_tx.at[to], dst_ref=so_rx, send_sem=so_ss.at[o - 1], recv_sem=so_rs,
            device_id=(blk, to), device_id_type=MESH)

    across_y = lax.rem(feat + 2, FEATS)
    place = ring_place(blk)
    half = feats_out.shape[-1] // 2

    def first_copy(d, m):
        return pltpu.make_async_remote_copy(
            src_ref=first_tx.at[d, m], dst_ref=first_rx.at[d, m], send_sem=first_ss.at[d, m],
            recv_sem=first_rs.at[d, m],
            device_id=(ring_blk(lax.rem(place + 1 + 6 * d, 8)), feat), device_id_type=MESH)

    def relay_copy(s):
        return pltpu.make_async_remote_copy(
            src_ref=cot_ref.at[s // 2 * FEATS + 2 * lax.div(across_y, 2) + s % 2],
            dst_ref=relay_rx.at[s], send_sem=relay_ss.at[s], recv_sem=relay_rs.at[s],
            device_id=(blk, across_y), device_id_type=MESH)

    @pl.when(step == 0)
    def _():
        bar = pltpu.get_barrier_semaphore()
        for o in range(1, PLACES):
            pl.semaphore_signal(
                bar, inc=1, device_id=(lax.rem(blk + o, PLACES), feat), device_id_type=MESH)
        for o in range(1, FEATS):
            pl.semaphore_signal(
                bar, inc=1, device_id=(blk, lax.rem(feat + o, FEATS)), device_id_type=MESH)
        total = cc_ref[0]
        for e in range(1, cc_ref.shape[0]):
            total = total + cc_ref[e]
        n_tx[...] = jnp.full(n_tx.shape, total, i32)
        n_rx[blk] = n_tx[...]
        for q in range(FEATS):
            at = pl.ds(pl.multiple_of(lax.rem(blk, 2) * 512 + q * 128, 128), 128)
            for t in range(TOWERS):
                so_tx[q, 2 * t:2 * t + 2] = so_ref[t, :, at]
                so_tx[q, 4 + 2 * t:6 + 2 * t] = so_ref[t, :, at]
        even, odd = lane_pairs(si_ref.shape[-1])
        rows = [[exact_dot(si_ref[t], v, ((1,), (0,))) for v in (even, odd)] for t in range(TOWERS)]
        s_ref[0:1] = rows[0][0][0:1] + rows[1][1][1:2]
        s_ref[1:2] = rows[0][0][1:2] + rows[1][1][0:1]
        s_ref[2:3] = rows[1][0][0:1] + rows[0][1][1:2]
        s_ref[3:8] = jnp.zeros((5, s_ref.shape[1]), f32)
        pl.semaphore_wait(bar, PLACES - 1 + FEATS - 1)
        for o in range(1, PLACES):
            n_copy(o).start()
        for s in range(4):
            relay_copy(s).start()

        @pl.when(holds)
        def _():
            so_rx[...] = so_tx[feat]
            for o in range(1, FEATS):
                so_copy(o).start()

    def chunk(e, carry):
        swap = pair_swap()
        at_row = pl.ds(pl.multiple_of(e * CHUNK, CHUNK), CHUNK)
        across = {}
        for row in range(MAP):
            line = [conv_ref[MAP * row + col, at_row].astype(f32) for col in range(MAP)]
            for v in range(GRID):
                across[row, v] = line[2 * v] + line[2 * v + 1] + line[2 * v + 2]
        own, other = s_ref[0:1], s_ref[1:2]
        parts = []
        for q1 in range(9):
            here = []
            for q0 in range(4):
                q = 4 * q1 + q0
                u, v = q // GRID, q % GRID
                pooled = (across[2 * u, v] + across[2 * u + 1, v] + across[2 * u + 2, v]) * f32(1 / 9)
                pooled_out[e, q] = pooled
                here.append((own * pooled + other * swap(pooled)).astype(bf16))
            parts.append(jnp.concatenate(here, axis=1))
        spread = jnp.dot(
            jnp.concatenate(parts, axis=0), perm_ref[...], preferred_element_type=f32)
        turned = [
            pltpu.roll(spread[q1 * CHUNK:(q1 + 1) * CHUNK, at:at + 128], 4 * q1, 1)
            if q1 else spread[0:CHUNK, at:at + 128] for q1 in range(9) for at in range(0, 512, 128)]
        for j in range(9):
            source = source_ref[j]
            tiles = turned[0:4]
            for q1 in range(1, 9):
                here = source == q1
                tiles = [jnp.where(here, turned[4 * q1 + k], tiles[k]) for k in range(4)]
            for k in range(4):
                n = 9 * (k % 2) + j
                feats_out[e, k // 2, :, n * 128:(n + 1) * 128] = tiles[k].astype(bf16)

        @pl.when(step == 0)
        def _():
            for m in range(PIECES):
                first_tx[e, m] = feats_out[e, m // 2, :, m % 2 * half:(m % 2 + 1) * half]
                first_copy(e, m).start()

        return carry

    lax.fori_loop(0, BATCH, chunk, 0)

    @pl.when(step == pl.num_programs(0) - 1)
    def _():
        for m in range(PIECES):
            for d in range(2):
                first_copy(d, m).wait()
        first_out[...] = first_rx[...]
        s_out[...] = s_ref[...]
        for o in range(1, PLACES):
            n_wait(o).wait_recv()
            n_copy(o).wait_send()

        @pl.when(holds)
        def _():
            for o in range(1, FEATS):
                so_copy(o).wait_send()

        @pl.when(jnp.logical_not(holds))
        def _():
            so_copy(1).wait_recv()

        for s in range(4):
            relay_copy(s).wait()
        chunks = jnp.int32(0)
        for q in range(PLACES):
            n = jnp.max(n_rx[q])
            n_out[q] = n
            chunks = chunks + lax.div(n + (CHUNK - 1), CHUNK)
        need = lax.div(chunks + 1, 2)
        pick_out[0] = sum(((need > c).astype(i32) for c in CLASSES), jnp.int32(0))
        so_out[...] = so_rx[...]
        relay_out[...] = relay_rx[...]


def exit_kernel(
    s_ref, perm_ref, source_ref, bg_ref, sog_ref, gf_ref, pooled_ref, wg_ref,
    conv_out, si_out, bg_out, sog_out, wg_out, acc, wg, wg_in, wg_back,
):
    step = pl.program_id(0)

    size = wg.shape[1] // WAYS

    def wg_read(e):
        at = pl.ds(e * size, size)
        return pltpu.make_async_copy(wg_ref.at[:, at], wg.at[:, at], wg_in.at[e])

    def wg_write(e):
        at = pl.ds(e * size, size)
        return pltpu.make_async_copy(wg.at[:, at], wg_out.at[:, at], wg_back.at[e])

    @pl.when(step == 0)
    def _():
        acc[...] = jnp.zeros_like(acc)
        for e in range(WAYS):
            wg_read(e).start()
    def chunk(e, carry):
        swap = pair_swap()
        at_row = pl.ds(pl.multiple_of(e * CHUNK, CHUNK), CHUNK)
        tiles = [
            gf_ref[e, k // 2, :, (9 * (k % 2) + j) * 128:(9 * (k % 2) + j + 1) * 128].astype(f32)
            for j in range(9) for k in range(4)]
        rows = []
        for q1 in range(9):
            source = source_ref[9 + q1]
            here = tiles[0:4]
            for j in range(1, 9):
                mask = source == j
                here = [jnp.where(mask, tiles[4 * j + k], here[k]) for k in range(4)]
            rows.append(jnp.concatenate(
                [pltpu.roll(v, 128 - 4 * q1, 1) if q1 else v for v in here], axis=1).astype(bf16))
        grads = lax.dot_general(
            jnp.concatenate(rows, axis=0), perm_ref[...], (((1,), (1,)), ((), ())),
            preferred_element_type=f32)
        own, other = s_ref[0:1] * f32(1 / 9), s_ref[2:3] * f32(1 / 9)
        same = acc[0]
        cross = acc[1]
        back = {}
        for q in range(GRID * GRID):
            q1, q0 = q // 4, q % 4
            grad = grads[q1 * CHUNK:(q1 + 1) * CHUNK, q0 * 128:(q0 + 1) * 128]
            pooled = pooled_ref[e, q]
            swapped = swap(grad)
            same = same + grad * pooled
            cross = cross + swapped * pooled
            back[q // GRID, q % GRID] = own * grad + other * swapped
        acc[0] = same
        acc[1] = cross
        lines = []
        for u in range(GRID):
            line = []
            for col in range(MAP):
                v = col // 2
                if col % 2:
                    line.append(back[u, v])
                elif col == 0:
                    line.append(back[u, 0])
                elif col == MAP - 1:
                    line.append(back[u, GRID - 1])
                else:
                    line.append(back[u, v - 1] + back[u, v])
            lines.append(line)
        for row in range(MAP):
            u = row // 2
            for col in range(MAP):
                if row % 2 or row == 0:
                    value = lines[u][col]
                elif row == MAP - 1:
                    value = lines[GRID - 1][col]
                else:
                    value = lines[u - 1][col] + lines[u][col]
                conv_out[MAP * row + col, at_row] = value.astype(bf16)
        return carry

    lax.fori_loop(0, LAST, chunk, 0)

    for n in range(STEPS):
        @pl.when(step == n)
        def _(n=n):
            for e in range(WAYS * n // STEPS, WAYS * (n + 1) // STEPS):
                wg_read(e).wait()
                wg_write(e).start()

    @pl.when(step == pl.num_programs(0) - 1)
    def _():
        sums = jnp.concatenate(
            [jnp.sum(acc[e], axis=0, keepdims=True) for e in range(2)] * 4, axis=0)
        chans = sums.shape[1] // TOWERS
        even, odd = (exact_dot(sums, v, ((1,), (1,))) for v in lane_pairs(chans))
        si_out[...] = jnp.zeros_like(si_out)
        si_out[0:1, 0:chans] = even[0:1]
        si_out[1:2, 0:chans] = odd[1:2]
        si_out[2:3, 0:chans] = even[1:2]
        si_out[3:4, 0:chans] = odd[0:1]
        bg_out[...] = bg_ref[...]
        for e in range(8):
            for t in range(TOWERS):
                sog_out[t, :, e * 128:(e + 1) * 128] = sog_ref[e, TOWERS * t:TOWERS * (t + 1)]
        for e in range(WAYS):
            wg_write(e).wait()


def total_kernel(x_ref, out, rx, ss, rs):
    blk, feat = lax.axis_index("blk"), lax.axis_index("feat")

    def copy(o):
        return pltpu.make_async_remote_copy(
            src_ref=x_ref, dst_ref=rx.at[blk], send_sem=ss.at[o - 1], recv_sem=rs.at[blk],
            device_id=(lax.rem(blk + o, PLACES), feat), device_id_type=MESH)

    def wait(o):
        src = lax.rem(blk + o, PLACES)
        return pltpu.make_async_remote_copy(
            src_ref=x_ref, dst_ref=rx.at[src], send_sem=ss.at[o - 1], recv_sem=rs.at[src],
            device_id=(src, feat), device_id_type=MESH)

    bar = pltpu.get_barrier_semaphore()
    for o in range(1, PLACES):
        pl.semaphore_signal(
            bar, inc=1, device_id=(lax.rem(blk + o, PLACES), feat), device_id_type=MESH)
    pl.semaphore_wait(bar, PLACES - 1)
    for o in range(1, PLACES):
        copy(o).start()
    rx[blk] = x_ref[...]
    for o in range(1, PLACES):
        wait(o).wait_recv()
    total = rx[0]
    for q in range(1, PLACES):
        total = total + rx[q]
    for t in range(TOWERS):
        out[t] = total[TOWERS * t:TOWERS * (t + 1), 0:out.shape[-1]]
    for o in range(1, PLACES):
        copy(o).wait_send()


def entry(counts, so, stitch, cot, conv):
    spots, rows, merged = conv.shape
    chunks = rows // CHUNK
    chans = merged // TOWERS
    wide = chans * GRID * GRID
    vm, dma = pltpu.VMEM, pltpu.SemaphoreType.DMA
    whole = pl.BlockSpec(memory_space=pltpu.VMEM)
    scalars = pl.BlockSpec(memory_space=pltpu.SMEM)
    return pl.pallas_call(
        entry_kernel,
        grid=(chunks // BATCH,),
        out_shape=(
            jax.ShapeDtypeStruct((chunks, TOWERS, CHUNK, wide), bf16),
            jax.ShapeDtypeStruct((chunks, GRID * GRID, CHUNK, merged), f32),
            jax.ShapeDtypeStruct((PLACES,), i32),
            jax.ShapeDtypeStruct((1,), i32),
            jax.ShapeDtypeStruct((8, 128), f32),
            jax.ShapeDtypeStruct((4,) + cot.shape[1:], bf16),
            jax.ShapeDtypeStruct((2, PIECES, CHUNK, wide // 2), bf16),
            jax.ShapeDtypeStruct((8, merged), f32),
        ),
        in_specs=[scalars] + [whole] * 5 + [
            pl.BlockSpec((spots, BATCH * CHUNK, merged), lambda c: (0, c, 0))],
        out_specs=(
            pl.BlockSpec((BATCH, TOWERS, CHUNK, wide), lambda c: (c, 0, 0, 0)),
            pl.BlockSpec((BATCH, GRID * GRID, CHUNK, merged), lambda c: (c, 0, 0, 0)),
            scalars, scalars, whole, whole, whole, whole,
        ),
        scratch_shapes=[
            vm((8, 128), i32), vm((PLACES, 8, 128), i32), vm((FEATS, 8, 128), f32), vm((8, 128), f32),
            vm((4,) + cot.shape[1:], bf16), vm((2, PIECES, CHUNK, wide // 2), bf16),
            vm((2, PIECES, CHUNK, wide // 2), bf16), vm((8, merged), f32),
            dma((PLACES - 1,)), dma((PLACES,)), dma((FEATS - 1,)), dma, dma((4,)), dma((4,)),
            dma((2, PIECES)), dma((2, PIECES)),
        ],
        cost_estimate=pl.CostEstimate(flops=1 << 30, bytes_accessed=10 << 20, transcendentals=0),
        compiler_params=pltpu.CompilerParams(
            collective_id=20, has_side_effects=True, vmem_limit_bytes=60 << 20),
    )(counts, so, stitch, jnp.asarray(layout_matrix(chans), bf16), jnp.asarray(lane_sources()), cot, conv)


def leave(s_rows, bias_grad, sog, gf, pooled, weight_grad, spots):
    chunks, towers, _, wide = gf.shape
    merged = pooled.shape[-1]
    vm = pltpu.VMEM
    whole = pl.BlockSpec(memory_space=pltpu.VMEM)
    share = pl.BlockSpec(memory_space=pl.ANY)
    return pl.pallas_call(
        exit_kernel,
        grid=(chunks // LAST,),
        out_shape=(
            jax.ShapeDtypeStruct((spots, chunks * CHUNK, merged), bf16),
            jax.ShapeDtypeStruct((8, 128), f32),
            jax.ShapeDtypeStruct(bias_grad.shape, f32),
            jax.ShapeDtypeStruct((TOWERS, TOWERS, 8 * sog.shape[-1]), f32),
            jax.ShapeDtypeStruct(weight_grad.shape, f32),
        ),
        in_specs=[whole] * 5 + [
            pl.BlockSpec((LAST, towers, CHUNK, wide), lambda c: (c, 0, 0, 0)),
            pl.BlockSpec((LAST, GRID * GRID, CHUNK, merged), lambda c: (c, 0, 0, 0)),
            share],
        out_specs=(
            pl.BlockSpec((spots, LAST * CHUNK, merged), lambda c: (0, c, 0)),
            whole, whole, whole, share,
        ),
        scratch_shapes=[
            vm((2, CHUNK, 128), f32), vm(weight_grad.shape, f32),
            pltpu.SemaphoreType.DMA((WAYS,)), pltpu.SemaphoreType.DMA((WAYS,))],
        cost_estimate=pl.CostEstimate(flops=1 << 30, bytes_accessed=30 << 20, transcendentals=0),
        compiler_params=pltpu.CompilerParams(vmem_limit_bytes=60 << 20),
    )(s_rows, jnp.asarray(layout_matrix(merged // TOWERS), bf16),
      jnp.asarray(lane_sources()), bias_grad, sog, gf, pooled, weight_grad)


def total_over_blk(value):
    whole = pl.BlockSpec(memory_space=pltpu.VMEM)
    dma = pltpu.SemaphoreType.DMA
    return pl.pallas_call(
        total_kernel,
        out_shape=jax.ShapeDtypeStruct((TOWERS, TOWERS, value.shape[1] // TOWERS), f32),
        in_specs=[whole],
        out_specs=whole,
        scratch_shapes=[
            pltpu.VMEM((PLACES,) + value.shape, f32), dma((PLACES - 1,)), dma((PLACES,))],
        compiler_params=pltpu.CompilerParams(
            collective_id=21, has_side_effects=True, vmem_limit_bytes=16 << 20),
    )(value)


def body_ring(conv_maps, crop_counts, fc_weight, fc_bias, stitch_in, stitch_out, cotangent):
    num_rows = conv_maps.shape[0]
    units = fc_weight.shape[1]
    quarter = units // FEATS
    chunks = num_rows // CHUNK
    cot = cotangent.reshape(chunks, CHUNK, TOWERS, 8, quarter).transpose(3, 0, 2, 1, 4)
    feats, pooled, n, pick, so, relay, first, s_rows = entry(
        crop_counts, stitch_out, stitch_in, cot, conv_maps.transpose(1, 0, 2))
    full = PLACES * chunks // 2
    kinds = CLASSES + (full,)
    act, gf, weight_grad, bias_grad, sog = lax.switch(
        pick[0],
        [functools.partial(fc_layer, steps, at) for at, steps in enumerate(kinds)],
        n, so, fc_bias, feats, first, cot, relay, fc_weight)
    activations = act.transpose(1, 3, 2, 0, 4).reshape(num_rows, TOWERS, -1)
    conv_grad, si, bias_grad, stitch_out_grad, weight_grad = leave(
        s_rows, bias_grad, sog, gf, pooled, weight_grad, conv_maps.shape[1])
    conv_grad = conv_grad.transpose(1, 0, 2)
    stitch_in_grad = total_over_blk(si)
    return (activations, conv_grad, weight_grad, bias_grad, stitch_in_grad, stitch_out_grad)


def solution(mesh):
    ring = mesh.shape["blk"] == PLACES and mesh.shape["feat"] == FEATS
    return jax.shard_map(
        body_ring if ring else body_plain,
        mesh=mesh,
        in_specs=(
            P("blk", None, "feat"),
            P("blk"),
            P(None, "blk", "feat"),
            P(),
            P(None, None, "feat"),
            P(None, None, "feat"),
            P("blk", None, "feat"),
        ),
        out_specs=(
            P("blk", None, "feat"),
            P("blk", None, "feat"),
            P(None, "blk", "feat"),
            P(None, "blk"),
            P(None, None, "feat"),
            P(None, None, "feat"),
        ),
        check_vma=False,
    )
```
